256 devices in a mesh: rows: 16 (over y, z_hi, core), cols: 16 (over z_lo, x).
Axes of the slice: x: 4, y: 4, z: 8 (z_hi: 2, z_lo: 4; z = z_hi * 4 + z_lo), core: 2. Of those that a mesh axis runs over, the one named last changes fastest.
Arguments:
- eigvecs: float32 [8192, 2048], P('rows', 'cols'), may hold values from -6 to 6
- wy_packed: float32 [256, 128, 128], P(('rows', 'cols')), may hold values from -6 to 6
- slot_block: int32 [16, 8, 2], P('rows'), may hold values from 0 to 1, each once within a row
Outputs:
- transformed: float32 [8192, 2048], P('rows', 'cols')
The draws below stay inside these ranges and needn't reach their ends.
Inputs may be any that keep to these rules, and one draw needn't show every extreme that they name: `slot_block`: for every group and level the 2 entries name each of 0 .. 1 once.
All inputs are finite; a program needn't handle non-finite values.
Results may differ from the reference program's by a relative error of at most 0.0003.
Values sent between devices are 32-bit elements; how exact they have to be, the bound alone decides.
No kernel may reach another device: no remote copies, remote signals or barrier semaphores. Data moves between devices by JAX's collectives and lax.ppermute only.
A program may use at most 64 MiB of HBM per device.

```python
import jax
import jax.numpy as jnp
from jax import lax

BAND = 128
LEVELS = 8
HALF = 2
BLOCKS = 256
ROWS = 8192
COLS = 2048
N_ROWS = 16


def steps_of(own_key, dims, split, least, largest):
    loudness = 1.0
    for axis_at, parts in split:
        steps = jax.random.uniform(jax.random.fold_in(jax.random.fold_in(own_key, 6), axis_at), (parts,), jnp.float32, least / len(split), largest / len(split))
        loudness = loudness * jnp.repeat(jnp.exp(steps), dims[axis_at] // parts).reshape((-1,) + (1,) * (len(dims) - 1 - axis_at))
    return loudness


def normal_values(own_key, dims, spread, most, cuts=(), kind=jnp.bfloat16):
    values = jax.random.normal(own_key, dims, jnp.float32) * spread
    if len(cuts) > 0:
        values = steps_of(own_key, dims, cuts, -0.22, 0.18) * values
    return jnp.clip(values, min=-most, max=most).astype(kind)


def setup_inputs(seed: int = 0) -> dict:
    seeds = jax.random.split(jax.random.key(seed), 4)
    eigvecs = normal_values(seeds[0], (ROWS, COLS), 1.0, 6.0, ((0, 16), (1, 16)), jnp.float32)
    wy_packed = normal_values(seeds[1], (BLOCKS, BAND, BAND), 1.0, 6.0, ((0, 256),), jnp.float32)
    slot_block = jax.vmap(lambda own: jax.random.permutation(own, HALF))(jax.random.split(seeds[2], N_ROWS * LEVELS)).reshape((N_ROWS, LEVELS, HALF)).astype(jnp.int32)
    return dict(eigvecs=eigvecs, wy_packed=wy_packed, slot_block=slot_block)


highest = lax.Precision.HIGHEST


def unpack(packed):
    blocks, band_width = packed.shape[0], packed.shape[1]
    flipped = jnp.swapaxes(packed, 1, 2)
    padded = jnp.pad(flipped, ((0, 0), (0, 0), (0, band_width + 1)))
    flattened = padded.reshape(blocks, band_width * (2 * band_width + 1))[:, : 2 * band_width * band_width]
    return flattened.reshape(blocks, band_width, 2 * band_width)


def upper_inverse(upper):
    band_width = upper.shape[1]
    index_row = jnp.arange(band_width, dtype=jnp.int32)
    diag_values = jnp.diagonal(upper, axis1=1, axis2=2)
    identity = jnp.eye(band_width, dtype=upper.dtype)
    inverted = identity[None] * (1.0 / diag_values)[:, None, :]
    width = 1
    while width < band_width:
        same_new = (index_row[:, None] // (2 * width)) == (index_row[None, :] // (2 * width))
        same_old = (index_row[:, None] // width) == (index_row[None, :] // width)
        selector = jnp.logical_and(same_new, jnp.logical_not(same_old)).astype(upper.dtype)
        corner = upper * selector[None]
        partial_block = jnp.einsum("nij,njk->nik", corner, inverted, precision=highest)
        inverted = inverted - jnp.einsum("nij,njk->nik", inverted, partial_block, precision=highest)
        width = 2 * width
    return inverted


def wy_factor(reflectors):
    band_width = reflectors.shape[1]
    gram_matrix = jnp.einsum("njr,nkr->njk", reflectors, reflectors, precision=highest)
    identity = jnp.eye(band_width, dtype=gram_matrix.dtype)
    triangle = jnp.triu(gram_matrix, 1) + 0.5 * gram_matrix * identity
    return upper_inverse(triangle)


def reflect(reflectors, factors, windows):
    projected = jnp.einsum("njr,nrc->njc", reflectors, windows, precision=highest)
    scaled = jnp.einsum("njk,nkc->njc", factors, projected, precision=highest)
    return windows - jnp.einsum("njr,njc->nrc", reflectors, scaled, precision=highest)


def reference(eigvecs, wy_packed, slot_block):
    band_width = wy_packed.shape[1]
    row_count, col_count = eigvecs.shape
    groups = slot_block.shape[0]
    levels_all = slot_block.shape[1]
    per_level = slot_block.shape[2]
    unpacked = unpack(wy_packed)
    reflectors_all = unpacked.reshape(groups, levels_all, per_level, band_width, 2 * band_width)
    factors_all = wy_factor(unpacked).reshape(groups, levels_all, per_level, band_width, band_width)
    current = eigvecs
    padding = jnp.zeros((band_width, col_count), eigvecs.dtype)
    for level_index in range(levels_all):
        chosen = slot_block[:, level_index].astype(jnp.int32)[:, :, None, None]
        reflectors = jnp.take_along_axis(reflectors_all[:, level_index], chosen, axis=1)
        reflectors = reflectors.reshape(groups * per_level, band_width, 2 * band_width)
        factors = jnp.take_along_axis(factors_all[:, level_index], chosen, axis=1)
        factors = factors.reshape(groups * per_level, band_width, band_width)
        if level_index % 2 == 0:
            windows = current.reshape(groups * per_level, 2 * band_width, col_count)
            current = reflect(reflectors, factors, windows).reshape(row_count, col_count)
        else:
            extended = jnp.concatenate([current[band_width:], padding], axis=0)
            windows = extended.reshape(groups * per_level, 2 * band_width, col_count)
            result = reflect(reflectors, factors, windows).reshape(row_count, col_count)
            current = jnp.concatenate([current[:band_width], result[: row_count - band_width]], axis=0)
    return current
```

```python
import jax
import jax.numpy as jnp
from jax import lax
from jax.experimental import pallas as pl
from jax.experimental.pallas import tpu as pltpu
from jax.sharding import PartitionSpec as P

F32 = jnp.float32
BF16 = jnp.bfloat16
W = 128
SUB = 32
VMEM = pltpu.VMEM
SMEM = pltpu.SMEM


def split(x):
    high = x.astype(BF16)
    low = (x - high.astype(F32)).astype(BF16)
    return high, low


def mm(a, b, dims=((1,), (0,))):
    return lax.dot_general(a, b, (dims, ((), ())), preferred_element_type=F32)


def dot3(a, b):
    ah, al = a
    bh, bl = b
    return mm(ah, bh) + (mm(ah, bl) + mm(al, bh))


def unpacked(packed):
    wide = jnp.concatenate([packed.T, jnp.zeros((W, W), F32)], axis=1)
    return pltpu.roll(wide, 0, axis=1, stride=1, stride_axis=0)


def diagonal_inverses(gram):
    row = lax.broadcasted_iota(jnp.int32, (SUB, W), 0)
    lane = lax.broadcasted_iota(jnp.int32, (SUB, W), 1)
    group = lane // SUB
    place = lane % SUB
    compact = gram[0:SUB]
    for d in range(1, 4):
        compact = jnp.where(group == d, gram[d * SUB : (d + 1) * SUB], compact)
    diagonal = jnp.sum(jnp.where(row == place, compact, 0.0), axis=0, keepdims=True)
    inverse_diagonal = jnp.broadcast_to(2.0 / diagonal, (SUB, W))
    scaled = compact * inverse_diagonal
    scaled = jnp.where(row < place, scaled, 0.0)
    rows = [jnp.where(row == place, 1.0, 0.0)[8 * i : 8 * i + 8] for i in range(4)]
    base = group * SUB
    for k in range(SUB - 1, 0, -1):
        tile, at = k // 8, k % 8
        pivot = jnp.broadcast_to(rows[tile][at : at + 1], (8, W))
        for i in range(tile + 1):
            if i * 8 >= k:
                continue
            factor = jnp.take_along_axis(
                scaled[8 * i : 8 * i + 8], base[8 * i : 8 * i + 8] + k, axis=1, mode="promise_in_bounds"
            )
            rows[i] = rows[i] - factor * pivot
    unit = jnp.concatenate(rows, axis=0)
    row_scale = jnp.take_along_axis(inverse_diagonal, base + row, axis=1, mode="promise_in_bounds")
    return unit * row_scale


def triangle_inverse(gram):
    small = diagonal_inverses(gram)
    lane = lax.broadcasted_iota(jnp.int32, (SUB, W), 1)
    group = lane // SUB
    parts = [jnp.where(group == d, small, 0.0) for d in range(4)]
    base = jnp.concatenate(parts, axis=0)
    base_parts = split(base)
    zero = jnp.zeros((SUB, W), F32)
    corner = jnp.concatenate(
        [jnp.where(group == 1, gram[0:SUB], 0.0), jnp.where(group == 3, gram[2 * SUB : 3 * SUB], 0.0)], axis=0
    )
    product = dot3(split(corner), base_parts)
    full = jnp.concatenate([product[0:SUB], zero, product[SUB:], zero], axis=0)
    left = jnp.concatenate([parts[0], parts[2]], axis=0)
    change = dot3(split(left), split(full))
    upper = jnp.concatenate([parts[0] - change[0:SUB], parts[1]], axis=0)
    lower = jnp.concatenate([parts[2] - change[SUB:], parts[3]], axis=0)
    half = 2 * SUB
    lane2 = lax.broadcasted_iota(jnp.int32, (half, W), 1)
    corner2 = jnp.where(lane2 >= half, gram[0:half], 0.0)
    stacked = jnp.concatenate([jnp.zeros((half, W), F32), lower], axis=0)
    product2 = dot3(split(corner2), split(stacked))
    stacked2 = jnp.concatenate([product2, jnp.zeros((half, W), F32)], axis=0)
    change2 = dot3(split(upper), split(stacked2))
    return jnp.concatenate([upper - change2, lower], axis=0)


def factor_block(packed, a_ref, v_ref, at):
    reflectors = unpacked(packed)
    rh, rl = split(reflectors)
    nt = ((1,), (1,))
    cross = mm(rh, rl, nt)
    gram = mm(rh, rh, nt) + (cross + mm(rl, rh, nt))
    inverse = triangle_inverse(gram)
    ah, al = split(dot3(split(inverse), (rh, rl)))
    a_ref[at, :, : 2 * W] = ah
    a_ref[at, :, 2 * W :] = al
    vh, vl = split(reflectors.T)
    v_ref[at, :, :W] = vh
    v_ref[at, :, W:] = vl


def factor_kernel(picks, foreign, scalars, *refs):
    pieces = refs[:4]
    rest = refs[4:]
    if foreign:
        other, rest = rest[0], rest[1:]
    a_ref, v_ref, held = rest
    for k in range(4):
        held[(scalars[0] + 4 - k) % 4] = pieces[k][...]
    for at, pick in enumerate(picks):
        packed = other[...] if pick is None else held[scalars[pick]]
        factor_block(packed, a_ref, v_ref, at)


def factor_call(scalars, pieces, picks, other=None):
    count = len(picks)
    args = [scalars, *pieces] + ([] if other is None else [other])
    return pl.pallas_call(
        lambda *refs: factor_kernel(picks, other is not None, *refs),
        out_shape=(
            jax.ShapeDtypeStruct((count, W, 4 * W), BF16),
            jax.ShapeDtypeStruct((count, 2 * W, 2 * W), BF16),
        ),
        in_specs=[pl.BlockSpec(memory_space=SMEM)] + [pl.BlockSpec(memory_space=VMEM)] * (len(args) - 1),
        out_specs=(pl.BlockSpec(memory_space=VMEM),) * 2,
        scratch_shapes=[pltpu.VMEM((4, W, W), F32)],
        compiler_params=pltpu.CompilerParams(vmem_limit_bytes=24 * 1024 * 1024),
        cost_estimate=pl.CostEstimate(flops=count * 100_000_000, bytes_accessed=count * 400_000, transcendentals=0),
        name="factors",
    )(*args)


def applied(x, a_ref, v_ref, at):
    xh, xl = split(x)
    a = a_ref[at]
    z = mm(a[:, : 2 * W], xl) + (mm(a[:, 2 * W :], xh) + mm(a[:, : 2 * W], xh))
    zh, zl = split(z)
    v = v_ref[at]
    return x - (mm(v[:, :W], zl) + (mm(v[:, W:], zh) + mm(v[:, :W], zh)))


def inner(top, low, a_ref, v_ref, at):
    middle = applied(jnp.concatenate([top[W:], low[:W]], axis=0), a_ref, v_ref, at)
    return jnp.concatenate([top[:W], middle[:W]], axis=0), jnp.concatenate([middle[W:], low[W:]], axis=0)


def first_kernel(x_ref, a0, v0, top_ref, low_ref):
    top = applied(x_ref[: 2 * W], a0, v0, 0)
    low = applied(x_ref[2 * W :], a0, v0, 1)
    top, low = inner(top, low, a0, v0, 2)
    top_ref[...] = top
    low_ref[...] = low


def boundary(last, low, below, a_ref, v_ref, at):
    seen = jnp.where(last, 0.0, below[:W])
    middle = applied(jnp.concatenate([low[W:], seen], axis=0), a_ref, v_ref, at)
    low = jnp.concatenate([low[:W], middle[:W]], axis=0)
    return low, jnp.concatenate([jnp.where(last, below[:W], middle[W:]), below[W:]], axis=0)


def boundary_kernel(scalars, low_ref, below_ref, a0, v0, a1, v1, low_out, below_out):
    last = scalars[1] == 1
    low, below = boundary(last, low_ref[...], below_ref[...], a0, v0, 3)
    low = applied(low, a1, v1, 0)
    below = applied(below, a1, v1, 1)
    low, below = boundary(last, low, below, a1, v1, 3)
    low_out[...] = low
    below_out[...] = below


def middle_kernel(low_ref, top_ref, a1, v1, a2, v2, low_out, top_out):
    top, low = inner(top_ref[...], low_ref[...], a1, v1, 2)
    top = applied(top, a2, v2, 0)
    low = applied(low, a2, v2, 1)
    top, low = inner(top, low, a2, v2, 2)
    low_out[...] = low
    top_out[...] = top


def last_kernel(low_ref, top_ref, a3, v3, out_ref):
    top, low = inner(top_ref[...], low_ref[...], a3, v3, 2)
    out_ref[: 2 * W] = top
    out_ref[2 * W :] = low


def apply_call(kernel, args, shapes, smem=0, diamonds=4):
    return pl.pallas_call(
        kernel,
        out_shape=tuple(jax.ShapeDtypeStruct(s, F32) for s in shapes),
        in_specs=[pl.BlockSpec(memory_space=SMEM)] * smem + [pl.BlockSpec(memory_space=VMEM)] * (len(args) - smem),
        out_specs=(pl.BlockSpec(memory_space=VMEM),) * len(shapes),
        compiler_params=pltpu.CompilerParams(vmem_limit_bytes=24 * 1024 * 1024),
        cost_estimate=pl.CostEstimate(flops=diamonds * 100_000_000, bytes_accessed=2_000_000, transcendentals=0),
        name=kernel.__name__,
    )(*args)


def shifted(value, axis, steps):
    count = lax.axis_size(axis)
    return lax.ppermute(value, axis, [(i, (i + steps) % count) for i in range(count)])


def per_device(eigvecs, wy_packed, slot_block):
    slots = slot_block[0]
    column = lax.axis_index("cols")
    plane, place = column // 4, column % 4
    last = (lax.axis_index("rows") == lax.axis_size("rows") - 1).astype(jnp.int32)
    packed = wy_packed[0]

    def along_x(value, k):
        return lax.ppermute(value, "cols", [(i, (i // 4) * 4 + (i + k) % 4) for i in range(16)])

    planes = [packed] + [shifted(packed, "cols", 4 * k) for k in (1, 2, 3)]
    ordered = [lax.select_n((plane + 4 - j) % 4, *planes) for j in range(4)]
    part0 = [ordered[0]] + [along_x(ordered[0], k) for k in (1, 2, 3)]
    part1 = [ordered[1]] + [along_x(ordered[1], k) for k in (1, 2, 3)]
    pair = jnp.stack(ordered[2:])
    pairs = [pair] + [along_x(pair, k) for k in (1, 2, 3)]
    part2 = [p[0] for p in pairs]
    part3 = [p[1] for p in pairs]

    def scalars_of(z):
        own = slots[2 * z : 2 * z + 2] + jnp.array([[0], [2]], jnp.int32)
        return jnp.concatenate([jnp.stack([place, last]), own.reshape(4)])

    scalars = [scalars_of(z) for z in range(4)]

    def for_above(part, z):
        return shifted(lax.select_n((place + 4 - slots[2 * z, 0]) % 4, *part), "rows", -1)

    half = (2 * W, eigvecs.shape[1])
    a0, v0 = factor_call(scalars[0], part0, (2, 3, 4, 5))
    top, low = apply_call(first_kernel, (eigvecs, a0, v0), (half, half), diamonds=3)
    below = shifted(top, "rows", -1)
    a1, v1 = factor_call(scalars[1], part1, (3, None, 4, 5), for_above(part1, 1))
    low, below = apply_call(boundary_kernel, (scalars[0], low, below, a0, v0, a1, v1), (half, half), smem=1)
    top = shifted(below, "rows", 1)
    a2, v2 = factor_call(scalars[2], part2, (2, 3, 4, 5))
    low, top = apply_call(middle_kernel, (low, top, a1, v1, a2, v2), (half, half))
    below = shifted(top, "rows", -1)
    a3, v3 = factor_call(scalars[3], part3, (3, None, 4, 5), for_above(part3, 3))
    low, below = apply_call(boundary_kernel, (scalars[0], low, below, a2, v2, a3, v3), (half, half), smem=1)
    top = shifted(below, "rows", 1)
    return apply_call(last_kernel, (low, top, a3, v3), (eigvecs.shape,), diamonds=1)[0]


def solution(mesh):
    placed = (P("rows", "cols"), P(("rows", "cols"), None, None), P("rows", None, None))
    return jax.shard_map(
        per_device, mesh=mesh, in_specs=placed, out_specs=P("rows", "cols"), check_vma=False
    )
```

```python
import jax
import jax.numpy as jnp
from jax import lax
from jax.experimental import pallas as pl
from jax.experimental.pallas import tpu as pltpu
from jax.sharding import PartitionSpec as P

F32 = jnp.float32
BF16 = jnp.bfloat16
W = 128
SUB = 32
VMEM = pltpu.VMEM
SMEM = pltpu.SMEM


def split(x):
    high = x.astype(BF16)
    low = (x - high.astype(F32)).astype(BF16)
    return high, low


def mm(a, b, dims=((1,), (0,))):
    return lax.dot_general(a, b, (dims, ((), ())), preferred_element_type=F32)


def dot3(a, b):
    ah, al = a
    bh, bl = b
    return mm(ah, bh) + (mm(ah, bl) + mm(al, bh))


def unpacked(packed):
    wide = jnp.concatenate([packed.T, jnp.zeros((W, W), F32)], axis=1)
    return pltpu.roll(wide, 0, axis=1, stride=1, stride_axis=0)


def diagonal_inverses(grams):
    row = lax.broadcasted_iota(jnp.int32, (SUB, W), 0)
    lane = lax.broadcasted_iota(jnp.int32, (SUB, W), 1)
    group = lane // SUB
    place = lane % SUB
    base = group * SUB

    def prepared(gram):
        compact = gram[0:SUB]
        for d in range(1, 4):
            compact = jnp.where(group == d, gram[d * SUB : (d + 1) * SUB], compact)
        diagonal = jnp.sum(jnp.where(row == place, compact, 0.0), axis=0, keepdims=True)
        scale = jnp.broadcast_to(2.0 / diagonal, (SUB, W))
        return jnp.where(row < place, compact * scale, 0.0), scale

    pairs = [prepared(gram) for gram in grams]
    start = [jnp.where(row == place, 1.0, 0.0)[8 * i : 8 * i + 8] for i in range(4)]
    rows = [list(start) for _ in grams]
    for k in range(SUB - 1, 0, -1):
        tile, at = k // 8, k % 8
        for n in range(len(grams)):
            pivot = jnp.broadcast_to(rows[n][tile][at : at + 1], (8, W))
            for i in range(tile + 1):
                if i * 8 < k:
                    factor = jnp.take_along_axis(
                        pairs[n][0][8 * i : 8 * i + 8], base[8 * i : 8 * i + 8] + k, axis=1, mode="promise_in_bounds"
                    )
                    rows[n][i] = rows[n][i] - factor * pivot
    row_scales = [jnp.take_along_axis(scale, base + row, axis=1, mode="promise_in_bounds") for _, scale in pairs]
    return [jnp.concatenate(r, axis=0) * s for r, s in zip(rows, row_scales)]


def dots3(lefts, rights):
    return [dot3(a, b) for a, b in zip(lefts, rights)]


def splits(values):
    return [split(v) for v in values]


def triangle_inverses(grams):
    small = diagonal_inverses(grams)
    lane = lax.broadcasted_iota(jnp.int32, (SUB, W), 1)
    group = lane // SUB
    half = 2 * SUB
    zero = jnp.zeros((SUB, W), F32)
    zeros = jnp.zeros((half, W), F32)
    parts = [[jnp.where(group == d, s, 0.0) for d in range(4)] for s in small]
    bases = splits([jnp.concatenate(p, axis=0) for p in parts])
    corners = splits(
        [
            jnp.concatenate(
                [jnp.where(group == 1, g[0:SUB], 0.0), jnp.where(group == 3, g[2 * SUB : 3 * SUB], 0.0)], axis=0
            )
            for g in grams
        ]
    )
    lane2 = lax.broadcasted_iota(jnp.int32, (half, W), 1)
    corners2 = splits([jnp.where(lane2 >= half, g[0:half], 0.0) for g in grams])
    products = dots3(corners, bases)
    fulls = splits([jnp.concatenate([p[0:SUB], zero, p[SUB:], zero], axis=0) for p in products])
    changes = dots3(splits([jnp.concatenate([p[0], p[2]], axis=0) for p in parts]), fulls)
    uppers = [jnp.concatenate([p[0] - c[0:SUB], p[1]], axis=0) for p, c in zip(parts, changes)]
    lowers = [jnp.concatenate([p[2] - c[SUB:], p[3]], axis=0) for p, c in zip(parts, changes)]
    products = dots3(corners2, splits([jnp.concatenate([zeros, low], axis=0) for low in lowers]))
    changes = dots3(splits(uppers), splits([jnp.concatenate([p, zeros], axis=0) for p in products]))
    return [jnp.concatenate([u - c, low], axis=0) for u, c, low in zip(uppers, changes, lowers)]


def factor_blocks(packed, a_ref, v_ref):
    reflectors = [unpacked(p) for p in packed]
    halves = splits(reflectors)
    nt = ((1,), (1,))
    grams = [mm(h, h, nt) + (mm(h, l, nt) + mm(l, h, nt)) for h, l in halves]
    for at, r in enumerate(reflectors):
        vh, vl = split(r.T)
        v_ref[at, :, :W] = vh
        v_ref[at, :, W:] = vl
    inverses = splits(triangle_inverses(grams))
    for at, a in enumerate(dots3(inverses, halves)):
        ah, al = split(a)
        a_ref[at, :, : 2 * W] = ah
        a_ref[at, :, 2 * W :] = al


def slot_of(scalars, level, half):
    return scalars[3 + 2 * level + half]


def gathered(scalars, pieces, held, at=None):
    for k in range(4):
        held[(scalars[0] + 4 - k) % 4] = pieces[k][...] if at is None else pieces[k][at]


def block_of(scalars, held, level, half):
    return held[2 * (level % 2) + slot_of(scalars, level, half)]


def applied(x, a_ref, v_ref, at):
    xh, xl = split(x)
    a = a_ref[at]
    z = mm(a[:, : 2 * W], xl) + (mm(a[:, 2 * W :], xh) + mm(a[:, : 2 * W], xh))
    zh, zl = split(z)
    v = v_ref[at]
    return x - (mm(v[:, :W], zl) + (mm(v[:, W:], zh) + mm(v[:, :W], zh)))


def across(top, low, a_ref, v_ref, at):
    middle = applied(jnp.concatenate([top[W:], low[:W]], axis=0), a_ref, v_ref, at)
    return jnp.concatenate([top[:W], middle[:W]], axis=0), jnp.concatenate([middle[W:], low[W:]], axis=0)


def across_below(last, low, below, a_ref, v_ref, at):
    new_low, new_below = across(low, jnp.where(last, 0.0, below), a_ref, v_ref, at)
    return new_low, jnp.where(last, below, new_below)


def across_above(first, above, top, a_ref, v_ref, at):
    new_above, new_top = across(above, top, a_ref, v_ref, at)
    return new_above, jnp.where(first, top, new_top)


def first_kernel(scalars, x_ref, p0, p1, p2, p3, q0, q1, q2, q3, message, low_ref, a0, v0, held):
    gathered(scalars, (q0, q1, q2, q3), held)
    message[2 * W :] = block_of(scalars, held, 2, 0)
    gathered(scalars, (p0, p1, p2, p3), held)
    factor_blocks([block_of(scalars, held, level, half) for level in (0, 1) for half in (0, 1)], a0, v0)
    top = applied(x_ref[: 2 * W], a0, v0, 0)
    low = applied(x_ref[2 * W :], a0, v0, 1)
    top, low = across(top, low, a0, v0, 2)
    message[: 2 * W] = top
    low_ref[...] = low


def factor1_kernel(scalars, after, p0, p1, p2, p3, o2, o3, a1, v1, pair, held):
    pair[0] = o2[...]
    pair[1] = o3[...]
    gathered(scalars, (p0, p1, p2, p3), held)
    factor_blocks([block_of(scalars, held, level, half) for level, half in ((2, 1), (3, 0), (3, 1))], a1, v1)


def second_kernel(scalars, low_ref, message, a0, v0, a1, v1, low_out, below_out, af, vf):
    last = scalars[1] == 1
    factor_blocks([message[2 * W :]], af, vf)
    low, below = across_below(last, low_ref[...], message[: 2 * W], a0, v0, 3)
    low = applied(low, a1, v1, 0)
    below = applied(below, af, vf, 0)
    low, below = across_below(last, low, below, a1, v1, 2)
    low_out[...] = low
    below_out[...] = below


def factor2_kernel(scalars, after, p0, p1, p2, p3, a2, v2, down, up, held):
    gathered(scalars, (p0, p1, p2, p3), held, 1)
    down[1] = block_of(scalars, held, 6, 1)
    down[2] = block_of(scalars, held, 7, 1)
    up[...] = block_of(scalars, held, 6, 0)
    gathered(scalars, (p0, p1, p2, p3), held, 0)
    down[0] = block_of(scalars, held, 5, 1)
    factor_blocks([block_of(scalars, held, level, half) for level in (4, 5) for half in (0, 1)], a2, v2)


def third_kernel(low_ref, top_ref, a1, v1, a2, v2, low_out, top_out):
    top, low = across(top_ref[...], low_ref[...], a1, v1, 1)
    top = applied(top, a2, v2, 0)
    low = applied(low, a2, v2, 1)
    top, low = across(top, low, a2, v2, 2)
    low_out[...] = low
    top_out[...] = top


def factor3_kernel(scalars, after, p0, p1, p2, p3, a3, v3, held):
    gathered(scalars, (p0, p1, p2, p3), held, 1)
    factor_blocks([block_of(scalars, held, level, half) for level in (6, 7) for half in (0, 1)], a3, v3)


def factor4_kernel(after, down, up, a4, v4):
    factor_blocks([down[0], down[1], down[2], up[...]], a4, v4)


def fourth_kernel(scalars, low_ref, top_ref, above_ref, below_ref, a2, v2, a3, v3, a4, v4, out_ref):
    last = scalars[1] == 1
    first = scalars[2] == 1
    low, below = across_below(last, low_ref[...], below_ref[...], a2, v2, 3)
    above, top = across_above(first, above_ref[...], top_ref[...], a4, v4, 0)
    above = applied(above, a4, v4, 1)
    top = applied(top, a3, v3, 0)
    low = applied(low, a3, v3, 1)
    below = applied(below, a4, v4, 3)
    _, top = across_above(first, above, top, a4, v4, 2)
    low, _ = across_below(last, low, below, a3, v3, 3)
    top, low = across(top, low, a3, v3, 2)
    out_ref[: 2 * W] = top
    out_ref[2 * W :] = low


def factor_shapes(count):
    return [jax.ShapeDtypeStruct((count, W, 4 * W), BF16), jax.ShapeDtypeStruct((count, 2 * W, 2 * W), BF16)]


def rows_shape(*shape):
    return jax.ShapeDtypeStruct(shape, F32)


HELD = [pltpu.VMEM((4, W, W), F32)]


def call(kernel, args, shapes, scratch=(), smem=1, flops=400_000_000):
    return pl.pallas_call(
        kernel,
        out_shape=tuple(shapes),
        in_specs=[pl.BlockSpec(memory_space=SMEM)] * smem + [pl.BlockSpec(memory_space=VMEM)] * (len(args) - smem),
        out_specs=(pl.BlockSpec(memory_space=VMEM),) * len(shapes),
        scratch_shapes=list(scratch),
        compiler_params=pltpu.CompilerParams(vmem_limit_bytes=24 * 1024 * 1024),
        cost_estimate=pl.CostEstimate(flops=flops, bytes_accessed=2_000_000, transcendentals=0),
        name=kernel.__name__,
    )(*args)


def shifted(value, axis, steps):
    count = lax.axis_size(axis)
    return lax.ppermute(value, axis, [(i, (i + steps) % count) for i in range(count)])


def along_x(value):
    return [value] + [lax.ppermute(value, "cols", [(i, (i // 4) * 4 + (i + k) % 4) for i in range(16)]) for k in (1, 2, 3)]


def per_device(eigvecs, wy_packed, slot_block):
    column = lax.axis_index("cols")
    row = lax.axis_index("rows")
    plane, place = column // 4, column % 4
    edges = jnp.stack([place, row == lax.axis_size("rows") - 1, row == 0]).astype(jnp.int32)
    scalars = jnp.concatenate([edges, slot_block.reshape(-1)])
    packed = wy_packed[0]
    half = rows_shape(2 * W, W)

    planes = [packed] + [shifted(packed, "cols", 4 * k) for k in (1, 2, 3)]
    ordered = [lax.select_n((plane + 4 - j) % 4, *planes) for j in range(4)]
    part0 = along_x(ordered[0])
    part1 = along_x(ordered[1])
    message, low, a0, v0 = call(
        first_kernel,
        (scalars, eigvecs, *part0, *part1),
        [rows_shape(3 * W, W), half, *factor_shapes(4)],
        HELD,
    )
    message = shifted(message, "rows", -1)
    a1, v1, pair = call(
        factor1_kernel,
        (scalars, low, *part1, ordered[2], ordered[3]),
        [*factor_shapes(3), rows_shape(2, W, W)],
        HELD,
    )
    pairs = along_x(pair)
    scratch = [pltpu.VMEM(s.shape, s.dtype) for s in factor_shapes(1)]
    low, below = call(second_kernel, (scalars, low, message, a0, v0, a1, v1), [half, half], scratch)
    top = shifted(below, "rows", 1)
    a2, v2, down, up = call(
        factor2_kernel,
        (scalars, low, *pairs),
        [*factor_shapes(4), rows_shape(3, W, W), rows_shape(W, W)],
        HELD,
    )
    down = shifted(down, "rows", 1)
    up = shifted(up, "rows", -1)
    low, top = call(third_kernel, (low, top, a1, v1, a2, v2), [half, half], smem=0)
    above = shifted(low, "rows", 1)
    below = shifted(top, "rows", -1)
    a3, v3 = call(factor3_kernel, (scalars, low, *pairs), factor_shapes(4), HELD)
    a4, v4 = call(factor4_kernel, (low, down, up), factor_shapes(4), smem=0)
    return call(
        fourth_kernel, (scalars, low, top, above, below, a2, v2, a3, v3, a4, v4), [rows_shape(*eigvecs.shape)]
    )[0]


def solution(mesh):
    placed = (P("rows", "cols"), P(("rows", "cols"), None, None), P("rows", None, None))
    return jax.shard_map(
        per_device, mesh=mesh, in_specs=placed, out_specs=P("rows", "cols"), check_vma=False
    )
```

```python
import jax
import jax.numpy as jnp
from jax import lax
from jax.experimental import pallas as pl
from jax.experimental.pallas import tpu as pltpu
from jax.sharding import PartitionSpec as P

F32 = jnp.float32
BF16 = jnp.bfloat16
W = 128
SUB = 32
VMEM = pltpu.VMEM
SMEM = pltpu.SMEM


def split(x):
    high = x.astype(BF16)
    low = (x - high.astype(F32)).astype(BF16)
    return high, low


def mm(a, b, dims=((1,), (0,))):
    return lax.dot_general(a, b, (dims, ((), ())), preferred_element_type=F32)


def dot3(a, b):
    ah, al = a
    bh, bl = b
    return mm(ah, bh) + (mm(ah, bl) + mm(al, bh))


def unpacked(packed):
    wide = jnp.concatenate([packed.T, jnp.zeros((W, W), F32)], axis=1)
    return pltpu.roll(wide, 0, axis=1, stride=1, stride_axis=0)


def diagonal_inverses(grams):
    row = lax.broadcasted_iota(jnp.int32, (SUB, W), 0)
    lane = lax.broadcasted_iota(jnp.int32, (SUB, W), 1)
    group = lane // SUB
    place = lane % SUB
    base = group * SUB

    def prepared(gram):
        compact = gram[0:SUB]
        for d in range(1, 4):
            compact = jnp.where(group == d, gram[d * SUB : (d + 1) * SUB], compact)
        diagonal = jnp.sum(jnp.where(row == place, compact, 0.0), axis=0, keepdims=True)
        scale = jnp.broadcast_to(2.0 / diagonal, (SUB, W))
        return jnp.where(row < place, compact * scale, 0.0), scale

    pairs = [prepared(gram) for gram in grams]
    start = [jnp.where(row == place, 1.0, 0.0)[8 * i : 8 * i + 8] for i in range(4)]
    rows = [list(start) for _ in grams]
    for k in range(SUB - 1, 0, -1):
        tile, at = k // 8, k % 8
        for n in range(len(grams)):
            pivot = jnp.broadcast_to(rows[n][tile][at : at + 1], (8, W))
            for i in range(tile + 1):
                if i * 8 < k:
                    factor = jnp.take_along_axis(
                        pairs[n][0][8 * i : 8 * i + 8], base[8 * i : 8 * i + 8] + k, axis=1, mode="promise_in_bounds"
                    )
                    rows[n][i] = rows[n][i] - factor * pivot
    row_scales = [jnp.take_along_axis(scale, base + row, axis=1, mode="promise_in_bounds") for _, scale in pairs]
    return [jnp.concatenate(r, axis=0) * s for r, s in zip(rows, row_scales)]


def dots3(lefts, rights):
    return [dot3(a, b) for a, b in zip(lefts, rights)]


def splits(values):
    return [split(v) for v in values]


def triangle_inverses(grams):
    small = diagonal_inverses(grams)
    lane = lax.broadcasted_iota(jnp.int32, (SUB, W), 1)
    group = lane // SUB
    half = 2 * SUB
    zero = jnp.zeros((SUB, W), F32)
    zeros = jnp.zeros((half, W), F32)
    parts = [[jnp.where(group == d, s, 0.0) for d in range(4)] for s in small]
    bases = splits([jnp.concatenate(p, axis=0) for p in parts])
    corners = splits(
        [
            jnp.concatenate(
                [jnp.where(group == 1, g[0:SUB], 0.0), jnp.where(group == 3, g[2 * SUB : 3 * SUB], 0.0)], axis=0
            )
            for g in grams
        ]
    )
    lane2 = lax.broadcasted_iota(jnp.int32, (half, W), 1)
    corners2 = splits([jnp.where(lane2 >= half, g[0:half], 0.0) for g in grams])
    products = dots3(corners, bases)
    fulls = splits([jnp.concatenate([p[0:SUB], zero, p[SUB:], zero], axis=0) for p in products])
    changes = dots3(splits([jnp.concatenate([p[0], p[2]], axis=0) for p in parts]), fulls)
    uppers = [jnp.concatenate([p[0] - c[0:SUB], p[1]], axis=0) for p, c in zip(parts, changes)]
    lowers = [jnp.concatenate([p[2] - c[SUB:], p[3]], axis=0) for p, c in zip(parts, changes)]
    products = dots3(corners2, splits([jnp.concatenate([zeros, low], axis=0) for low in lowers]))
    changes = dots3(splits(uppers), splits([jnp.concatenate([p, zeros], axis=0) for p in products]))
    return [jnp.concatenate([u - c, low], axis=0) for u, c, low in zip(uppers, changes, lowers)]


def factors(packed):
    reflectors = [unpacked(p) for p in packed]
    halves = splits(reflectors)
    nt = ((1,), (1,))
    grams = [mm(h, h, nt) + (mm(h, l, nt) + mm(l, h, nt)) for h, l in halves]
    inverses = splits(triangle_inverses(grams))
    products = splits(dots3(inverses, halves))
    return [(*a, *split(r.T)) for a, r in zip(products, reflectors)]


def stored_factors(packed, a_ref, v_ref):
    for at, (ah, al, vh, vl) in enumerate(factors(packed)):
        a_ref[at, :, : 2 * W] = ah
        a_ref[at, :, 2 * W :] = al
        v_ref[at, :, :W] = vh
        v_ref[at, :, W:] = vl


def loaded(a_ref, v_ref, at):
    a, v = a_ref[at], v_ref[at]
    return a[:, : 2 * W], a[:, 2 * W :], v[:, :W], v[:, W:]


def slot_of(scalars, level, half):
    return scalars[3 + 2 * level + half]


def gathered(scalars, pieces, held, at):
    for k in range(4):
        held[(scalars[0] + 4 - k) % 4] = pieces[k][at]


def block_of(scalars, held, level, half):
    return held[2 * (level % 2) + slot_of(scalars, level, half)]


def applied(x, factor):
    ah, al, vh, vl = factor
    x_parts = split(x)
    z_parts = split(dot3((ah, al), x_parts))
    return x - dot3((vh, vl), z_parts)


def across(top, low, factor):
    middle = applied(jnp.concatenate([top[W:], low[:W]], axis=0), factor)
    return jnp.concatenate([top[:W], middle[:W]], axis=0), jnp.concatenate([middle[W:], low[W:]], axis=0)


def across_below(last, low, below, factor):
    new_low, new_below = across(low, jnp.where(last, 0.0, below), factor)
    return new_low, jnp.where(last, below, new_below)


def across_above(first, above, top, factor):
    new_above, new_top = across(above, top, factor)
    return new_above, jnp.where(first, top, new_top)


def order_kernel(plane, p0, p1, p2, p3, near, far, held):
    for k, piece in enumerate((p0, p1, p2, p3)):
        held[(plane[0] + 4 - k) % 4] = piece[...]
    near[...] = held[0:2]
    far[...] = held[2:4]


def first_kernel(scalars, x_ref, p0, p1, p2, p3, message, low_ref, a0, v0, held):
    pieces = (p0, p1, p2, p3)
    gathered(scalars, pieces, held, 1)
    message[2 * W :] = block_of(scalars, held, 2, 0)
    gathered(scalars, pieces, held, 0)
    stored_factors([block_of(scalars, held, level, half) for level in (0, 1) for half in (0, 1)], a0, v0)
    top = applied(x_ref[: 2 * W], loaded(a0, v0, 0))
    low = applied(x_ref[2 * W :], loaded(a0, v0, 1))
    top, low = across(top, low, loaded(a0, v0, 2))
    message[: 2 * W] = top
    low_ref[...] = low


def factor1_kernel(scalars, after, p0, p1, p2, p3, far, a1, v1, sent, held):
    sent[...] = far[...]
    gathered(scalars, (p0, p1, p2, p3), held, 1)
    stored_factors([block_of(scalars, held, level, half) for level, half in ((2, 1), (3, 0), (3, 1))], a1, v1)


def second_kernel(scalars, low_ref, message, a0, v0, a1, v1, low_out, below_out):
    last = scalars[1] == 1
    (foreign,) = factors([message[2 * W :]])
    low, below = across_below(last, low_ref[...], message[: 2 * W], loaded(a0, v0, 3))
    low = applied(low, loaded(a1, v1, 0))
    below = applied(below, foreign)
    low, below = across_below(last, low, below, loaded(a1, v1, 2))
    low_out[...] = low
    below_out[...] = below


def choose_kernel(scalars, after, p0, p1, p2, p3, down, up, held):
    pieces = (p0, p1, p2, p3)
    gathered(scalars, pieces, held, 1)
    down[1] = block_of(scalars, held, 6, 1)
    down[2] = block_of(scalars, held, 7, 1)
    up[...] = block_of(scalars, held, 6, 0)
    gathered(scalars, pieces, held, 0)
    down[0] = block_of(scalars, held, 5, 1)


def factor2_kernel(scalars, after, p0, p1, p2, p3, a2, v2, held):
    gathered(scalars, (p0, p1, p2, p3), held, 0)
    stored_factors([block_of(scalars, held, level, half) for level in (4, 5) for half in (0, 1)], a2, v2)


def third_kernel(low_ref, top_ref, up, a1, v1, a2, v2, low_out, message):
    message[2 * W :] = up[...]
    top, low = across(top_ref[...], low_ref[...], loaded(a1, v1, 1))
    top = applied(top, loaded(a2, v2, 0))
    low = applied(low, loaded(a2, v2, 1))
    top, low = across(top, low, loaded(a2, v2, 2))
    low_out[...] = low
    message[: 2 * W] = top


def factor3_kernel(scalars, after, p0, p1, p2, p3, a3, v3, held):
    gathered(scalars, (p0, p1, p2, p3), held, 1)
    stored_factors([block_of(scalars, held, level, half) for level in (6, 7) for half in (0, 1)], a3, v3)


def factor4_kernel(after, down, a4, v4):
    stored_factors([down[0], down[1], down[2]], a4, v4)


def fourth_kernel(scalars, low_ref, own, above_ref, message, a2, v2, a3, v3, a4, v4, out_ref):
    last = scalars[1] == 1
    first = scalars[2] == 1
    (foreign,) = factors([message[2 * W :]])
    low, below = across_below(last, low_ref[...], message[: 2 * W], loaded(a2, v2, 3))
    above, top = across_above(first, above_ref[...], own[: 2 * W], loaded(a4, v4, 0))
    above = applied(above, loaded(a4, v4, 1))
    top = applied(top, loaded(a3, v3, 0))
    low = applied(low, loaded(a3, v3, 1))
    below = applied(below, foreign)
    _, top = across_above(first, above, top, loaded(a4, v4, 2))
    low, _ = across_below(last, low, below, loaded(a3, v3, 3))
    top, low = across(top, low, loaded(a3, v3, 2))
    out_ref[: 2 * W] = top
    out_ref[2 * W :] = low


def factor_shapes(count):
    return [jax.ShapeDtypeStruct((count, W, 4 * W), BF16), jax.ShapeDtypeStruct((count, 2 * W, 2 * W), BF16)]


def rows_shape(*shape):
    return jax.ShapeDtypeStruct(shape, F32)


HELD = [pltpu.VMEM((4, W, W), F32)]


def call(kernel, args, shapes, scratch=(), smem=1, flops=400_000_000):
    return pl.pallas_call(
        kernel,
        out_shape=tuple(shapes),
        in_specs=[pl.BlockSpec(memory_space=SMEM)] * smem + [pl.BlockSpec(memory_space=VMEM)] * (len(args) - smem),
        out_specs=(pl.BlockSpec(memory_space=VMEM),) * len(shapes),
        scratch_shapes=list(scratch),
        compiler_params=pltpu.CompilerParams(vmem_limit_bytes=24 * 1024 * 1024),
        cost_estimate=pl.CostEstimate(flops=flops, bytes_accessed=2_000_000, transcendentals=0),
        name=kernel.__name__,
    )(*args)


def shifted(value, axis, steps):
    count = lax.axis_size(axis)
    return lax.ppermute(value, axis, [(i, (i + steps) % count) for i in range(count)])


def along_x(value):
    return [value] + [lax.ppermute(value, "cols", [(i, (i // 4) * 4 + (i + k) % 4) for i in range(16)]) for k in (1, 2, 3)]


def per_device(eigvecs, wy_packed, slot_block):
    column = lax.axis_index("cols")
    row = lax.axis_index("rows")
    plane, place = column // 4, column % 4
    edges = jnp.stack([place, row == lax.axis_size("rows") - 1, row == 0]).astype(jnp.int32)
    scalars = jnp.concatenate([edges, slot_block.reshape(-1)])
    packed = wy_packed[0]
    half = rows_shape(2 * W, W)

    planes = [packed] + [shifted(packed, "cols", 4 * k) for k in (1, 2, 3)]
    pair = rows_shape(2, W, W)
    near, far = call(order_kernel, (plane.reshape(1), *planes), [pair, pair], HELD)
    near = along_x(near)
    message, low, a0, v0 = call(
        first_kernel, (scalars, eigvecs, *near), [rows_shape(3 * W, W), half, *factor_shapes(4)], HELD
    )
    message = shifted(message, "rows", -1)
    a1, v1, far = call(factor1_kernel, (scalars, low, *near, far), [*factor_shapes(3), pair], HELD)
    far = along_x(far)
    low, below = call(second_kernel, (scalars, low, message, a0, v0, a1, v1), [half, half])
    top = shifted(below, "rows", 1)
    down, up = call(choose_kernel, (scalars, low, *far), [rows_shape(3, W, W), rows_shape(W, W)], HELD)
    a2, v2 = call(factor2_kernel, (scalars, up, *far), factor_shapes(4), HELD)
    down = shifted(down, "rows", 1)
    low, own = call(third_kernel, (low, top, up, a1, v1, a2, v2), [half, rows_shape(3 * W, W)], smem=0)
    above = shifted(low, "rows", 1)
    message = shifted(own, "rows", -1)
    a3, v3 = call(factor3_kernel, (scalars, low, *far), factor_shapes(4), HELD)
    a4, v4 = call(factor4_kernel, (low, down), factor_shapes(3), smem=0)
    return call(
        fourth_kernel, (scalars, low, own, above, message, a2, v2, a3, v3, a4, v4), [rows_shape(*eigvecs.shape)]
    )[0]


def solution(mesh):
    placed = (P("rows", "cols"), P(("rows", "cols"), None, None), P("rows", None, None))
    return jax.shard_map(
        per_device, mesh=mesh, in_specs=placed, out_specs=P("rows", "cols"), check_vma=False
    )
```

```python
import jax
import jax.numpy as jnp
from jax import lax
from jax.experimental import pallas as pl
from jax.experimental.pallas import tpu as pltpu
from jax.sharding import PartitionSpec as P

F32 = jnp.float32
BF16 = jnp.bfloat16
W = 128
SUB = 32
VMEM = pltpu.VMEM
SMEM = pltpu.SMEM


def split(x):
    high = x.astype(BF16)
    low = (x - high.astype(F32)).astype(BF16)
    return high, low


def mm(a, b, dims=((1,), (0,))):
    return lax.dot_general(a, b, (dims, ((), ())), preferred_element_type=F32)


def dot3(a, b):
    ah, al = a
    bh, bl = b
    return mm(ah, bh) + (mm(ah, bl) + mm(al, bh))


def unpacked(packed):
    wide = jnp.concatenate([packed.T, jnp.zeros((W, W), F32)], axis=1)
    return pltpu.roll(wide, 0, axis=1, stride=1, stride_axis=0)


def diagonal_inverses(grams):
    row = lax.broadcasted_iota(jnp.int32, (SUB, W), 0)
    lane = lax.broadcasted_iota(jnp.int32, (SUB, W), 1)
    group = lane // SUB
    place = lane % SUB
    base = group * SUB

    def prepared(gram):
        compact = gram[0:SUB]
        for d in range(1, 4):
            compact = jnp.where(group == d, gram[d * SUB : (d + 1) * SUB], compact)
        diagonal = jnp.sum(jnp.where(row == place, compact, 0.0), axis=0, keepdims=True)
        scale = jnp.broadcast_to(2.0 / diagonal, (SUB, W))
        return jnp.where(row < place, compact * scale, 0.0), scale

    pairs = [prepared(gram) for gram in grams]
    start = [jnp.where(row == place, 1.0, 0.0)[8 * i : 8 * i + 8] for i in range(4)]
    rows = [list(start) for _ in grams]
    for k in range(SUB - 1, 0, -1):
        tile, at = k // 8, k % 8
        for n in range(len(grams)):
            pivot = jnp.broadcast_to(rows[n][tile][at : at + 1], (8, W))
            for i in range(tile + 1):
                if i * 8 < k:
                    factor = jnp.take_along_axis(
                        pairs[n][0][8 * i : 8 * i + 8], base[8 * i : 8 * i + 8] + k, axis=1, mode="promise_in_bounds"
                    )
                    rows[n][i] = rows[n][i] - factor * pivot
    row_scales = [jnp.take_along_axis(scale, base + row, axis=1, mode="promise_in_bounds") for _, scale in pairs]
    return [jnp.concatenate(r, axis=0) * s for r, s in zip(rows, row_scales)]


def dots3(lefts, rights):
    return [dot3(a, b) for a, b in zip(lefts, rights)]


def splits(values):
    return [split(v) for v in values]


def triangle_inverses(grams):
    small = diagonal_inverses(grams)
    lane = lax.broadcasted_iota(jnp.int32, (SUB, W), 1)
    group = lane // SUB
    half = 2 * SUB
    zero = jnp.zeros((SUB, W), F32)
    zeros = jnp.zeros((half, W), F32)
    parts = [[jnp.where(group == d, s, 0.0) for d in range(4)] for s in small]
    bases = splits([jnp.concatenate(p, axis=0) for p in parts])
    corners = splits(
        [
            jnp.concatenate(
                [jnp.where(group == 1, g[0:SUB], 0.0), jnp.where(group == 3, g[2 * SUB : 3 * SUB], 0.0)], axis=0
            )
            for g in grams
        ]
    )
    lane2 = lax.broadcasted_iota(jnp.int32, (half, W), 1)
    corners2 = splits([jnp.where(lane2 >= half, g[0:half], 0.0) for g in grams])
    products = dots3(corners, bases)
    fulls = splits([jnp.concatenate([p[0:SUB], zero, p[SUB:], zero], axis=0) for p in products])
    changes = dots3(splits([jnp.concatenate([p[0], p[2]], axis=0) for p in parts]), fulls)
    uppers = [jnp.concatenate([p[0] - c[0:SUB], p[1]], axis=0) for p, c in zip(parts, changes)]
    lowers = [jnp.concatenate([p[2] - c[SUB:], p[3]], axis=0) for p, c in zip(parts, changes)]
    products = dots3(corners2, splits([jnp.concatenate([zeros, low], axis=0) for low in lowers]))
    changes = dots3(splits(uppers), splits([jnp.concatenate([p, zeros], axis=0) for p in products]))
    return [jnp.concatenate([u - c, low], axis=0) for u, c, low in zip(uppers, changes, lowers)]


def factors(packed):
    reflectors = [unpacked(p) for p in packed]
    halves = splits(reflectors)
    nt = ((1,), (1,))
    grams = [mm(h, h, nt) + (mm(h, l, nt) + mm(l, h, nt)) for h, l in halves]
    inverses = splits(triangle_inverses(grams))
    products = splits(dots3(inverses, halves))
    return [(*a, *split(r.T)) for a, r in zip(products, reflectors)]


def stored_factors(packed, a_ref, v_ref):
    for at, (ah, al, vh, vl) in enumerate(factors(packed)):
        a_ref[at, :, : 2 * W] = ah
        a_ref[at, :, 2 * W :] = al
        v_ref[at, :, :W] = vh
        v_ref[at, :, W:] = vl


def loaded(a_ref, v_ref, at):
    a, v = a_ref[at], v_ref[at]
    return a[:, : 2 * W], a[:, 2 * W :], v[:, :W], v[:, W:]


def slot_of(scalars, level, half):
    return scalars[3 + 2 * level + half]


def gathered(scalars, pieces, held, at):
    for k in range(4):
        held[(scalars[0] + 4 - k) % 4] = pieces[k][at]


def block_of(scalars, held, level, half):
    return held[2 * (level % 2) + slot_of(scalars, level, half)]


def applied(x, factor):
    ah, al, vh, vl = factor
    x_parts = split(x)
    z_parts = split(dot3((ah, al), x_parts))
    return x - dot3((vh, vl), z_parts)


def across(top, low, factor):
    middle = applied(jnp.concatenate([top[W:], low[:W]], axis=0), factor)
    return jnp.concatenate([top[:W], middle[:W]], axis=0), jnp.concatenate([middle[W:], low[W:]], axis=0)


def across_below(last, low, below, factor):
    new_low, new_below = across(low, jnp.where(last, 0.0, below), factor)
    return new_low, jnp.where(last, below, new_below)


def across_above(first, above, top, factor):
    new_above, new_top = across(above, top, factor)
    return new_above, jnp.where(first, top, new_top)


def order_kernel(plane, p0, p1, p2, p3, near, far, held):
    for k, piece in enumerate((p0, p1, p2, p3)):
        held[(plane[0] + 4 - k) % 4] = piece[...]
    near[...] = held[0:2]
    far[...] = held[2:4]


def first_kernel(scalars, x_ref, p0, p1, p2, p3, message, low_ref, a0, v0, held):
    pieces = (p0, p1, p2, p3)
    gathered(scalars, pieces, held, 1)
    message[2 * W :] = block_of(scalars, held, 2, 0)
    gathered(scalars, pieces, held, 0)
    stored_factors([block_of(scalars, held, level, half) for level in (0, 1) for half in (0, 1)], a0, v0)
    top = applied(x_ref[: 2 * W], loaded(a0, v0, 0))
    low = applied(x_ref[2 * W :], loaded(a0, v0, 1))
    top, low = across(top, low, loaded(a0, v0, 2))
    message[: 2 * W] = top
    low_ref[...] = low


def factor1_kernel(scalars, after, p0, p1, p2, p3, a1, v1, held):
    gathered(scalars, (p0, p1, p2, p3), held, 1)
    stored_factors([block_of(scalars, held, level, half) for level, half in ((2, 1), (3, 0), (3, 1))], a1, v1)


def second_kernel(scalars, low_ref, message, a0, v0, a1, v1, low_out, below_out):
    last = scalars[1] == 1
    (foreign,) = factors([message[2 * W :]])
    low, below = across_below(last, low_ref[...], message[: 2 * W], loaded(a0, v0, 3))
    low = applied(low, loaded(a1, v1, 0))
    below = applied(below, foreign)
    low, below = across_below(last, low, below, loaded(a1, v1, 2))
    low_out[...] = low
    below_out[...] = below


def choose_kernel(scalars, after, p0, p1, p2, p3, down, up, held):
    pieces = (p0, p1, p2, p3)
    gathered(scalars, pieces, held, 1)
    down[1] = block_of(scalars, held, 6, 1)
    down[2] = block_of(scalars, held, 7, 1)
    up[...] = block_of(scalars, held, 6, 0)
    gathered(scalars, pieces, held, 0)
    down[0] = block_of(scalars, held, 5, 1)


def factor2_kernel(scalars, after, p0, p1, p2, p3, a2, v2, held):
    gathered(scalars, (p0, p1, p2, p3), held, 0)
    stored_factors([block_of(scalars, held, level, half) for level in (4, 5) for half in (0, 1)], a2, v2)


def third_kernel(low_ref, top_ref, after1, after2, a1, v1, a2, v2, low_out, top_out):
    top, low = across(top_ref[...], low_ref[...], loaded(a1, v1, 1))
    top = applied(top, loaded(a2, v2, 0))
    low = applied(low, loaded(a2, v2, 1))
    top, low = across(top, low, loaded(a2, v2, 2))
    low_out[...] = low
    top_out[...] = top


def factor3_kernel(scalars, after, p0, p1, p2, p3, a3, v3, held):
    gathered(scalars, (p0, p1, p2, p3), held, 1)
    stored_factors([block_of(scalars, held, level, half) for level in (6, 7) for half in (0, 1)], a3, v3)


def factor4_kernel(after, down, up, a4, v4):
    stored_factors([down[0], down[1], down[2], up[...]], a4, v4)


def fourth_kernel(scalars, low_ref, top_ref, above_ref, below_ref, a2, v2, a3, v3, a4, v4, out_ref):
    last = scalars[1] == 1
    first = scalars[2] == 1
    low, below = across_below(last, low_ref[...], below_ref[...], loaded(a2, v2, 3))
    above, top = across_above(first, above_ref[...], top_ref[...], loaded(a4, v4, 0))
    above = applied(above, loaded(a4, v4, 1))
    top = applied(top, loaded(a3, v3, 0))
    low = applied(low, loaded(a3, v3, 1))
    below = applied(below, loaded(a4, v4, 3))
    _, top = across_above(first, above, top, loaded(a4, v4, 2))
    low, _ = across_below(last, low, below, loaded(a3, v3, 3))
    top, low = across(top, low, loaded(a3, v3, 2))
    out_ref[: 2 * W] = top
    out_ref[2 * W :] = low


def factor_shapes(count):
    return [jax.ShapeDtypeStruct((count, W, 4 * W), BF16), jax.ShapeDtypeStruct((count, 2 * W, 2 * W), BF16)]


def rows_shape(*shape):
    return jax.ShapeDtypeStruct(shape, F32)


HELD = [pltpu.VMEM((4, W, W), F32)]


def call(kernel, args, shapes, scratch=(), smem=1, flops=400_000_000):
    return pl.pallas_call(
        kernel,
        out_shape=tuple(shapes),
        in_specs=[pl.BlockSpec(memory_space=SMEM)] * smem + [pl.BlockSpec(memory_space=VMEM)] * (len(args) - smem),
        out_specs=(pl.BlockSpec(memory_space=VMEM),) * len(shapes),
        scratch_shapes=list(scratch),
        compiler_params=pltpu.CompilerParams(vmem_limit_bytes=24 * 1024 * 1024),
        cost_estimate=pl.CostEstimate(flops=flops, bytes_accessed=2_000_000, transcendentals=0),
        name=kernel.__name__,
    )(*args)


def shifted(value, axis, steps):
    count = lax.axis_size(axis)
    return lax.ppermute(value, axis, [(i, (i + steps) % count) for i in range(count)])


def along_x(value):
    return [value] + [lax.ppermute(value, "cols", [(i, (i // 4) * 4 + (i + k) % 4) for i in range(16)]) for k in (1, 2, 3)]


def per_device(eigvecs, wy_packed, slot_block):
    column = lax.axis_index("cols")
    row = lax.axis_index("rows")
    plane, place = column // 4, column % 4
    edges = jnp.stack([place, row == lax.axis_size("rows") - 1, row == 0]).astype(jnp.int32)
    scalars = jnp.concatenate([edges, slot_block.reshape(-1)])
    packed = wy_packed[0]
    half = rows_shape(2 * W, W)

    planes = [packed] + [shifted(packed, "cols", 4 * k) for k in (1, 2, 3)]
    pair = rows_shape(2, W, W)
    near, far = call(order_kernel, (plane.reshape(1), *planes), [pair, pair], HELD)
    near = along_x(near)
    far = along_x(far)
    message, low, a0, v0 = call(
        first_kernel, (scalars, eigvecs, *near), [rows_shape(3 * W, W), half, *factor_shapes(4)], HELD
    )
    message = shifted(message, "rows", -1)
    a1, v1 = call(factor1_kernel, (scalars, low, *near), factor_shapes(3), HELD)
    down, up = call(choose_kernel, (scalars, low, *far), [rows_shape(3, W, W), rows_shape(W, W)], HELD)
    down = shifted(down, "rows", 1)
    up = shifted(up, "rows", -1)
    low, below = call(second_kernel, (scalars, low, message, a0, v0, a1, v1), [half, half])
    top = shifted(below, "rows", 1)
    a2, v2 = call(factor2_kernel, (scalars, low, *far), factor_shapes(4), HELD)
    low, own = call(third_kernel, (low, top, up, down, a1, v1, a2, v2), [half, half], smem=0)
    above = shifted(low, "rows", 1)
    below = shifted(own, "rows", -1)
    a3, v3 = call(factor3_kernel, (scalars, low, *far), factor_shapes(4), HELD)
    a4, v4 = call(factor4_kernel, (low, down, up), factor_shapes(4), smem=0)
    return call(
        fourth_kernel, (scalars, low, own, above, below, a2, v2, a3, v3, a4, v4), [rows_shape(*eigvecs.shape)]
    )[0]


def solution(mesh):
    placed = (P("rows", "cols"), P(("rows", "cols"), None, None), P("rows", None, None))
    return jax.shard_map(
        per_device, mesh=mesh, in_specs=placed, out_specs=P("rows", "cols"), check_vma=False
    )
```

```python
import jax
import jax.numpy as jnp
from jax import lax
from jax.experimental import pallas as pl
from jax.experimental.pallas import tpu as pltpu
from jax.sharding import PartitionSpec as P

F32 = jnp.float32
BF16 = jnp.bfloat16
W = 128
SUB = 32
VMEM = pltpu.VMEM
SMEM = pltpu.SMEM


def split(x):
    high = x.astype(BF16)
    low = (x - high.astype(F32)).astype(BF16)
    return high, low


def mm(a, b, dims=((1,), (0,))):
    return lax.dot_general(a, b, (dims, ((), ())), preferred_element_type=F32)


def dot3(a, b):
    ah, al = a
    bh, bl = b
    return mm(ah, bh) + (mm(ah, bl) + mm(al, bh))


def unpacked(packed):
    wide = jnp.concatenate([packed.T, jnp.zeros((W, W), F32)], axis=1)
    return pltpu.roll(wide, 0, axis=1, stride=1, stride_axis=0)


def diagonal_inverses(grams):
    row = lax.broadcasted_iota(jnp.int32, (SUB, W), 0)
    lane = lax.broadcasted_iota(jnp.int32, (SUB, W), 1)
    group = lane // SUB
    place = lane % SUB
    base = group * SUB

    def prepared(gram):
        compact = gram[0:SUB]
        for d in range(1, 4):
            compact = jnp.where(group == d, gram[d * SUB : (d + 1) * SUB], compact)
        diagonal = jnp.sum(jnp.where(row == place, compact, 0.0), axis=0, keepdims=True)
        scale = jnp.broadcast_to(2.0 / diagonal, (SUB, W))
        return jnp.where(row < place, compact * scale, 0.0), scale

    pairs = [prepared(gram) for gram in grams]
    start = [jnp.where(row == place, 1.0, 0.0)[8 * i : 8 * i + 8] for i in range(4)]
    rows = [list(start) for _ in grams]
    for k in range(SUB - 1, 0, -1):
        tile, at = k // 8, k % 8
        for n in range(len(grams)):
            pivot = jnp.broadcast_to(rows[n][tile][at : at + 1], (8, W))
            for i in range(tile + 1):
                if i * 8 < k:
                    factor = jnp.take_along_axis(
                        pairs[n][0][8 * i : 8 * i + 8], base[8 * i : 8 * i + 8] + k, axis=1, mode="promise_in_bounds"
                    )
                    rows[n][i] = rows[n][i] - factor * pivot
    row_scales = [jnp.take_along_axis(scale, base + row, axis=1, mode="promise_in_bounds") for _, scale in pairs]
    return [jnp.concatenate(r, axis=0) * s for r, s in zip(rows, row_scales)]


def dots3(lefts, rights):
    return [dot3(a, b) for a, b in zip(lefts, rights)]


def splits(values):
    return [split(v) for v in values]


def triangle_inverses(grams):
    small = diagonal_inverses(grams)
    lane = lax.broadcasted_iota(jnp.int32, (SUB, W), 1)
    group = lane // SUB
    half = 2 * SUB
    zero = jnp.zeros((SUB, W), F32)
    zeros = jnp.zeros((half, W), F32)
    parts = [[jnp.where(group == d, s, 0.0) for d in range(4)] for s in small]
    bases = splits([jnp.concatenate(p, axis=0) for p in parts])
    corners = splits(
        [
            jnp.concatenate(
                [jnp.where(group == 1, g[0:SUB], 0.0), jnp.where(group == 3, g[2 * SUB : 3 * SUB], 0.0)], axis=0
            )
            for g in grams
        ]
    )
    lane2 = lax.broadcasted_iota(jnp.int32, (half, W), 1)
    corners2 = splits([jnp.where(lane2 >= half, g[0:half], 0.0) for g in grams])
    products = dots3(corners, bases)
    fulls = splits([jnp.concatenate([p[0:SUB], zero, p[SUB:], zero], axis=0) for p in products])
    changes = dots3(splits([jnp.concatenate([p[0], p[2]], axis=0) for p in parts]), fulls)
    uppers = [jnp.concatenate([p[0] - c[0:SUB], p[1]], axis=0) for p, c in zip(parts, changes)]
    lowers = [jnp.concatenate([p[2] - c[SUB:], p[3]], axis=0) for p, c in zip(parts, changes)]
    products = dots3(corners2, splits([jnp.concatenate([zeros, low], axis=0) for low in lowers]))
    changes = dots3(splits(uppers), splits([jnp.concatenate([p, zeros], axis=0) for p in products]))
    return [jnp.concatenate([u - c, low], axis=0) for u, c, low in zip(uppers, changes, lowers)]


def factors(packed):
    reflectors = [unpacked(p) for p in packed]
    halves = splits(reflectors)
    nt = ((1,), (1,))
    grams = [mm(h, h, nt) + (mm(h, l, nt) + mm(l, h, nt)) for h, l in halves]
    inverses = splits(triangle_inverses(grams))
    products = splits(dots3(inverses, halves))
    return [(*a, *split(r.T)) for a, r in zip(products, reflectors)]


def whole(factor):
    ah, al, vh, vl = factor
    return jnp.concatenate(split(dot3((vh, vl), (ah, al))), axis=1)


def stored_wholes(packed, g_ref):
    for at, factor in enumerate(factors(packed)):
        g_ref[at] = whole(factor)


def slot_of(scalars, level, half):
    return scalars[2 + 2 * level + half]


def gathered(scalars, pieces, held, at):
    for k in range(4):
        held[(scalars[0] + 4 - k) % 4] = pieces[k][at]


def block_of(scalars, held, level, half):
    return held[2 * (level % 2) + slot_of(scalars, level, half)]


def twice(factor):
    ah, al, vh, vl = factor

    def update(x):
        return x - dot3((vh, vl), split(dot3((ah, al), split(x))))

    return update


def once(g_ref, at):
    g = g_ref[at]

    def update(x):
        xh, xl = split(x)
        wide = mm(g[:, : 2 * W], jnp.concatenate([xh, xl], axis=1))
        return x - (wide[:, :W] + (wide[:, W:] + mm(g[:, 2 * W :], xh)))

    return update


def across(top, low, update):
    middle = update(jnp.concatenate([top[W:], low[:W]], axis=0))
    return jnp.concatenate([top[:W], middle[:W]], axis=0), jnp.concatenate([middle[W:], low[W:]], axis=0)


def across_below(last, low, below, update):
    new_low, new_below = across(low, jnp.where(last, 0.0, below), update)
    return new_low, jnp.where(last, below, new_below)


def order_kernel(plane, p0, p1, p2, p3, near, far, held):
    for k, piece in enumerate((p0, p1, p2, p3)):
        held[(plane[0] + 4 - k) % 4] = piece[...]
    near[...] = held[0:2]
    far[...] = held[2:4]


def first_kernel(scalars, x_ref, p0, p1, p2, p3, message, low_ref, held):
    pieces = (p0, p1, p2, p3)
    gathered(scalars, pieces, held, 1)
    message[2 * W :] = block_of(scalars, held, 2, 0)
    gathered(scalars, pieces, held, 0)
    found = factors([block_of(scalars, held, level, half) for level, half in ((0, 0), (0, 1), (1, 0))])
    top = twice(found[0])(x_ref[: 2 * W])
    low = twice(found[1])(x_ref[2 * W :])
    top, low = across(top, low, twice(found[2]))
    message[: 2 * W] = top
    low_ref[...] = low


def factor1_kernel(scalars, after, p0, p1, p2, p3, far, g1, sent, held):
    sent[...] = far[...]
    pieces = (p0, p1, p2, p3)
    gathered(scalars, pieces, held, 0)
    early = block_of(scalars, held, 1, 1)
    gathered(scalars, pieces, held, 1)
    late = [block_of(scalars, held, level, half) for level, half in ((2, 1), (3, 0), (3, 1))]
    stored_wholes([*late, early], g1)


def second_kernel(scalars, low_ref, message, g1, low_out, below_out):
    last = scalars[1] == 1
    (foreign,) = factors([message[2 * W :]])
    low, below = across_below(last, low_ref[...], message[: 2 * W], once(g1, 3))
    low = once(g1, 0)(low)
    below = twice(foreign)(below)
    low, below = across_below(last, low, below, once(g1, 2))
    low_out[...] = low
    below_out[...] = below


def choose_kernel(scalars, after, p0, p1, p2, p3, up, held):
    gathered(scalars, (p0, p1, p2, p3), held, 1)
    up[...] = block_of(scalars, held, 6, 0)


def factor2_kernel(scalars, after, p0, p1, p2, p3, g2, held):
    gathered(scalars, (p0, p1, p2, p3), held, 0)
    stored_wholes([block_of(scalars, held, level, half) for level in (4, 5) for half in (0, 1)], g2)


def third_kernel(low_ref, top_ref, after, g1, g2, low_out, top_out):
    top, low = across(top_ref[...], low_ref[...], once(g1, 1))
    top = once(g2, 0)(top)
    low = once(g2, 1)(low)
    top, low = across(top, low, once(g2, 2))
    low_out[...] = low
    top_out[...] = top


def factor3_kernel(scalars, after, up, p0, p1, p2, p3, g3, held):
    gathered(scalars, (p0, p1, p2, p3), held, 1)
    own = [block_of(scalars, held, level, half) for level, half in ((6, 1), (7, 0), (7, 1))]
    stored_wholes([*own, up[...]], g3)


def fourth_kernel(scalars, low_ref, below_ref, g2, g3, low_out, below_out):
    last = scalars[1] == 1
    low, below = across_below(last, low_ref[...], below_ref[...], once(g2, 3))
    low = once(g3, 0)(low)
    below = once(g3, 3)(below)
    low, below = across_below(last, low, below, once(g3, 2))
    low_out[...] = low
    below_out[...] = below


def last_kernel(low_ref, top_ref, g3, out_ref):
    top, low = across(top_ref[...], low_ref[...], once(g3, 1))
    out_ref[: 2 * W] = top
    out_ref[2 * W :] = low


def wholes(count):
    return jax.ShapeDtypeStruct((count, 2 * W, 4 * W), BF16)


def rows_shape(*shape):
    return jax.ShapeDtypeStruct(shape, F32)


HELD = [pltpu.VMEM((4, W, W), F32)]


def call(kernel, args, shapes, scratch=(), smem=1, flops=400_000_000):
    return pl.pallas_call(
        kernel,
        out_shape=tuple(shapes),
        in_specs=[pl.BlockSpec(memory_space=SMEM)] * smem + [pl.BlockSpec(memory_space=VMEM)] * (len(args) - smem),
        out_specs=(pl.BlockSpec(memory_space=VMEM),) * len(shapes),
        scratch_shapes=list(scratch),
        compiler_params=pltpu.CompilerParams(vmem_limit_bytes=24 * 1024 * 1024),
        cost_estimate=pl.CostEstimate(flops=flops, bytes_accessed=2_000_000, transcendentals=0),
        name=kernel.__name__,
    )(*args)


def shifted(value, axis, steps):
    count = lax.axis_size(axis)
    return lax.ppermute(value, axis, [(i, (i + steps) % count) for i in range(count)])


def along_x(value):
    return [value] + [lax.ppermute(value, "cols", [(i, (i // 4) * 4 + (i + k) % 4) for i in range(16)]) for k in (1, 2, 3)]


def per_device(eigvecs, wy_packed, slot_block):
    column = lax.axis_index("cols")
    row = lax.axis_index("rows")
    plane, place = column // 4, column % 4
    edges = jnp.stack([place, row == lax.axis_size("rows") - 1]).astype(jnp.int32)
    scalars = jnp.concatenate([edges, slot_block.reshape(-1)])
    packed = wy_packed[0]
    half = rows_shape(2 * W, W)

    planes = [packed] + [shifted(packed, "cols", 4 * k) for k in (1, 2, 3)]
    pair = rows_shape(2, W, W)
    near, far = call(order_kernel, (plane.reshape(1), *planes), [pair, pair], HELD)
    near = along_x(near)
    message, low = call(first_kernel, (scalars, eigvecs, *near), [rows_shape(3 * W, W), half], HELD)
    message = shifted(message, "rows", -1)
    g1, far = call(factor1_kernel, (scalars, low, *near, far), [wholes(4), pair], HELD)
    far = along_x(far)
    low, below = call(second_kernel, (scalars, low, message, g1), [half, half])
    top = shifted(below, "rows", 1)
    (up,) = call(choose_kernel, (scalars, low, *far), [rows_shape(W, W)], HELD)
    (g2,) = call(factor2_kernel, (scalars, up, *far), [wholes(4)], HELD)
    up = shifted(up, "rows", -1)
    low, top = call(third_kernel, (low, top, up, g1, g2), [half, half], smem=0)
    below = shifted(top, "rows", -1)
    (g3,) = call(factor3_kernel, (scalars, low, up, *far), [wholes(4)], HELD)
    low, below = call(fourth_kernel, (scalars, low, below, g2, g3), [half, half])
    top = shifted(below, "rows", 1)
    return call(last_kernel, (low, top, g3), [rows_shape(*eigvecs.shape)], smem=0)[0]


def solution(mesh):
    placed = (P("rows", "cols"), P(("rows", "cols"), None, None), P("rows", None, None))
    return jax.shard_map(
        per_device, mesh=mesh, in_specs=placed, out_specs=P("rows", "cols"), check_vma=False
    )
```

```python
import jax
import jax.numpy as jnp
from jax import lax
from jax.experimental import pallas as pl
from jax.experimental.pallas import tpu as pltpu
from jax.sharding import PartitionSpec as P

F32 = jnp.float32
BF16 = jnp.bfloat16
W = 128
SUB = 32
VMEM = pltpu.VMEM
SMEM = pltpu.SMEM


def split(x):
    high = x.astype(BF16)
    low = (x - high.astype(F32)).astype(BF16)
    return high, low


def mm(a, b, dims=((1,), (0,))):
    return lax.dot_general(a, b, (dims, ((), ())), preferred_element_type=F32)


def dot3(a, b):
    ah, al = a
    bh, bl = b
    return mm(ah, bh) + (mm(ah, bl) + mm(al, bh))


def unpacked(packed):
    wide = jnp.concatenate([packed.T, jnp.zeros((W, W), F32)], axis=1)
    return pltpu.roll(wide, 0, axis=1, stride=1, stride_axis=0)


def diagonal_inverses(grams):
    row = lax.broadcasted_iota(jnp.int32, (SUB, W), 0)
    lane = lax.broadcasted_iota(jnp.int32, (SUB, W), 1)
    group = lane // SUB
    place = lane % SUB
    base = group * SUB

    def prepared(gram):
        compact = gram[0:SUB]
        for d in range(1, 4):
            compact = jnp.where(group == d, gram[d * SUB : (d + 1) * SUB], compact)
        diagonal = jnp.sum(jnp.where(row == place, compact, 0.0), axis=0, keepdims=True)
        scale = jnp.broadcast_to(2.0 / diagonal, (SUB, W))
        return jnp.where(row < place, compact * scale, 0.0), scale

    pairs = [prepared(gram) for gram in grams]
    start = [jnp.where(row == place, 1.0, 0.0)[8 * i : 8 * i + 8] for i in range(4)]
    rows = [list(start) for _ in grams]
    for k in range(SUB - 1, 0, -1):
        tile, at = k // 8, k % 8
        for n in range(len(grams)):
            pivot = jnp.broadcast_to(rows[n][tile][at : at + 1], (8, W))
            for i in range(tile + 1):
                if i * 8 < k:
                    factor = jnp.take_along_axis(
                        pairs[n][0][8 * i : 8 * i + 8], base[8 * i : 8 * i + 8] + k, axis=1, mode="promise_in_bounds"
                    )
                    rows[n][i] = rows[n][i] - factor * pivot
    row_scales = [jnp.take_along_axis(scale, base + row, axis=1, mode="promise_in_bounds") for _, scale in pairs]
    return [jnp.concatenate(r, axis=0) * s for r, s in zip(rows, row_scales)]


def dots3(lefts, rights):
    return [dot3(a, b) for a, b in zip(lefts, rights)]


def splits(values):
    return [split(v) for v in values]


def triangle_inverses(grams):
    small = diagonal_inverses(grams)
    lane = lax.broadcasted_iota(jnp.int32, (SUB, W), 1)
    group = lane // SUB
    half = 2 * SUB
    zero = jnp.zeros((SUB, W), F32)
    zeros = jnp.zeros((half, W), F32)
    parts = [[jnp.where(group == d, s, 0.0) for d in range(4)] for s in small]
    bases = splits([jnp.concatenate(p, axis=0) for p in parts])
    corners = splits(
        [
            jnp.concatenate(
                [jnp.where(group == 1, g[0:SUB], 0.0), jnp.where(group == 3, g[2 * SUB : 3 * SUB], 0.0)], axis=0
            )
            for g in grams
        ]
    )
    lane2 = lax.broadcasted_iota(jnp.int32, (half, W), 1)
    corners2 = splits([jnp.where(lane2 >= half, g[0:half], 0.0) for g in grams])
    products = dots3(corners, bases)
    fulls = splits([jnp.concatenate([p[0:SUB], zero, p[SUB:], zero], axis=0) for p in products])
    changes = dots3(splits([jnp.concatenate([p[0], p[2]], axis=0) for p in parts]), fulls)
    uppers = [jnp.concatenate([p[0] - c[0:SUB], p[1]], axis=0) for p, c in zip(parts, changes)]
    lowers = [jnp.concatenate([p[2] - c[SUB:], p[3]], axis=0) for p, c in zip(parts, changes)]
    products = dots3(corners2, splits([jnp.concatenate([zeros, low], axis=0) for low in lowers]))
    changes = dots3(splits(uppers), splits([jnp.concatenate([p, zeros], axis=0) for p in products]))
    return [jnp.concatenate([u - c, low], axis=0) for u, c, low in zip(uppers, changes, lowers)]


def factors(packed):
    reflectors = [unpacked(p) for p in packed]
    halves = splits(reflectors)
    nt = ((1,), (1,))
    grams = [mm(h, h, nt) + (mm(h, l, nt) + mm(l, h, nt)) for h, l in halves]
    inverses = splits(triangle_inverses(grams))
    products = splits(dots3(inverses, halves))
    return [(*a, *split(r.T)) for a, r in zip(products, reflectors)]


def whole(factor):
    ah, al, vh, vl = factor
    return jnp.concatenate(split(dot3((vh, vl), (ah, al))), axis=1)


def stored_wholes(packed, g_ref):
    for at, factor in enumerate(factors(packed)):
        g_ref[at] = whole(factor)


def slot_of(scalars, level, half):
    return scalars[3 + 2 * level + half]


def gathered(scalars, pieces, held, at):
    for k in range(4):
        held[(scalars[0] + 4 - k) % 4] = pieces[k][at]


def block_of(scalars, held, level, half):
    return held[2 * (level % 2) + slot_of(scalars, level, half)]


def twice(factor):
    ah, al, vh, vl = factor

    def update(x):
        return x - dot3((vh, vl), split(dot3((ah, al), split(x))))

    return update


def once(g_ref, at):
    g = g_ref[at]

    def update(x):
        xh, xl = split(x)
        wide = mm(g[:, : 2 * W], jnp.concatenate([xh, xl], axis=1))
        return x - (wide[:, :W] + (wide[:, W:] + mm(g[:, 2 * W :], xh)))

    return update


def across(top, low, update):
    middle = update(jnp.concatenate([top[W:], low[:W]], axis=0))
    return jnp.concatenate([top[:W], middle[:W]], axis=0), jnp.concatenate([middle[W:], low[W:]], axis=0)


def across_below(last, low, below, update):
    return across(low, jnp.where(last, 0.0, below), update)


def order_kernel(plane, p0, p1, p2, p3, near, far, held):
    for k, piece in enumerate((p0, p1, p2, p3)):
        held[(plane[0] + 4 - k) % 4] = piece[...]
    near[...] = held[0:2]
    far[...] = held[2:4]


def first_kernel(scalars, x_ref, p0, p1, p2, p3, message, low_ref, held):
    pieces = (p0, p1, p2, p3)
    gathered(scalars, pieces, held, 1)
    message[2 * W :] = block_of(scalars, held, 2, 0)
    gathered(scalars, pieces, held, 0)
    found = factors([block_of(scalars, held, level, half) for level, half in ((0, 0), (0, 1), (1, 0))])
    top = twice(found[0])(x_ref[: 2 * W])
    low = twice(found[1])(x_ref[2 * W :])
    top, low = across(top, low, twice(found[2]))
    message[: 2 * W] = top
    low_ref[...] = low


def factor1_kernel(scalars, after, p0, p1, p2, p3, far, g1, sent, held):
    sent[...] = far[...]
    pieces = (p0, p1, p2, p3)
    gathered(scalars, pieces, held, 0)
    early = block_of(scalars, held, 1, 1)
    gathered(scalars, pieces, held, 1)
    late = [block_of(scalars, held, level, half) for level, half in ((2, 1), (3, 0), (3, 1))]
    stored_wholes([*late, early, block_of(scalars, held, 2, 0)], g1)


def second_kernel(scalars, low_ref, own, message, g1, low_out, below_out, top_out):
    last = scalars[1] == 1
    (foreign,) = factors([message[2 * W :]])
    low, below = across_below(last, low_ref[...], message[: 2 * W], once(g1, 3))
    low = once(g1, 0)(low)
    below = twice(foreign)(below)
    top_out[...] = once(g1, 4)(own[: 2 * W])
    low, below = across_below(last, low, below, once(g1, 2))
    low_out[...] = low
    below_out[...] = below


def factor2_kernel(scalars, after, p0, p1, p2, p3, g2, up, held):
    pieces = (p0, p1, p2, p3)
    gathered(scalars, pieces, held, 1)
    up[...] = block_of(scalars, held, 6, 0)
    gathered(scalars, pieces, held, 0)
    stored_wholes([block_of(scalars, held, level, half) for level in (4, 5) for half in (0, 1)], g2)


def third_kernel(scalars, low_ref, mine, top_ref, up, g1, g2, low_out, message):
    message[2 * W :] = up[...]
    top = jnp.where(scalars[2] == 1, mine[...], top_ref[...])
    top, low = across(top, low_ref[...], once(g1, 1))
    top = once(g2, 0)(top)
    low = once(g2, 1)(low)
    top, low = across(top, low, once(g2, 2))
    low_out[...] = low
    message[: 2 * W] = top


def factor3_kernel(scalars, after, p0, p1, p2, p3, g3, held):
    gathered(scalars, (p0, p1, p2, p3), held, 1)
    stored_wholes([block_of(scalars, held, level, half) for level, half in ((6, 1), (7, 0), (7, 1), (6, 0))], g3)


def fourth_kernel(scalars, low_ref, own, message, g2, g3, low_out, below_out, top_out):
    last = scalars[1] == 1
    (foreign,) = factors([message[2 * W :]])
    low, below = across_below(last, low_ref[...], message[: 2 * W], once(g2, 3))
    low = once(g3, 0)(low)
    below = twice(foreign)(below)
    top_out[...] = once(g3, 3)(own[: 2 * W])
    low, below = across_below(last, low, below, once(g3, 2))
    low_out[...] = low
    below_out[...] = below


def last_kernel(scalars, low_ref, mine, top_ref, g3, out_ref):
    top = jnp.where(scalars[2] == 1, mine[...], top_ref[...])
    top, low = across(top, low_ref[...], once(g3, 1))
    out_ref[: 2 * W] = top
    out_ref[2 * W :] = low


def wholes(count):
    return jax.ShapeDtypeStruct((count, 2 * W, 4 * W), BF16)


def rows_shape(*shape):
    return jax.ShapeDtypeStruct(shape, F32)


HELD = [pltpu.VMEM((4, W, W), F32)]


def call(kernel, args, shapes, scratch=(), smem=1, flops=400_000_000):
    return pl.pallas_call(
        kernel,
        out_shape=tuple(shapes),
        in_specs=[pl.BlockSpec(memory_space=SMEM)] * smem + [pl.BlockSpec(memory_space=VMEM)] * (len(args) - smem),
        out_specs=(pl.BlockSpec(memory_space=VMEM),) * len(shapes),
        scratch_shapes=list(scratch),
        compiler_params=pltpu.CompilerParams(vmem_limit_bytes=24 * 1024 * 1024),
        cost_estimate=pl.CostEstimate(flops=flops, bytes_accessed=2_000_000, transcendentals=0),
        name=kernel.__name__,
    )(*args)


def shifted(value, axis, steps):
    count = lax.axis_size(axis)
    return lax.ppermute(value, axis, [(i, (i + steps) % count) for i in range(count)])


def to_neighbour(value, steps):
    count = lax.axis_size("rows")
    return lax.ppermute(value, "rows", [(i, i + steps) for i in range(count) if 0 <= i + steps < count])


def along_x(value):
    return [value] + [lax.ppermute(value, "cols", [(i, (i // 4) * 4 + (i + k) % 4) for i in range(16)]) for k in (1, 2, 3)]


def per_device(eigvecs, wy_packed, slot_block):
    column = lax.axis_index("cols")
    row = lax.axis_index("rows")
    plane, place = column // 4, column % 4
    edges = jnp.stack([place, row == lax.axis_size("rows") - 1, row == 0]).astype(jnp.int32)
    scalars = jnp.concatenate([edges, slot_block.reshape(-1)])
    packed = wy_packed[0]
    half = rows_shape(2 * W, W)

    planes = [packed] + [shifted(packed, "cols", 4 * k) for k in (1, 2, 3)]
    pair = rows_shape(2, W, W)
    near, far = call(order_kernel, (plane.reshape(1), *planes), [pair, pair], HELD)
    near = along_x(near)
    three = rows_shape(3 * W, W)
    own, low = call(first_kernel, (scalars, eigvecs, *near), [three, half], HELD)
    message = to_neighbour(own, -1)
    g1, far = call(factor1_kernel, (scalars, low, *near, far), [wholes(5), pair], HELD)
    far = along_x(far)
    low, below, mine = call(second_kernel, (scalars, low, own, message, g1), [half, half, half])
    top = to_neighbour(below, 1)
    g2, up = call(factor2_kernel, (scalars, low, *far), [wholes(4), rows_shape(W, W)], HELD)
    low, own = call(third_kernel, (scalars, low, mine, top, up, g1, g2), [half, three])
    message = to_neighbour(own, -1)
    (g3,) = call(factor3_kernel, (scalars, low, *far), [wholes(4)], HELD)
    low, below, mine = call(fourth_kernel, (scalars, low, own, message, g2, g3), [half, half, half])
    top = to_neighbour(below, 1)
    return call(last_kernel, (scalars, low, mine, top, g3), [rows_shape(*eigvecs.shape)])[0]


def solution(mesh):
    placed = (P("rows", "cols"), P(("rows", "cols"), None, None), P("rows", None, None))
    return jax.shard_map(
        per_device, mesh=mesh, in_specs=placed, out_specs=P("rows", "cols"), check_vma=False
    )
```

```python
import jax
import jax.numpy as jnp
from jax import lax
from jax.experimental import pallas as pl
from jax.experimental.pallas import tpu as pltpu
from jax.sharding import PartitionSpec as P

F32 = jnp.float32
BF16 = jnp.bfloat16
W = 128
SUB = 32
VMEM = pltpu.VMEM
SMEM = pltpu.SMEM


def split(x):
    high = x.astype(BF16)
    low = (x - high.astype(F32)).astype(BF16)
    return high, low


def mm(a, b, dims=((1,), (0,))):
    return lax.dot_general(a, b, (dims, ((), ())), preferred_element_type=F32)


def dot3(a, b):
    ah, al = a
    bh, bl = b
    return mm(ah, bh) + (mm(ah, bl) + mm(al, bh))


def unpacked(packed):
    wide = jnp.concatenate([packed.T, jnp.zeros((W, W), F32)], axis=1)
    return pltpu.roll(wide, 0, axis=1, stride=1, stride_axis=0)


def diagonal_inverses(grams):
    row = lax.broadcasted_iota(jnp.int32, (SUB, W), 0)
    lane = lax.broadcasted_iota(jnp.int32, (SUB, W), 1)
    group = lane // SUB
    place = lane % SUB
    base = group * SUB

    def prepared(gram):
        compact = gram[0:SUB]
        for d in range(1, 4):
            compact = jnp.where(group == d, gram[d * SUB : (d + 1) * SUB], compact)
        diagonal = jnp.sum(jnp.where(row == place, compact, 0.0), axis=0, keepdims=True)
        scale = jnp.broadcast_to(2.0 / diagonal, (SUB, W))
        return jnp.where(row < place, compact * scale, 0.0), scale

    pairs = [prepared(gram) for gram in grams]
    start = [jnp.where(row == place, 1.0, 0.0)[8 * i : 8 * i + 8] for i in range(4)]
    rows = [list(start) for _ in grams]
    for k in range(SUB - 1, 0, -1):
        tile, at = k // 8, k % 8
        for n in range(len(grams)):
            pivot = jnp.broadcast_to(rows[n][tile][at : at + 1], (8, W))
            for i in range(tile + 1):
                if i * 8 < k:
                    factor = jnp.take_along_axis(
                        pairs[n][0][8 * i : 8 * i + 8], base[8 * i : 8 * i + 8] + k, axis=1, mode="promise_in_bounds"
                    )
                    rows[n][i] = rows[n][i] - factor * pivot
    row_scales = [jnp.take_along_axis(scale, base + row, axis=1, mode="promise_in_bounds") for _, scale in pairs]
    return [jnp.concatenate(r, axis=0) * s for r, s in zip(rows, row_scales)]


def dots3(lefts, rights):
    return [dot3(a, b) for a, b in zip(lefts, rights)]


def splits(values):
    return [split(v) for v in values]


def triangle_inverses(grams):
    small = diagonal_inverses(grams)
    lane = lax.broadcasted_iota(jnp.int32, (SUB, W), 1)
    group = lane // SUB
    half = 2 * SUB
    zero = jnp.zeros((SUB, W), F32)
    zeros = jnp.zeros((half, W), F32)
    parts = [[jnp.where(group == d, s, 0.0) for d in range(4)] for s in small]
    bases = splits([jnp.concatenate(p, axis=0) for p in parts])
    corners = splits(
        [
            jnp.concatenate(
                [jnp.where(group == 1, g[0:SUB], 0.0), jnp.where(group == 3, g[2 * SUB : 3 * SUB], 0.0)], axis=0
            )
            for g in grams
        ]
    )
    lane2 = lax.broadcasted_iota(jnp.int32, (half, W), 1)
    corners2 = splits([jnp.where(lane2 >= half, g[0:half], 0.0) for g in grams])
    products = dots3(corners, bases)
    fulls = splits([jnp.concatenate([p[0:SUB], zero, p[SUB:], zero], axis=0) for p in products])
    changes = dots3(splits([jnp.concatenate([p[0], p[2]], axis=0) for p in parts]), fulls)
    uppers = [jnp.concatenate([p[0] - c[0:SUB], p[1]], axis=0) for p, c in zip(parts, changes)]
    lowers = [jnp.concatenate([p[2] - c[SUB:], p[3]], axis=0) for p, c in zip(parts, changes)]
    products = dots3(corners2, splits([jnp.concatenate([zeros, low], axis=0) for low in lowers]))
    changes = dots3(splits(uppers), splits([jnp.concatenate([p, zeros], axis=0) for p in products]))
    return [jnp.concatenate([u - c, low], axis=0) for u, c, low in zip(uppers, changes, lowers)]


def factors(packed):
    reflectors = [unpacked(p) for p in packed]
    halves = splits(reflectors)
    nt = ((1,), (1,))
    grams = [mm(h, h, nt) + (mm(h, l, nt) + mm(l, h, nt)) for h, l in halves]
    inverses = splits(triangle_inverses(grams))
    products = splits(dots3(inverses, halves))
    return [(*a, *split(r.T)) for a, r in zip(products, reflectors)]


def whole(factor):
    ah, al, vh, vl = factor
    return jnp.concatenate(split(dot3((vh, vl), (ah, al))), axis=1)


def stored_wholes(packed, g_ref):
    for at, factor in enumerate(factors(packed)):
        g_ref[at] = whole(factor)


def slot_of(scalars, level, half):
    return scalars[3 + 2 * level + half]


def gathered(scalars, pieces, held, at):
    for k in range(4):
        held[(scalars[0] + 4 - k) % 4] = pieces[k][at]


def block_of(scalars, held, level, half):
    return held[2 * (level % 2) + slot_of(scalars, level, half)]


def twice(factor):
    ah, al, vh, vl = factor

    def update(x):
        return x - dot3((vh, vl), split(dot3((ah, al), split(x))))

    return update


def once(g_ref, at):
    g = g_ref[at]

    def update(x):
        xh, xl = split(x)
        wide = mm(g[:, : 2 * W], jnp.concatenate([xh, xl], axis=1))
        return x - (wide[:, :W] + (wide[:, W:] + mm(g[:, 2 * W :], xh)))

    return update


def across(top, low, update):
    middle = update(jnp.concatenate([top[W:], low[:W]], axis=0))
    return jnp.concatenate([top[:W], middle[:W]], axis=0), jnp.concatenate([middle[W:], low[W:]], axis=0)


def across_below(last, low, below, update):
    return across(low, jnp.where(last, 0.0, below), update)


def across_above(first, above, top, update):
    new_above, new_top = across(above, top, update)
    return new_above, jnp.where(first, top, new_top)


def order_kernel(plane, p0, p1, p2, p3, near, far, held):
    for k, piece in enumerate((p0, p1, p2, p3)):
        held[(plane[0] + 4 - k) % 4] = piece[...]
    near[...] = held[0:2]
    far[...] = held[2:4]


def first_kernel(scalars, x_ref, p0, p1, p2, p3, message, low_ref, held):
    pieces = (p0, p1, p2, p3)
    gathered(scalars, pieces, held, 1)
    message[2 * W :] = block_of(scalars, held, 2, 0)
    gathered(scalars, pieces, held, 0)
    found = factors([block_of(scalars, held, level, half) for level, half in ((0, 0), (0, 1), (1, 0))])
    top = twice(found[0])(x_ref[: 2 * W])
    low = twice(found[1])(x_ref[2 * W :])
    top, low = across(top, low, twice(found[2]))
    message[: 2 * W] = top
    low_ref[...] = low


def factor1_kernel(scalars, after, p0, p1, p2, p3, far, g1, sent, held):
    sent[...] = far[...]
    pieces = (p0, p1, p2, p3)
    gathered(scalars, pieces, held, 0)
    early = block_of(scalars, held, 1, 1)
    gathered(scalars, pieces, held, 1)
    late = [block_of(scalars, held, level, half) for level, half in ((2, 1), (3, 0), (3, 1))]
    stored_wholes([*late, early, block_of(scalars, held, 2, 0)], g1)


def second_kernel(scalars, low_ref, own, message, g1, low_out, below_out, top_out):
    last = scalars[1] == 1
    (foreign,) = factors([message[2 * W :]])
    low, below = across_below(last, low_ref[...], message[: 2 * W], once(g1, 3))
    low = once(g1, 0)(low)
    below = twice(foreign)(below)
    top_out[...] = once(g1, 4)(own[: 2 * W])
    low, below = across_below(last, low, below, once(g1, 2))
    low_out[...] = low
    below_out[...] = below


def factor2_kernel(scalars, after, p0, p1, p2, p3, g2, up, down, held):
    pieces = (p0, p1, p2, p3)
    gathered(scalars, pieces, held, 1)
    up[...] = block_of(scalars, held, 6, 0)
    down[1] = block_of(scalars, held, 6, 1)
    down[2] = block_of(scalars, held, 7, 1)
    gathered(scalars, pieces, held, 0)
    down[0] = block_of(scalars, held, 5, 1)
    stored_wholes([block_of(scalars, held, level, half) for level in (4, 5) for half in (0, 1)], g2)


def third_kernel(scalars, low_ref, mine, top_ref, up, g1, g2, low_out, message):
    message[2 * W :] = up[...]
    top = jnp.where(scalars[2] == 1, mine[...], top_ref[...])
    top, low = across(top, low_ref[...], once(g1, 1))
    top = once(g2, 0)(top)
    low = once(g2, 1)(low)
    top, low = across(top, low, once(g2, 2))
    low_out[...] = low
    message[: 2 * W] = top


def factor3_kernel(scalars, after, p0, p1, p2, p3, g3, held):
    gathered(scalars, (p0, p1, p2, p3), held, 1)
    stored_wholes([block_of(scalars, held, level, half) for level, half in ((6, 0), (6, 1), (7, 0), (7, 1))], g3)


def factor4_kernel(after, down, g4):
    stored_wholes([down[0], down[1], down[2]], g4)


def fourth_kernel(scalars, low_ref, own, above_ref, message, g2, g3, g4, out_ref):
    last = scalars[1] == 1
    first = scalars[2] == 1
    (foreign,) = factors([message[2 * W :]])
    low, below = across_below(last, low_ref[...], message[: 2 * W], once(g2, 3))
    above, top = across_above(first, above_ref[...], own[: 2 * W], once(g4, 0))
    above = once(g4, 1)(above)
    top = once(g3, 0)(top)
    low = once(g3, 1)(low)
    _, top = across_above(first, above, top, once(g4, 2))
    below = twice(foreign)(below)
    low, _ = across_below(last, low, below, once(g3, 3))
    top, low = across(top, low, once(g3, 2))
    out_ref[: 2 * W] = top
    out_ref[2 * W :] = low


def wholes(count):
    return jax.ShapeDtypeStruct((count, 2 * W, 4 * W), BF16)


def rows_shape(*shape):
    return jax.ShapeDtypeStruct(shape, F32)


HELD = [pltpu.VMEM((4, W, W), F32)]


def call(kernel, args, shapes, scratch=(), smem=1, flops=400_000_000):
    return pl.pallas_call(
        kernel,
        out_shape=tuple(shapes),
        in_specs=[pl.BlockSpec(memory_space=SMEM)] * smem + [pl.BlockSpec(memory_space=VMEM)] * (len(args) - smem),
        out_specs=(pl.BlockSpec(memory_space=VMEM),) * len(shapes),
        scratch_shapes=list(scratch),
        compiler_params=pltpu.CompilerParams(vmem_limit_bytes=24 * 1024 * 1024),
        cost_estimate=pl.CostEstimate(flops=flops, bytes_accessed=2_000_000, transcendentals=0),
        name=kernel.__name__,
    )(*args)


def shifted(value, axis, steps):
    count = lax.axis_size(axis)
    return lax.ppermute(value, axis, [(i, (i + steps) % count) for i in range(count)])


def to_neighbour(value, steps):
    count = lax.axis_size("rows")
    return lax.ppermute(value, "rows", [(i, i + steps) for i in range(count) if 0 <= i + steps < count])


def along_x(value):
    found = {k: lax.ppermute(value, "cols", [(i, (i // 4) * 4 + (i + k) % 4) for i in range(16)]) for k in (1, 3, 2)}
    return [value, found[1], found[2], found[3]]


def per_device(eigvecs, wy_packed, slot_block):
    column = lax.axis_index("cols")
    row = lax.axis_index("rows")
    plane, place = column // 4, column % 4
    edges = jnp.stack([place, row == lax.axis_size("rows") - 1, row == 0]).astype(jnp.int32)
    scalars = jnp.concatenate([edges, slot_block.reshape(-1)])
    packed = wy_packed[0]
    half = rows_shape(2 * W, W)

    planes = [packed] + [shifted(packed, "cols", 4 * k) for k in (1, 2, 3)]
    pair = rows_shape(2, W, W)
    near, far = call(order_kernel, (plane.reshape(1), *planes), [pair, pair], HELD)
    near = along_x(near)
    three = rows_shape(3 * W, W)
    own, low = call(first_kernel, (scalars, eigvecs, *near), [three, half], HELD)
    message = to_neighbour(own, -1)
    g1, far = call(factor1_kernel, (scalars, low, *near, far), [wholes(5), pair], HELD)
    far = along_x(far)
    low, below, mine = call(second_kernel, (scalars, low, own, message, g1), [half, half, half])
    top = to_neighbour(below, 1)
    blocks = [wholes(4), rows_shape(W, W), rows_shape(3, W, W)]
    g2, up, down = call(factor2_kernel, (scalars, low, *far), blocks, HELD)
    down = to_neighbour(down, 1)
    low, own = call(third_kernel, (scalars, low, mine, top, up, g1, g2), [half, three])
    above = to_neighbour(low, 1)
    message = to_neighbour(own, -1)
    (g3,) = call(factor3_kernel, (scalars, low, *far), [wholes(4)], HELD)
    (g4,) = call(factor4_kernel, (low, down), [wholes(3)], smem=0)
    return call(
        fourth_kernel, (scalars, low, own, above, message, g2, g3, g4), [rows_shape(*eigvecs.shape)]
    )[0]


def solution(mesh):
    placed = (P("rows", "cols"), P(("rows", "cols"), None, None), P("rows", None, None))
    return jax.shard_map(
        per_device, mesh=mesh, in_specs=placed, out_specs=P("rows", "cols"), check_vma=False
    )
```

```python
import jax
import jax.numpy as jnp
from jax import lax
from jax.experimental import pallas as pl
from jax.experimental.pallas import tpu as pltpu
from jax.sharding import PartitionSpec as P

F32 = jnp.float32
BF16 = jnp.bfloat16
W = 128
SUB = 32
VMEM = pltpu.VMEM
SMEM = pltpu.SMEM


def split(x):
    high = x.astype(BF16)
    low = (x - high.astype(F32)).astype(BF16)
    return high, low


def mm(a, b, dims=((1,), (0,))):
    return lax.dot_general(a, b, (dims, ((), ())), preferred_element_type=F32)


def dot3(a, b):
    ah, al = a
    bh, bl = b
    return mm(ah, bh) + (mm(ah, bl) + mm(al, bh))


def unpacked(packed):
    wide = jnp.concatenate([packed.T, jnp.zeros((W, W), F32)], axis=1)
    return pltpu.roll(wide, 0, axis=1, stride=1, stride_axis=0)


def diagonal_inverses(grams):
    row = lax.broadcasted_iota(jnp.int32, (SUB, W), 0)
    lane = lax.broadcasted_iota(jnp.int32, (SUB, W), 1)
    group = lane // SUB
    place = lane % SUB
    base = group * SUB

    def prepared(gram):
        compact = gram[0:SUB]
        for d in range(1, 4):
            compact = jnp.where(group == d, gram[d * SUB : (d + 1) * SUB], compact)
        diagonal = jnp.sum(jnp.where(row == place, compact, 0.0), axis=0, keepdims=True)
        scale = jnp.broadcast_to(2.0 / diagonal, (SUB, W))
        return jnp.where(row < place, compact * scale, 0.0), scale

    pairs = [prepared(gram) for gram in grams]
    start = [jnp.where(row == place, 1.0, 0.0)[8 * i : 8 * i + 8] for i in range(4)]
    rows = [list(start) for _ in grams]
    for k in range(SUB - 1, 0, -1):
        tile, at = k // 8, k % 8
        for n in range(len(grams)):
            pivot = jnp.broadcast_to(rows[n][tile][at : at + 1], (8, W))
            for i in range(tile + 1):
                if i * 8 < k:
                    factor = jnp.take_along_axis(
                        pairs[n][0][8 * i : 8 * i + 8], base[8 * i : 8 * i + 8] + k, axis=1, mode="promise_in_bounds"
                    )
                    rows[n][i] = rows[n][i] - factor * pivot
    row_scales = [jnp.take_along_axis(scale, base + row, axis=1, mode="promise_in_bounds") for _, scale in pairs]
    return [jnp.concatenate(r, axis=0) * s for r, s in zip(rows, row_scales)]


def dots3(lefts, rights):
    return [dot3(a, b) for a, b in zip(lefts, rights)]


def splits(values):
    return [split(v) for v in values]


def triangle_inverses(grams):
    small = diagonal_inverses(grams)
    lane = lax.broadcasted_iota(jnp.int32, (SUB, W), 1)
    group = lane // SUB
    half = 2 * SUB
    zero = jnp.zeros((SUB, W), F32)
    zeros = jnp.zeros((half, W), F32)
    parts = [[jnp.where(group == d, s, 0.0) for d in range(4)] for s in small]
    bases = splits([jnp.concatenate(p, axis=0) for p in parts])
    corners = splits(
        [
            jnp.concatenate(
                [jnp.where(group == 1, g[0:SUB], 0.0), jnp.where(group == 3, g[2 * SUB : 3 * SUB], 0.0)], axis=0
            )
            for g in grams
        ]
    )
    lane2 = lax.broadcasted_iota(jnp.int32, (half, W), 1)
    corners2 = splits([jnp.where(lane2 >= half, g[0:half], 0.0) for g in grams])
    products = dots3(corners, bases)
    fulls = splits([jnp.concatenate([p[0:SUB], zero, p[SUB:], zero], axis=0) for p in products])
    changes = dots3(splits([jnp.concatenate([p[0], p[2]], axis=0) for p in parts]), fulls)
    uppers = [jnp.concatenate([p[0] - c[0:SUB], p[1]], axis=0) for p, c in zip(parts, changes)]
    lowers = [jnp.concatenate([p[2] - c[SUB:], p[3]], axis=0) for p, c in zip(parts, changes)]
    products = dots3(corners2, splits([jnp.concatenate([zeros, low], axis=0) for low in lowers]))
    changes = dots3(splits(uppers), splits([jnp.concatenate([p, zeros], axis=0) for p in products]))
    return [jnp.concatenate([u - c, low], axis=0) for u, c, low in zip(uppers, changes, lowers)]


def factors(packed):
    reflectors = [unpacked(p) for p in packed]
    halves = splits(reflectors)
    nt = ((1,), (1,))
    grams = [mm(h, h, nt) + (mm(h, l, nt) + mm(l, h, nt)) for h, l in halves]
    inverses = splits(triangle_inverses(grams))
    products = splits(dots3(inverses, halves))
    return [(*a, *split(r.T)) for a, r in zip(products, reflectors)]


def whole(factor):
    ah, al, vh, vl = factor
    return jnp.concatenate(split(dot3((vh, vl), (ah, al))), axis=1)


def stored_wholes(packed, g_ref):
    for at, factor in enumerate(factors(packed)):
        g_ref[at] = whole(factor)


def slot_of(scalars, level, half):
    return scalars[3 + 2 * level + half]


def gathered(scalars, pieces, held, at):
    for k in range(4):
        held[(scalars[0] + 4 - k) % 4] = pieces[k][at]


def block_of(scalars, held, level, half):
    return held[2 * (level % 2) + slot_of(scalars, level, half)]


def twice(factor):
    ah, al, vh, vl = factor

    def update(x):
        return x - dot3((vh, vl), split(dot3((ah, al), split(x))))

    return update


def once(g_ref, at):
    g = g_ref[at]

    def update(x):
        xh, xl = split(x)
        wide = mm(g[:, : 2 * W], jnp.concatenate([xh, xl], axis=1))
        return x - (wide[:, :W] + (wide[:, W:] + mm(g[:, 2 * W :], xh)))

    return update


def across(top, low, update):
    middle = update(jnp.concatenate([top[W:], low[:W]], axis=0))
    return jnp.concatenate([top[:W], middle[:W]], axis=0), jnp.concatenate([middle[W:], low[W:]], axis=0)


def joined(g_ref, at):
    g = g_ref[at]
    return g[:W, :W].astype(F32) + g[:W, 2 * W : 3 * W].astype(F32)


def below_rows(message):
    return message[:W], message[W : 2 * W], message[2 * W :]


def across_below(last, low, near, update):
    middle = update(jnp.concatenate([low[W:], jnp.where(last, 0.0, near)], axis=0))
    return jnp.concatenate([low[:W], middle[:W]], axis=0), middle[W:]


def carried(settled, quarter, change):
    return settled + (change - dot3(split(quarter), split(change)))


def across_above(first, above, top, update):
    new_above, new_top = across(above, top, update)
    return new_above, jnp.where(first, top, new_top)


def keep_kernel(piece, kept):
    kept[...] = piece[...]


def order_kernel(plane, p0, p1, p2, p3, near, far, held):
    for k, piece in enumerate((p0, p1, p2, p3)):
        held[(plane[0] + 4 - k) % 4] = piece[...]
    near[...] = held[0:2]
    far[...] = held[2:4]


def first_kernel(scalars, x_ref, p0, p1, p2, p3, message, low_ref, rest, held):
    pieces = (p0, p1, p2, p3)
    gathered(scalars, pieces, held, 1)
    ahead = block_of(scalars, held, 2, 0)
    gathered(scalars, pieces, held, 0)
    found = factors([block_of(scalars, held, level, half) for level, half in ((0, 0), (0, 1), (1, 0))] + [ahead])
    ah, al, vh, vl = found[3]
    left = dot3((vh, vl), (ah[:, :W], al[:, :W]))
    top = twice(found[0])(x_ref[: 2 * W])
    low = twice(found[1])(x_ref[2 * W :])
    top, low = across(top, low, twice(found[2]))
    settled = twice(found[3])(top)
    message[:W] = top[:W]
    message[W : 2 * W] = settled[:W]
    message[2 * W :] = left[:W]
    rest[:W] = settled[W:]
    rest[W:] = left[W:]
    low_ref[...] = low


def factor1_kernel(scalars, after, p0, p1, p2, p3, far, g1, sent, held):
    sent[...] = far[...]
    pieces = (p0, p1, p2, p3)
    gathered(scalars, pieces, held, 0)
    early = block_of(scalars, held, 1, 1)
    gathered(scalars, pieces, held, 1)
    late = [block_of(scalars, held, level, half) for level, half in ((2, 1), (3, 0), (3, 1))]
    stored_wholes([*late, early], g1)


def second_kernel(scalars, low_ref, message, g1, low_out, back):
    last = scalars[1] == 1
    near, settled, quarter = below_rows(message)
    low, moved = across_below(last, low_ref[...], near, once(g1, 3))
    change = moved - near
    low = once(g1, 0)(low)
    low, moved = across_below(last, low, carried(settled, quarter, change), once(g1, 2))
    low_out[...] = low
    back[:W] = moved
    back[W:] = change


def choose_kernel(scalars, after, p0, p1, p2, p3, down, held):
    pieces = (p0, p1, p2, p3)
    gathered(scalars, pieces, held, 1)
    down[1] = block_of(scalars, held, 6, 1)
    down[2] = block_of(scalars, held, 7, 1)
    gathered(scalars, pieces, held, 0)
    down[0] = block_of(scalars, held, 5, 1)


def factor2_kernel(scalars, after, p0, p1, p2, p3, g2, held):
    gathered(scalars, (p0, p1, p2, p3), held, 0)
    stored_wholes([block_of(scalars, held, level, half) for level in (4, 5) for half in (0, 1)], g2)


def third_kernel(scalars, low_ref, own, rest, back, g1, g2, g3, low_out, top_out, message):
    upper = jnp.where(scalars[2] == 1, own[W : 2 * W], back[:W])
    lower = rest[:W] - dot3(split(rest[W:]), split(back[W:]))
    top, low = across(jnp.concatenate([upper, lower], axis=0), low_ref[...], once(g1, 1))
    top = once(g2, 0)(top)
    low = once(g2, 1)(low)
    top, low = across(top, low, once(g2, 2))
    low_out[...] = low
    top_out[...] = top
    message[:W] = top[:W]
    message[W : 2 * W] = once(g3, 0)(top)[:W]
    message[2 * W :] = joined(g3, 0)


def factor3_kernel(scalars, after, p0, p1, p2, p3, g3, held):
    gathered(scalars, (p0, p1, p2, p3), held, 1)
    stored_wholes([block_of(scalars, held, level, half) for level, half in ((6, 0), (6, 1), (7, 0), (7, 1))], g3)


def factor4_kernel(after, down, g4):
    stored_wholes([down[0], down[1], down[2]], g4)


def fourth_kernel(scalars, low_ref, top_ref, above_ref, message, g2, g3, g4, out_ref):
    last = scalars[1] == 1
    first = scalars[2] == 1
    near, settled, quarter = below_rows(message)
    low, moved = across_below(last, low_ref[...], near, once(g2, 3))
    above, top = across_above(first, above_ref[...], top_ref[...], once(g4, 0))
    above = once(g4, 1)(above)
    top = once(g3, 0)(top)
    low = once(g3, 1)(low)
    _, top = across_above(first, above, top, once(g4, 2))
    low, _ = across_below(last, low, carried(settled, quarter, moved - near), once(g3, 3))
    top, low = across(top, low, once(g3, 2))
    out_ref[: 2 * W] = top
    out_ref[2 * W :] = low


def wholes(count):
    return jax.ShapeDtypeStruct((count, 2 * W, 4 * W), BF16)


def rows_shape(*shape):
    return jax.ShapeDtypeStruct(shape, F32)


HELD = [pltpu.VMEM((4, W, W), F32)]


def call(kernel, args, shapes, scratch=(), smem=1, flops=400_000_000):
    return pl.pallas_call(
        kernel,
        out_shape=tuple(shapes),
        in_specs=[pl.BlockSpec(memory_space=SMEM)] * smem + [pl.BlockSpec(memory_space=VMEM)] * (len(args) - smem),
        out_specs=(pl.BlockSpec(memory_space=VMEM),) * len(shapes),
        scratch_shapes=list(scratch),
        compiler_params=pltpu.CompilerParams(vmem_limit_bytes=24 * 1024 * 1024),
        cost_estimate=pl.CostEstimate(flops=flops, bytes_accessed=2_000_000, transcendentals=0),
        name=kernel.__name__,
    )(*args)


def shifted(value, axis, steps):
    count = lax.axis_size(axis)
    return lax.ppermute(value, axis, [(i, (i + steps) % count) for i in range(count)])


def to_neighbour(value, steps):
    count = lax.axis_size("rows")
    return lax.ppermute(value, "rows", [(i, i + steps) for i in range(count) if 0 <= i + steps < count])


def along_x(value):
    found = {k: lax.ppermute(value, "cols", [(i, (i // 4) * 4 + (i + k) % 4) for i in range(16)]) for k in (1, 3, 2)}
    return [value, found[1], found[2], found[3]]


def per_device(eigvecs, wy_packed, slot_block):
    column = lax.axis_index("cols")
    row = lax.axis_index("rows")
    plane, place = column // 4, column % 4
    edges = jnp.stack([place, row == lax.axis_size("rows") - 1, row == 0]).astype(jnp.int32)
    scalars = jnp.concatenate([edges, slot_block.reshape(-1)])
    packed = wy_packed[0]
    half = rows_shape(2 * W, W)

    (held,) = call(keep_kernel, (packed,), [rows_shape(W, W)], smem=0)
    planes = [packed] + [shifted(packed, "cols", 4 * k) for k in (1, 2, 3)]
    pair = rows_shape(2, W, W)
    near, far = call(order_kernel, (plane.reshape(1), held, *planes[1:]), [pair, pair], HELD)
    near = along_x(near)
    three = rows_shape(3 * W, W)
    three = rows_shape(3 * W, W)
    own, low, rest = call(first_kernel, (scalars, eigvecs, *near), [three, half, half], HELD)
    message = to_neighbour(own, -1)
    g1, far = call(factor1_kernel, (scalars, low, *near, far), [wholes(4), pair], HELD)
    far = along_x(far)
    low, back = call(second_kernel, (scalars, low, message, g1), [half, half])
    back = to_neighbour(back, 1)
    (down,) = call(choose_kernel, (scalars, low, *far), [rows_shape(3, W, W)], HELD)
    (g2,) = call(factor2_kernel, (scalars, down, *far), [wholes(4)], HELD)
    (g3,) = call(factor3_kernel, (scalars, down, *far), [wholes(4)], HELD)
    down = to_neighbour(down, 1)
    low, top, message = call(third_kernel, (scalars, low, own, rest, back, g1, g2, g3), [half, half, three])
    above = to_neighbour(low, 1)
    message = to_neighbour(message, -1)
    (g4,) = call(factor4_kernel, (low, down), [wholes(3)], smem=0)
    return call(
        fourth_kernel, (scalars, low, top, above, message, g2, g3, g4), [rows_shape(*eigvecs.shape)]
    )[0]


def solution(mesh):
    placed = (P("rows", "cols"), P(("rows", "cols"), None, None), P("rows", None, None))
    return jax.shard_map(
        per_device, mesh=mesh, in_specs=placed, out_specs=P("rows", "cols"), check_vma=False
    )
```

```python
import jax
import jax.numpy as jnp
from jax import lax
from jax.experimental import pallas as pl
from jax.experimental.pallas import tpu as pltpu
from jax.sharding import PartitionSpec as P

F32 = jnp.float32
BF16 = jnp.bfloat16
W = 128
SUB = 32
VMEM = pltpu.VMEM
SMEM = pltpu.SMEM


def split(x):
    high = x.astype(BF16)
    low = (x - high.astype(F32)).astype(BF16)
    return high, low


def mm(a, b, dims=((1,), (0,))):
    return lax.dot_general(a, b, (dims, ((), ())), preferred_element_type=F32)


def dot3(a, b):
    ah, al = a
    bh, bl = b
    return mm(ah, bh) + (mm(ah, bl) + mm(al, bh))


def unpacked(packed):
    wide = jnp.concatenate([packed.T, jnp.zeros((W, W), F32)], axis=1)
    return pltpu.roll(wide, 0, axis=1, stride=1, stride_axis=0)


def diagonal_inverses(grams):
    row = lax.broadcasted_iota(jnp.int32, (SUB, W), 0)
    lane = lax.broadcasted_iota(jnp.int32, (SUB, W), 1)
    group = lane // SUB
    place = lane % SUB
    base = group * SUB

    def prepared(gram):
        compact = gram[0:SUB]
        for d in range(1, 4):
            compact = jnp.where(group == d, gram[d * SUB : (d + 1) * SUB], compact)
        diagonal = jnp.sum(jnp.where(row == place, compact, 0.0), axis=0, keepdims=True)
        scale = jnp.broadcast_to(2.0 / diagonal, (SUB, W))
        return jnp.where(row < place, compact * scale, 0.0), scale

    pairs = [prepared(gram) for gram in grams]
    start = [jnp.where(row == place, 1.0, 0.0)[8 * i : 8 * i + 8] for i in range(4)]
    rows = [list(start) for _ in grams]
    for k in range(SUB - 1, 0, -1):
        tile, at = k // 8, k % 8
        for n in range(len(grams)):
            pivot = jnp.broadcast_to(rows[n][tile][at : at + 1], (8, W))
            for i in range(tile + 1):
                if i * 8 < k:
                    factor = jnp.take_along_axis(
                        pairs[n][0][8 * i : 8 * i + 8], base[8 * i : 8 * i + 8] + k, axis=1, mode="promise_in_bounds"
                    )
                    rows[n][i] = rows[n][i] - factor * pivot
    row_scales = [jnp.take_along_axis(scale, base + row, axis=1, mode="promise_in_bounds") for _, scale in pairs]
    return [jnp.concatenate(r, axis=0) * s for r, s in zip(rows, row_scales)]


def dots3(lefts, rights):
    return [dot3(a, b) for a, b in zip(lefts, rights)]


def splits(values):
    return [split(v) for v in values]


def triangle_inverses(grams):
    small = diagonal_inverses(grams)
    lane = lax.broadcasted_iota(jnp.int32, (SUB, W), 1)
    group = lane // SUB
    half = 2 * SUB
    zero = jnp.zeros((SUB, W), F32)
    zeros = jnp.zeros((half, W), F32)
    parts = [[jnp.where(group == d, s, 0.0) for d in range(4)] for s in small]
    bases = splits([jnp.concatenate(p, axis=0) for p in parts])
    corners = splits(
        [
            jnp.concatenate(
                [jnp.where(group == 1, g[0:SUB], 0.0), jnp.where(group == 3, g[2 * SUB : 3 * SUB], 0.0)], axis=0
            )
            for g in grams
        ]
    )
    lane2 = lax.broadcasted_iota(jnp.int32, (half, W), 1)
    corners2 = splits([jnp.where(lane2 >= half, g[0:half], 0.0) for g in grams])
    products = dots3(corners, bases)
    fulls = splits([jnp.concatenate([p[0:SUB], zero, p[SUB:], zero], axis=0) for p in products])
    changes = dots3(splits([jnp.concatenate([p[0], p[2]], axis=0) for p in parts]), fulls)
    uppers = [jnp.concatenate([p[0] - c[0:SUB], p[1]], axis=0) for p, c in zip(parts, changes)]
    lowers = [jnp.concatenate([p[2] - c[SUB:], p[3]], axis=0) for p, c in zip(parts, changes)]
    products = dots3(corners2, splits([jnp.concatenate([zeros, low], axis=0) for low in lowers]))
    changes = dots3(splits(uppers), splits([jnp.concatenate([p, zeros], axis=0) for p in products]))
    return [jnp.concatenate([u - c, low], axis=0) for u, c, low in zip(uppers, changes, lowers)]


def factors(packed):
    reflectors = [unpacked(p) for p in packed]
    halves = splits(reflectors)
    nt = ((1,), (1,))
    grams = [mm(h, h, nt) + (mm(h, l, nt) + mm(l, h, nt)) for h, l in halves]
    inverses = splits(triangle_inverses(grams))
    products = splits(dots3(inverses, halves))
    return [(*a, *split(r.T)) for a, r in zip(products, reflectors)]


def whole(factor):
    ah, al, vh, vl = factor
    return jnp.concatenate(split(dot3((vh, vl), (ah, al))), axis=1)


def stored_wholes(packed, g_ref):
    for at, factor in enumerate(factors(packed)):
        g_ref[at] = whole(factor)


def slot_of(scalars, level, half):
    return scalars[4 + 2 * level + half]


def gathered(scalars, pieces, held, at):
    for k in range(4):
        held[(scalars[0] + 4 - k) % 4] = pieces[k][at]


def block_of(scalars, held, level, half):
    return held[2 * (level % 2) + slot_of(scalars, level, half)]


def twice(factor):
    ah, al, vh, vl = factor

    def update(x):
        return x - dot3((vh, vl), split(dot3((ah, al), split(x))))

    return update


def once(g_ref, at):
    g = g_ref[at]

    def update(x):
        xh, xl = split(x)
        wide = mm(g[:, : 2 * W], jnp.concatenate([xh, xl], axis=1))
        return x - (wide[:, :W] + (wide[:, W:] + mm(g[:, 2 * W :], xh)))

    return update


def across(top, low, update):
    middle = update(jnp.concatenate([top[W:], low[:W]], axis=0))
    return jnp.concatenate([top[:W], middle[:W]], axis=0), jnp.concatenate([middle[W:], low[W:]], axis=0)


def joined(g_ref, at):
    g = g_ref[at]
    return g[:W, :W].astype(F32) + g[:W, 2 * W : 3 * W].astype(F32)


def below_rows(message):
    return message[:W], message[W : 2 * W], message[2 * W :]


def across_below(last, low, near, update):
    middle = update(jnp.concatenate([low[W:], jnp.where(last, 0.0, near)], axis=0))
    return jnp.concatenate([low[:W], middle[:W]], axis=0), middle[W:]


def carried(settled, quarter, change):
    return settled + (change - dot3(split(quarter), split(change)))


def across_above(first, above, top, update):
    new_above, new_top = across(above, top, update)
    return new_above, jnp.where(first, top, new_top)


def keep_kernel(piece, kept):
    kept[...] = piece[...]


def order_kernel(plane, p0, p1, p2, p3, near, far, held):
    for k, piece in enumerate((p0, p1, p2, p3)):
        held[(plane[0] + 4 - k) % 4] = piece[...]
    near[...] = held[0:2]
    far[...] = held[2:4]


def first_kernel(scalars, x_ref, p0, p1, p2, p3, message, low_ref, rest, held):
    pieces = (p0, p1, p2, p3)
    gathered(scalars, pieces, held, 1)
    ahead = block_of(scalars, held, 2, 0)
    gathered(scalars, pieces, held, 0)
    found = factors([block_of(scalars, held, level, half) for level, half in ((0, 0), (0, 1), (1, 0))] + [ahead])
    ah, al, vh, vl = found[3]
    left = dot3((vh, vl), (ah[:, :W], al[:, :W]))
    top = twice(found[0])(x_ref[: 2 * W])
    low = twice(found[1])(x_ref[2 * W :])
    top, low = across(top, low, twice(found[2]))
    settled = twice(found[3])(top)
    message[:W] = top[:W]
    message[W : 2 * W] = settled[:W]
    message[2 * W :] = left[:W]
    rest[:W] = settled[W:]
    rest[W:] = left[W:]
    low_ref[...] = low


def factor1_kernel(scalars, after, p0, p1, p2, p3, g1, held):
    pieces = (p0, p1, p2, p3)
    gathered(scalars, pieces, held, 0)
    early = block_of(scalars, held, 1, 1)
    gathered(scalars, pieces, held, 1)
    late = [block_of(scalars, held, level, half) for level, half in ((2, 1), (3, 0), (3, 1))]
    stored_wholes([*late, early], g1)


def second_kernel(scalars, low_ref, message, g1, low_out, back):
    last = scalars[1] == 1
    near, settled, quarter = below_rows(message)
    low, moved = across_below(last, low_ref[...], near, once(g1, 3))
    change = moved - near
    low = once(g1, 0)(low)
    low, moved = across_below(last, low, carried(settled, quarter, change), once(g1, 2))
    low_out[...] = low
    back[:W] = moved
    back[W:] = change


def choose_kernel(scalars, after, p0, p1, p2, p3, down, held):
    pieces = (p0, p1, p2, p3)
    gathered(scalars, pieces, held, 1)
    down[1] = block_of(scalars, held, 6, 1)
    down[2] = block_of(scalars, held, 7, 1)
    gathered(scalars, pieces, held, 0)
    down[0] = block_of(scalars, held, 5, 1)


def factor2_kernel(scalars, after, p0, p1, p2, p3, g2, held):
    pieces = (p0, p1, p2, p3)
    gathered(scalars, pieces, held, 1)
    later = block_of(scalars, held, 6, 0)
    gathered(scalars, pieces, held, 0)
    stored_wholes([block_of(scalars, held, level, half) for level in (4, 5) for half in (0, 1)] + [later], g2)


def third_kernel(scalars, low_ref, own, rest, back, g1, g2, low_out, top_out, far_out, near_out):
    upper = jnp.where(scalars[2] == 1, own[W : 2 * W], back[:W])
    lower = rest[:W] - dot3(split(rest[W:]), split(back[W:]))
    top, low = across(jnp.concatenate([upper, lower], axis=0), low_ref[...], once(g1, 1))
    top = once(g2, 0)(top)
    low = once(g2, 1)(low)
    top, low = across(top, low, once(g2, 2))
    low_out[...] = low
    top_out[...] = top
    settled = once(g2, 4)(top)
    odd = scalars[3] == 1
    for at, (up, down) in enumerate(((top[:W], low[:W]), (settled[:W], low[W:]), (joined(g2, 4), top[W:]))):
        far_out[at * W : (at + 1) * W] = jnp.where(odd, down, up)
        near_out[at * W : (at + 1) * W] = jnp.where(odd, up, down)


def factor3_kernel(scalars, after, p0, p1, p2, p3, g3, held):
    gathered(scalars, (p0, p1, p2, p3), held, 1)
    stored_wholes([block_of(scalars, held, level, half) for level, half in ((6, 1), (7, 0), (7, 1))], g3)


def factor4_kernel(after, down, g4):
    stored_wholes([down[0], down[1], down[2]], g4)


def fourth_kernel(scalars, low_ref, top_ref, far, near, g2, g3, g4, out_ref):
    last = scalars[1] == 1
    first = scalars[2] == 1
    odd = scalars[3] == 1
    above = jnp.where(odd, near[: 2 * W], far[: 2 * W])
    near, settled, quarter = below_rows(jnp.where(odd, far[...], near[...]))
    low, moved = across_below(last, low_ref[...], near, once(g2, 3))
    above, top = across_above(first, above, top_ref[...], once(g4, 0))
    above = once(g4, 1)(above)
    top = once(g2, 4)(top)
    low = once(g3, 0)(low)
    _, top = across_above(first, above, top, once(g4, 2))
    low, _ = across_below(last, low, carried(settled, quarter, moved - near), once(g3, 2))
    top, low = across(top, low, once(g3, 1))
    out_ref[: 2 * W] = top
    out_ref[2 * W :] = low


def wholes(count):
    return jax.ShapeDtypeStruct((count, 2 * W, 4 * W), BF16)


def rows_shape(*shape):
    return jax.ShapeDtypeStruct(shape, F32)


HELD = [pltpu.VMEM((4, W, W), F32)]


def call(kernel, args, shapes, scratch=(), smem=1, flops=400_000_000):
    return pl.pallas_call(
        kernel,
        out_shape=tuple(shapes),
        in_specs=[pl.BlockSpec(memory_space=SMEM)] * smem + [pl.BlockSpec(memory_space=VMEM)] * (len(args) - smem),
        out_specs=(pl.BlockSpec(memory_space=VMEM),) * len(shapes),
        scratch_shapes=list(scratch),
        compiler_params=pltpu.CompilerParams(vmem_limit_bytes=24 * 1024 * 1024),
        cost_estimate=pl.CostEstimate(flops=flops, bytes_accessed=2_000_000, transcendentals=0),
        name=kernel.__name__,
    )(*args)


def shifted(value, axis, steps):
    count = lax.axis_size(axis)
    return lax.ppermute(value, axis, [(i, (i + steps) % count) for i in range(count)])


def to_neighbour(value, steps):
    count = lax.axis_size("rows")
    return lax.ppermute(value, "rows", [(i, i + steps) for i in range(count) if 0 <= i + steps < count])


def swapped(value, start):
    count = lax.axis_size("rows")
    pairs = [(i, i + 1) for i in range(start, count - 1, 2)]
    return lax.ppermute(value, "rows", pairs + [(j, i) for i, j in pairs])


def along_x(value):
    found = {k: lax.ppermute(value, "cols", [(i, (i // 4) * 4 + (i + k) % 4) for i in range(16)]) for k in (1, 3, 2)}
    return [value, found[1], found[2], found[3]]


def per_device(eigvecs, wy_packed, slot_block):
    column = lax.axis_index("cols")
    row = lax.axis_index("rows")
    plane, place = column // 4, column % 4
    edges = jnp.stack([place, row == lax.axis_size("rows") - 1, row == 0, row % 2]).astype(jnp.int32)
    scalars = jnp.concatenate([edges, slot_block.reshape(-1)])
    packed = wy_packed[0]
    half = rows_shape(2 * W, W)

    (held,) = call(keep_kernel, (packed,), [rows_shape(W, W)], smem=0)
    planes = [packed] + [shifted(packed, "cols", 4 * k) for k in (1, 2, 3)]
    pair = rows_shape(2, W, W)
    near, far = call(order_kernel, (plane.reshape(1), held, *planes[1:]), [pair, pair], HELD)
    near = along_x(near)
    far = along_x(far)
    three = rows_shape(3 * W, W)
    three = rows_shape(3 * W, W)
    own, low, rest = call(first_kernel, (scalars, eigvecs, *near), [three, half, half], HELD)
    message = to_neighbour(own, -1)
    (g1,) = call(factor1_kernel, (scalars, low, *near), [wholes(4)], HELD)
    low, back = call(second_kernel, (scalars, low, message, g1), [half, half])
    back = to_neighbour(back, 1)
    (down,) = call(choose_kernel, (scalars, low, *far), [rows_shape(3, W, W)], HELD)
    (g2,) = call(factor2_kernel, (scalars, down, *far), [wholes(5)], HELD)
    down = to_neighbour(down, 1)
    low, top, far_out, near_out = call(
        third_kernel, (scalars, low, own, rest, back, g1, g2), [half, half, three, three]
    )
    from_far = swapped(far_out, 1)
    from_near = swapped(near_out, 0)
    (g3,) = call(factor3_kernel, (scalars, low, *far), [wholes(3)], HELD)
    (g4,) = call(factor4_kernel, (low, down), [wholes(3)], smem=0)
    return call(
        fourth_kernel, (scalars, low, top, from_far, from_near, g2, g3, g4), [rows_shape(*eigvecs.shape)]
    )[0]


def solution(mesh):
    placed = (P("rows", "cols"), P(("rows", "cols"), None, None), P("rows", None, None))
    return jax.shard_map(
        per_device, mesh=mesh, in_specs=placed, out_specs=P("rows", "cols"), check_vma=False
    )
```

```python
import jax
import jax.numpy as jnp
from jax import lax
from jax.experimental import pallas as pl
from jax.experimental.pallas import tpu as pltpu
from jax.sharding import PartitionSpec as P

F32 = jnp.float32
BF16 = jnp.bfloat16
W = 128
SUB = 32
VMEM = pltpu.VMEM
SMEM = pltpu.SMEM


def split(x):
    high = x.astype(BF16)
    low = (x - high.astype(F32)).astype(BF16)
    return high, low


def mm(a, b, dims=((1,), (0,))):
    return lax.dot_general(a, b, (dims, ((), ())), preferred_element_type=F32)


def dot3(a, b):
    ah, al = a
    bh, bl = b
    return mm(ah, bh) + (mm(ah, bl) + mm(al, bh))


def unpacked(packed):
    wide = jnp.concatenate([packed.T, jnp.zeros((W, W), F32)], axis=1)
    return pltpu.roll(wide, 0, axis=1, stride=1, stride_axis=0)


def diagonal_inverses(grams):
    row = lax.broadcasted_iota(jnp.int32, (SUB, W), 0)
    lane = lax.broadcasted_iota(jnp.int32, (SUB, W), 1)
    group = lane // SUB
    place = lane % SUB
    base = group * SUB

    def prepared(gram):
        compact = gram[0:SUB]
        for d in range(1, 4):
            compact = jnp.where(group == d, gram[d * SUB : (d + 1) * SUB], compact)
        diagonal = jnp.sum(jnp.where(row == place, compact, 0.0), axis=0, keepdims=True)
        scale = jnp.broadcast_to(2.0 / diagonal, (SUB, W))
        return jnp.where(row < place, compact * scale, 0.0), scale

    pairs = [prepared(gram) for gram in grams]
    start = [jnp.where(row == place, 1.0, 0.0)[8 * i : 8 * i + 8] for i in range(4)]
    rows = [list(start) for _ in grams]
    for k in range(SUB - 1, 0, -1):
        tile, at = k // 8, k % 8
        for n in range(len(grams)):
            pivot = jnp.broadcast_to(rows[n][tile][at : at + 1], (8, W))
            for i in range(tile + 1):
                if i * 8 < k:
                    factor = jnp.take_along_axis(
                        pairs[n][0][8 * i : 8 * i + 8], base[8 * i : 8 * i + 8] + k, axis=1, mode="promise_in_bounds"
                    )
                    rows[n][i] = rows[n][i] - factor * pivot
    row_scales = [jnp.take_along_axis(scale, base + row, axis=1, mode="promise_in_bounds") for _, scale in pairs]
    return [jnp.concatenate(r, axis=0) * s for r, s in zip(rows, row_scales)]


def dots3(lefts, rights):
    return [dot3(a, b) for a, b in zip(lefts, rights)]


def splits(values):
    return [split(v) for v in values]


def triangle_inverses(grams):
    small = diagonal_inverses(grams)
    lane = lax.broadcasted_iota(jnp.int32, (SUB, W), 1)
    group = lane // SUB
    half = 2 * SUB
    zero = jnp.zeros((SUB, W), F32)
    zeros = jnp.zeros((half, W), F32)
    parts = [[jnp.where(group == d, s, 0.0) for d in range(4)] for s in small]
    bases = splits([jnp.concatenate(p, axis=0) for p in parts])
    corners = splits(
        [
            jnp.concatenate(
                [jnp.where(group == 1, g[0:SUB], 0.0), jnp.where(group == 3, g[2 * SUB : 3 * SUB], 0.0)], axis=0
            )
            for g in grams
        ]
    )
    lane2 = lax.broadcasted_iota(jnp.int32, (half, W), 1)
    corners2 = splits([jnp.where(lane2 >= half, g[0:half], 0.0) for g in grams])
    products = dots3(corners, bases)
    fulls = splits([jnp.concatenate([p[0:SUB], zero, p[SUB:], zero], axis=0) for p in products])
    changes = dots3(splits([jnp.concatenate([p[0], p[2]], axis=0) for p in parts]), fulls)
    uppers = [jnp.concatenate([p[0] - c[0:SUB], p[1]], axis=0) for p, c in zip(parts, changes)]
    lowers = [jnp.concatenate([p[2] - c[SUB:], p[3]], axis=0) for p, c in zip(parts, changes)]
    products = dots3(corners2, splits([jnp.concatenate([zeros, low], axis=0) for low in lowers]))
    changes = dots3(splits(uppers), splits([jnp.concatenate([p, zeros], axis=0) for p in products]))
    return [jnp.concatenate([u - c, low], axis=0) for u, c, low in zip(uppers, changes, lowers)]


def factors(packed):
    reflectors = [unpacked(p) for p in packed]
    halves = splits(reflectors)
    nt = ((1,), (1,))
    grams = [mm(h, h, nt) + (mm(h, l, nt) + mm(l, h, nt)) for h, l in halves]
    inverses = splits(triangle_inverses(grams))
    products = splits(dots3(inverses, halves))
    return [(*a, *split(r.T)) for a, r in zip(products, reflectors)]


def whole(factor):
    ah, al, vh, vl = factor
    return jnp.concatenate(split(dot3((vh, vl), (ah, al))), axis=1)


def stored_wholes(packed, g_ref):
    for at, factor in enumerate(factors(packed)):
        g_ref[at] = whole(factor)


def slot_of(scalars, level, half):
    return scalars[4 + 2 * level + half]


def gathered(scalars, pieces, held, at):
    for k in range(4):
        held[(scalars[0] + 4 - k) % 4] = pieces[k][at]


def block_of(scalars, held, level, half):
    return held[2 * (level % 2) + slot_of(scalars, level, half)]


def twice(factor):
    ah, al, vh, vl = factor

    def update(x):
        return x - dot3((vh, vl), split(dot3((ah, al), split(x))))

    return update


def once(g_ref, at):
    g = g_ref[at]

    def update(x):
        xh, xl = split(x)
        wide = mm(g[:, : 2 * W], jnp.concatenate([xh, xl], axis=1))
        return x - (wide[:, :W] + (wide[:, W:] + mm(g[:, 2 * W :], xh)))

    return update


def across(top, low, update):
    middle = update(jnp.concatenate([top[W:], low[:W]], axis=0))
    return jnp.concatenate([top[:W], middle[:W]], axis=0), jnp.concatenate([middle[W:], low[W:]], axis=0)


def joined(g_ref, at):
    g = g_ref[at]
    return g[:W, :W].astype(F32) + g[:W, 2 * W : 3 * W].astype(F32)


def below_rows(message):
    return message[:W], message[W : 2 * W], message[2 * W :]


def across_below(last, low, near, update):
    middle = update(jnp.concatenate([low[W:], jnp.where(last, 0.0, near)], axis=0))
    return jnp.concatenate([low[:W], middle[:W]], axis=0), middle[W:]


def carried(settled, quarter, change):
    return settled + (change - dot3(split(quarter), split(change)))


def across_above(first, above, top, update):
    new_above, new_top = across(above, top, update)
    return new_above, jnp.where(first, top, new_top)


def keep_kernel(piece, kept):
    kept[...] = piece[...]


def order_kernel(plane, p0, p1, p2, p3, near, far, held):
    for k, piece in enumerate((p0, p1, p2, p3)):
        held[(plane[0] + 4 - k) % 4] = piece[...]
    near[...] = held[0:2]
    far[...] = held[2:4]


def first_kernel(scalars, x_ref, p0, p1, p2, p3, message, low_ref, rest, held):
    pieces = (p0, p1, p2, p3)
    gathered(scalars, pieces, held, 1)
    ahead = block_of(scalars, held, 2, 0)
    gathered(scalars, pieces, held, 0)
    found = factors([block_of(scalars, held, level, half) for level, half in ((0, 0), (0, 1), (1, 0))] + [ahead])
    ah, al, vh, vl = found[3]
    left = dot3((vh, vl), (ah[:, :W], al[:, :W]))
    top = twice(found[0])(x_ref[: 2 * W])
    low = twice(found[1])(x_ref[2 * W :])
    top, low = across(top, low, twice(found[2]))
    settled = twice(found[3])(top)
    message[:W] = top[:W]
    message[W : 2 * W] = settled[:W]
    message[2 * W :] = left[:W]
    rest[:W] = settled[W:]
    rest[W:] = left[W:]
    low_ref[...] = low


def factor1_kernel(scalars, after, p0, p1, p2, p3, g1, held):
    pieces = (p0, p1, p2, p3)
    gathered(scalars, pieces, held, 0)
    early = block_of(scalars, held, 1, 1)
    gathered(scalars, pieces, held, 1)
    late = [block_of(scalars, held, level, half) for level, half in ((2, 1), (3, 0), (3, 1))]
    stored_wholes([*late, early], g1)


def second_kernel(scalars, low_ref, message, g1, low_out, back):
    last = scalars[1] == 1
    near, settled, quarter = below_rows(message)
    low, moved = across_below(last, low_ref[...], near, once(g1, 3))
    change = moved - near
    low = once(g1, 0)(low)
    low, moved = across_below(last, low, carried(settled, quarter, change), once(g1, 2))
    low_out[...] = low
    back[:W] = moved
    back[W:] = change


def choose_kernel(scalars, after, p0, p1, p2, p3, down, held):
    pieces = (p0, p1, p2, p3)
    gathered(scalars, pieces, held, 1)
    down[1] = block_of(scalars, held, 6, 1)
    down[2] = block_of(scalars, held, 7, 1)
    gathered(scalars, pieces, held, 0)
    down[0] = block_of(scalars, held, 5, 1)


def factor2_kernel(scalars, after, p0, p1, p2, p3, g2, held):
    pieces = (p0, p1, p2, p3)
    gathered(scalars, pieces, held, 1)
    later = block_of(scalars, held, 6, 0)
    gathered(scalars, pieces, held, 0)
    stored_wholes([block_of(scalars, held, level, half) for level in (4, 5) for half in (0, 1)] + [later], g2)


def third_kernel(scalars, low_ref, own, rest, back, g1, g2, low_out, top_out, far_out, near_out):
    upper = jnp.where(scalars[2] == 1, own[W : 2 * W], back[:W])
    lower = rest[:W] - dot3(split(rest[W:]), split(back[W:]))
    top, low = across(jnp.concatenate([upper, lower], axis=0), low_ref[...], once(g1, 1))
    top = once(g2, 0)(top)
    low = once(g2, 1)(low)
    top, low = across(top, low, once(g2, 2))
    low_out[...] = low
    top_out[...] = top
    settled = once(g2, 4)(top)
    odd = scalars[3] == 1
    for at, (up, down) in enumerate(((top[:W], low[:W]), (settled[:W], low[W:]), (joined(g2, 4), top[W:]))):
        far_out[at * W : (at + 1) * W] = jnp.where(odd, down, up)
        near_out[at * W : (at + 1) * W] = jnp.where(odd, up, down)


def factor3_kernel(scalars, after, p0, p1, p2, p3, g3, held):
    gathered(scalars, (p0, p1, p2, p3), held, 1)
    stored_wholes([block_of(scalars, held, level, half) for level, half in ((6, 1), (7, 0), (7, 1))], g3)


def factor4_kernel(after, down, g4):
    stored_wholes([down[0], down[1], down[2]], g4)


def fourth_kernel(scalars, low_ref, top_ref, far, near, g2, g3, g4, out_ref):
    last = scalars[1] == 1
    first = scalars[2] == 1
    odd = scalars[3] == 1
    above = jnp.where(odd, near[: 2 * W], far[: 2 * W])
    near, settled, quarter = below_rows(jnp.where(odd, far[...], near[...]))
    low, moved = across_below(last, low_ref[...], near, once(g2, 3))
    above, top = across_above(first, above, top_ref[...], once(g4, 0))
    above = once(g4, 1)(above)
    top = once(g2, 4)(top)
    low = once(g3, 0)(low)
    _, top = across_above(first, above, top, once(g4, 2))
    low, _ = across_below(last, low, carried(settled, quarter, moved - near), once(g3, 2))
    top, low = across(top, low, once(g3, 1))
    out_ref[: 2 * W] = top
    out_ref[2 * W :] = low


def wholes(count):
    return jax.ShapeDtypeStruct((count, 2 * W, 4 * W), BF16)


def rows_shape(*shape):
    return jax.ShapeDtypeStruct(shape, F32)


HELD = [pltpu.VMEM((4, W, W), F32)]


def call(kernel, args, shapes, scratch=(), smem=1, flops=400_000_000):
    return pl.pallas_call(
        kernel,
        out_shape=tuple(shapes),
        in_specs=[pl.BlockSpec(memory_space=SMEM)] * smem + [pl.BlockSpec(memory_space=VMEM)] * (len(args) - smem),
        out_specs=(pl.BlockSpec(memory_space=VMEM),) * len(shapes),
        scratch_shapes=list(scratch),
        compiler_params=pltpu.CompilerParams(vmem_limit_bytes=24 * 1024 * 1024),
        cost_estimate=pl.CostEstimate(flops=flops, bytes_accessed=2_000_000, transcendentals=0),
        name=kernel.__name__,
    )(*args)


def shifted(value, axis, steps):
    count = lax.axis_size(axis)
    return lax.ppermute(value, axis, [(i, (i + steps) % count) for i in range(count)])


def to_neighbour(value, steps):
    count = lax.axis_size("rows")
    return lax.ppermute(value, "rows", [(i, i + steps) for i in range(count) if 0 <= i + steps < count])


def swapped(value, start):
    count = lax.axis_size("rows")
    pairs = [(i, i + 1) for i in range(start, count - 1, 2)]
    return lax.ppermute(value, "rows", pairs + [(j, i) for i, j in pairs])


def along_x(value):
    found = {k: lax.ppermute(value, "cols", [(i, (i // 4) * 4 + (i + k) % 4) for i in range(16)]) for k in (1, 3, 2)}
    return [value, found[1], found[2], found[3]]


def per_device(eigvecs, wy_packed, slot_block):
    column = lax.axis_index("cols")
    row = lax.axis_index("rows")
    plane, place = column // 4, column % 4
    edges = jnp.stack([place, row == lax.axis_size("rows") - 1, row == 0, row % 2]).astype(jnp.int32)
    scalars = jnp.concatenate([edges, slot_block.reshape(-1)])
    packed = wy_packed[0]
    half = rows_shape(2 * W, W)

    (held,) = call(keep_kernel, (packed,), [rows_shape(W, W)], smem=0)
    planes = [packed] + [shifted(packed, "cols", 4 * k) for k in (1, 2, 3)]
    pair = rows_shape(2, W, W)
    near, far = call(order_kernel, (plane.reshape(1), held, *planes[1:]), [pair, pair], HELD)
    near = along_x(near)
    far = along_x(far)
    three = rows_shape(3 * W, W)
    three = rows_shape(3 * W, W)
    own, low, rest = call(first_kernel, (scalars, eigvecs, *near), [three, half, half], HELD)
    message = to_neighbour(own, -1)
    (down,) = call(choose_kernel, (scalars, low, *far), [rows_shape(3, W, W)], HELD)
    (g1,) = call(factor1_kernel, (scalars, down, *near), [wholes(4)], HELD)
    low, back = call(second_kernel, (scalars, low, message, g1), [half, half])
    back = to_neighbour(back, 1)
    (g2,) = call(factor2_kernel, (scalars, low, *far), [wholes(5)], HELD)
    down = to_neighbour(down, 1)
    low, top, far_out, near_out = call(
        third_kernel, (scalars, low, own, rest, back, g1, g2), [half, half, three, three]
    )
    from_far = swapped(far_out, 1)
    from_near = swapped(near_out, 0)
    (g3,) = call(factor3_kernel, (scalars, low, *far), [wholes(3)], HELD)
    (g4,) = call(factor4_kernel, (low, down), [wholes(3)], smem=0)
    return call(
        fourth_kernel, (scalars, low, top, from_far, from_near, g2, g3, g4), [rows_shape(*eigvecs.shape)]
    )[0]


def solution(mesh):
    placed = (P("rows", "cols"), P(("rows", "cols"), None, None), P("rows", None, None))
    return jax.shard_map(
        per_device, mesh=mesh, in_specs=placed, out_specs=P("rows", "cols"), check_vma=False
    )
```

```python
import jax
import jax.numpy as jnp
from jax import lax
from jax.experimental import pallas as pl
from jax.experimental.pallas import tpu as pltpu
from jax.sharding import PartitionSpec as P

F32 = jnp.float32
BF16 = jnp.bfloat16
W = 128
SUB = 32
VMEM = pltpu.VMEM
SMEM = pltpu.SMEM


def split(x):
    high = x.astype(BF16)
    low = (x - high.astype(F32)).astype(BF16)
    return high, low


def mm(a, b, dims=((1,), (0,))):
    return lax.dot_general(a, b, (dims, ((), ())), preferred_element_type=F32)


def dot3(a, b):
    ah, al = a
    bh, bl = b
    return mm(ah, bh) + (mm(ah, bl) + mm(al, bh))


def unpacked(packed):
    wide = jnp.concatenate([packed.T, jnp.zeros((W, W), F32)], axis=1)
    return pltpu.roll(wide, 0, axis=1, stride=1, stride_axis=0)


def diagonal_inverses(grams):
    row = lax.broadcasted_iota(jnp.int32, (SUB, W), 0)
    lane = lax.broadcasted_iota(jnp.int32, (SUB, W), 1)
    group = lane // SUB
    place = lane % SUB
    base = group * SUB

    def prepared(gram):
        compact = gram[0:SUB]
        for d in range(1, 4):
            compact = jnp.where(group == d, gram[d * SUB : (d + 1) * SUB], compact)
        diagonal = jnp.sum(jnp.where(row == place, compact, 0.0), axis=0, keepdims=True)
        scale = jnp.broadcast_to(2.0 / diagonal, (SUB, W))
        return jnp.where(row < place, compact * scale, 0.0), scale

    pairs = [prepared(gram) for gram in grams]
    start = [jnp.where(row == place, 1.0, 0.0)[8 * i : 8 * i + 8] for i in range(4)]
    rows = [list(start) for _ in grams]
    for k in range(SUB - 1, 0, -1):
        tile, at = k // 8, k % 8
        for n in range(len(grams)):
            pivot = jnp.broadcast_to(rows[n][tile][at : at + 1], (8, W))
            for i in range(tile + 1):
                if i * 8 < k:
                    factor = jnp.take_along_axis(
                        pairs[n][0][8 * i : 8 * i + 8], base[8 * i : 8 * i + 8] + k, axis=1, mode="promise_in_bounds"
                    )
                    rows[n][i] = rows[n][i] - factor * pivot
    row_scales = [jnp.take_along_axis(scale, base + row, axis=1, mode="promise_in_bounds") for _, scale in pairs]
    return [jnp.concatenate(r, axis=0) * s for r, s in zip(rows, row_scales)]


def dots3(lefts, rights):
    return [dot3(a, b) for a, b in zip(lefts, rights)]


def splits(values):
    return [split(v) for v in values]


def triangle_inverses(grams):
    small = diagonal_inverses(grams)
    lane = lax.broadcasted_iota(jnp.int32, (SUB, W), 1)
    group = lane // SUB
    half = 2 * SUB
    zero = jnp.zeros((SUB, W), F32)
    zeros = jnp.zeros((half, W), F32)
    parts = [[jnp.where(group == d, s, 0.0) for d in range(4)] for s in small]
    bases = splits([jnp.concatenate(p, axis=0) for p in parts])
    corners = splits(
        [
            jnp.concatenate(
                [jnp.where(group == 1, g[0:SUB], 0.0), jnp.where(group == 3, g[2 * SUB : 3 * SUB], 0.0)], axis=0
            )
            for g in grams
        ]
    )
    lane2 = lax.broadcasted_iota(jnp.int32, (half, W), 1)
    corners2 = splits([jnp.where(lane2 >= half, g[0:half], 0.0) for g in grams])
    products = dots3(corners, bases)
    fulls = splits([jnp.concatenate([p[0:SUB], zero, p[SUB:], zero], axis=0) for p in products])
    changes = dots3(splits([jnp.concatenate([p[0], p[2]], axis=0) for p in parts]), fulls)
    uppers = [jnp.concatenate([p[0] - c[0:SUB], p[1]], axis=0) for p, c in zip(parts, changes)]
    lowers = [jnp.concatenate([p[2] - c[SUB:], p[3]], axis=0) for p, c in zip(parts, changes)]
    products = dots3(corners2, splits([jnp.concatenate([zeros, low], axis=0) for low in lowers]))
    changes = dots3(splits(uppers), splits([jnp.concatenate([p, zeros], axis=0) for p in products]))
    return [jnp.concatenate([u - c, low], axis=0) for u, c, low in zip(uppers, changes, lowers)]


def factors(packed):
    reflectors = [unpacked(p) for p in packed]
    halves = splits(reflectors)
    nt = ((1,), (1,))
    grams = [mm(h, h, nt) + (mm(h, l, nt) + mm(l, h, nt)) for h, l in halves]
    inverses = splits(triangle_inverses(grams))
    products = splits(dots3(inverses, halves))
    return [(*a, *split(r.T)) for a, r in zip(products, reflectors)]


def whole(factor):
    ah, al, vh, vl = factor
    return jnp.concatenate(split(dot3((vh, vl), (ah, al))), axis=1)


def stored_wholes(packed, g_ref):
    for at, factor in enumerate(factors(packed)):
        g_ref[at] = whole(factor)


def slot_of(scalars, level, half):
    return scalars[4 + 2 * level + half]


def gathered(scalars, pieces, held, at):
    for k in range(4):
        held[(scalars[0] + 4 - k) % 4] = pieces[k][at]


def block_of(scalars, held, level, half):
    return held[2 * (level % 2) + slot_of(scalars, level, half)]


def twice(factor):
    ah, al, vh, vl = factor

    def update(x):
        return x - dot3((vh, vl), split(dot3((ah, al), split(x))))

    return update


def once(g_ref, at):
    g = g_ref[at]

    def update(x):
        xh, xl = split(x)
        wide = mm(g[:, : 2 * W], jnp.concatenate([xh, xl], axis=1))
        return x - (wide[:, :W] + (wide[:, W:] + mm(g[:, 2 * W :], xh)))

    return update


def across(top, low, update):
    middle = update(jnp.concatenate([top[W:], low[:W]], axis=0))
    return jnp.concatenate([top[:W], middle[:W]], axis=0), jnp.concatenate([middle[W:], low[W:]], axis=0)


def joined(g_ref, at):
    g = g_ref[at]
    return g[:W, :W].astype(F32) + g[:W, 2 * W : 3 * W].astype(F32)


def below_rows(message):
    return message[:W], message[W : 2 * W], message[2 * W :]


def across_below(last, low, near, update):
    middle = update(jnp.concatenate([low[W:], jnp.where(last, 0.0, near)], axis=0))
    return jnp.concatenate([low[:W], middle[:W]], axis=0), middle[W:]


def carried(settled, quarter, change):
    return settled + (change - dot3(split(quarter), split(change)))


def across_above(first, above, top, update):
    new_above, new_top = across(above, top, update)
    return new_above, jnp.where(first, top, new_top)


def keep_kernel(piece, kept):
    kept[...] = piece[...]


def order_kernel(plane, p0, p1, p2, p3, near, far, held):
    for k, piece in enumerate((p0, p1, p2, p3)):
        held[(plane[0] + 4 - k) % 4] = piece[...]
    near[...] = held[0:2]
    far[...] = held[2:4]


def first_kernel(scalars, x_ref, p0, p1, p2, p3, message, low_ref, rest, held):
    pieces = (p0, p1, p2, p3)
    gathered(scalars, pieces, held, 1)
    ahead = block_of(scalars, held, 2, 0)
    gathered(scalars, pieces, held, 0)
    found = factors([block_of(scalars, held, level, half) for level, half in ((0, 0), (0, 1), (1, 0))] + [ahead])
    ah, al, vh, vl = found[3]
    left = dot3((vh, vl), (ah[:, :W], al[:, :W]))
    top = twice(found[0])(x_ref[: 2 * W])
    low = twice(found[1])(x_ref[2 * W :])
    top, low = across(top, low, twice(found[2]))
    settled = twice(found[3])(top)
    message[:W] = top[:W]
    message[W : 2 * W] = settled[:W]
    message[2 * W :] = left[:W]
    rest[:W] = settled[W:]
    rest[W:] = left[W:]
    low_ref[...] = low


def factor1_kernel(scalars, after, p0, p1, p2, p3, g1, held):
    pieces = (p0, p1, p2, p3)
    gathered(scalars, pieces, held, 0)
    early = block_of(scalars, held, 1, 1)
    gathered(scalars, pieces, held, 1)
    late = [block_of(scalars, held, level, half) for level, half in ((2, 1), (3, 0), (3, 1))]
    stored_wholes([*late, early], g1)


def second_kernel(scalars, low_ref, message, g1, low_out, back):
    last = scalars[1] == 1
    near, settled, quarter = below_rows(message)
    low, moved = across_below(last, low_ref[...], near, once(g1, 3))
    change = moved - near
    low = once(g1, 0)(low)
    low, moved = across_below(last, low, carried(settled, quarter, change), once(g1, 2))
    low_out[...] = low
    back[:W] = moved
    back[W:] = change


def choose_kernel(scalars, after, p0, p1, p2, p3, down, held):
    pieces = (p0, p1, p2, p3)
    gathered(scalars, pieces, held, 1)
    down[1] = block_of(scalars, held, 6, 1)
    down[2] = block_of(scalars, held, 7, 1)
    gathered(scalars, pieces, held, 0)
    down[0] = block_of(scalars, held, 5, 1)


def factor2_kernel(scalars, after, p0, p1, p2, p3, g2, held):
    pieces = (p0, p1, p2, p3)
    gathered(scalars, pieces, held, 1)
    later = block_of(scalars, held, 6, 0)
    gathered(scalars, pieces, held, 0)
    stored_wholes([block_of(scalars, held, level, half) for level in (4, 5) for half in (0, 1)] + [later], g2)


def third_kernel(scalars, low_ref, own, rest, back, g1, g2, low_out, top_out, far_out, near_out):
    upper = jnp.where(scalars[2] == 1, own[W : 2 * W], back[:W])
    lower = rest[:W] - dot3(split(rest[W:]), split(back[W:]))
    top, low = across(jnp.concatenate([upper, lower], axis=0), low_ref[...], once(g1, 1))
    top = once(g2, 0)(top)
    low = once(g2, 1)(low)
    top, low = across(top, low, once(g2, 2))
    low_out[...] = low
    top_out[...] = top
    settled = once(g2, 4)(top)
    odd = scalars[3] == 1
    for at, (up, down) in enumerate(((top[:W], low[:W]), (settled[:W], low[W:]), (joined(g2, 4), top[W:]))):
        far_out[at * W : (at + 1) * W] = jnp.where(odd, down, up)
        near_out[at * W : (at + 1) * W] = jnp.where(odd, up, down)


def factor3_kernel(scalars, after, p0, p1, p2, p3, g3, held):
    gathered(scalars, (p0, p1, p2, p3), held, 1)
    stored_wholes([block_of(scalars, held, level, half) for level, half in ((6, 1), (7, 0), (7, 1))], g3)


def factor4_kernel(after, down, g4):
    stored_wholes([down[0], down[1], down[2]], g4)


def fourth_kernel(scalars, low_ref, top_ref, far, near, g2, g3, g4, out_ref):
    last = scalars[1] == 1
    first = scalars[2] == 1
    odd = scalars[3] == 1
    above = jnp.where(odd, near[: 2 * W], far[: 2 * W])
    near, settled, quarter = below_rows(jnp.where(odd, far[...], near[...]))
    low, moved = across_below(last, low_ref[...], near, once(g2, 3))
    above, top = across_above(first, above, top_ref[...], once(g4, 0))
    above = once(g4, 1)(above)
    top = once(g2, 4)(top)
    low = once(g3, 0)(low)
    _, top = across_above(first, above, top, once(g4, 2))
    low, _ = across_below(last, low, carried(settled, quarter, moved - near), once(g3, 2))
    top, low = across(top, low, once(g3, 1))
    out_ref[: 2 * W] = top
    out_ref[2 * W :] = low


def wholes(count):
    return jax.ShapeDtypeStruct((count, 2 * W, 4 * W), BF16)


def rows_shape(*shape):
    return jax.ShapeDtypeStruct(shape, F32)


HELD = [pltpu.VMEM((4, W, W), F32)]


def call(kernel, args, shapes, scratch=(), smem=1, flops=400_000_000):
    return pl.pallas_call(
        kernel,
        out_shape=tuple(shapes),
        in_specs=[pl.BlockSpec(memory_space=SMEM)] * smem + [pl.BlockSpec(memory_space=VMEM)] * (len(args) - smem),
        out_specs=(pl.BlockSpec(memory_space=VMEM),) * len(shapes),
        scratch_shapes=list(scratch),
        compiler_params=pltpu.CompilerParams(vmem_limit_bytes=24 * 1024 * 1024),
        cost_estimate=pl.CostEstimate(flops=flops, bytes_accessed=2_000_000, transcendentals=0),
        name=kernel.__name__,
    )(*args)


def shifted(value, axis, steps):
    count = lax.axis_size(axis)
    return lax.ppermute(value, axis, [(i, (i + steps) % count) for i in range(count)])


def to_neighbour(value, steps):
    count = lax.axis_size("rows")
    return lax.ppermute(value, "rows", [(i, i + steps) for i in range(count) if 0 <= i + steps < count])


def swapped(value, start):
    count = lax.axis_size("rows")
    pairs = [(i, i + 1) for i in range(start, count - 1, 2)]
    return lax.ppermute(value, "rows", pairs + [(j, i) for i, j in pairs])


def along_x(value):
    found = {k: lax.ppermute(value, "cols", [(i, (i // 4) * 4 + (i + k) % 4) for i in range(16)]) for k in (3, 2, 1)}
    return [value, found[1], found[2], found[3]]


def per_device(eigvecs, wy_packed, slot_block):
    column = lax.axis_index("cols")
    row = lax.axis_index("rows")
    plane, place = column // 4, column % 4
    edges = jnp.stack([place, row == lax.axis_size("rows") - 1, row == 0, row % 2]).astype(jnp.int32)
    scalars = jnp.concatenate([edges, slot_block.reshape(-1)])
    packed = wy_packed[0]
    half = rows_shape(2 * W, W)

    (held,) = call(keep_kernel, (packed,), [rows_shape(W, W)], smem=0)
    planes = [packed] + [shifted(packed, "cols", 4 * k) for k in (1, 2, 3)]
    pair = rows_shape(2, W, W)
    near, far = call(order_kernel, (plane.reshape(1), held, *planes[1:]), [pair, pair], HELD)
    near = along_x(near)
    far = along_x(far)
    three = rows_shape(3 * W, W)
    three = rows_shape(3 * W, W)
    own, low, rest = call(first_kernel, (scalars, eigvecs, *near), [three, half, half], HELD)
    message = to_neighbour(own, -1)
    (down,) = call(choose_kernel, (scalars, low, *far), [rows_shape(3, W, W)], HELD)
    (g1,) = call(factor1_kernel, (scalars, down, *near), [wholes(4)], HELD)
    low, back = call(second_kernel, (scalars, low, message, g1), [half, half])
    back = to_neighbour(back, 1)
    (g2,) = call(factor2_kernel, (scalars, low, *far), [wholes(5)], HELD)
    down = to_neighbour(down, 1)
    low, top, far_out, near_out = call(
        third_kernel, (scalars, low, own, rest, back, g1, g2), [half, half, three, three]
    )
    from_far = swapped(far_out, 1)
    from_near = swapped(near_out, 0)
    (g3,) = call(factor3_kernel, (scalars, low, *far), [wholes(3)], HELD)
    (g4,) = call(factor4_kernel, (low, down), [wholes(3)], smem=0)
    return call(
        fourth_kernel, (scalars, low, top, from_far, from_near, g2, g3, g4), [rows_shape(*eigvecs.shape)]
    )[0]


def solution(mesh):
    placed = (P("rows", "cols"), P(("rows", "cols"), None, None), P("rows", None, None))
    return jax.shard_map(
        per_device, mesh=mesh, in_specs=placed, out_specs=P("rows", "cols"), check_vma=False
    )
```

```python
import jax
import jax.numpy as jnp
from jax import lax
from jax.experimental import pallas as pl
from jax.experimental.pallas import tpu as pltpu
from jax.sharding import PartitionSpec as P

F32 = jnp.float32
BF16 = jnp.bfloat16
W = 128
SUB = 32
VMEM = pltpu.VMEM
SMEM = pltpu.SMEM


def split(x):
    high = x.astype(BF16)
    low = (x - high.astype(F32)).astype(BF16)
    return high, low


def mm(a, b, dims=((1,), (0,))):
    return lax.dot_general(a, b, (dims, ((), ())), preferred_element_type=F32)


def dot3(a, b):
    ah, al = a
    bh, bl = b
    return mm(ah, bh) + (mm(ah, bl) + mm(al, bh))


def unpacked(packed):
    wide = jnp.concatenate([packed.T, jnp.zeros((W, W), F32)], axis=1)
    return pltpu.roll(wide, 0, axis=1, stride=1, stride_axis=0)


def diagonal_inverses(grams):
    row = lax.broadcasted_iota(jnp.int32, (SUB, W), 0)
    lane = lax.broadcasted_iota(jnp.int32, (SUB, W), 1)
    group = lane // SUB
    place = lane % SUB
    base = group * SUB

    def prepared(gram):
        compact = gram[0:SUB]
        for d in range(1, 4):
            compact = jnp.where(group == d, gram[d * SUB : (d + 1) * SUB], compact)
        diagonal = jnp.sum(jnp.where(row == place, compact, 0.0), axis=0, keepdims=True)
        scale = jnp.broadcast_to(2.0 / diagonal, (SUB, W))
        return jnp.where(row < place, compact * scale, 0.0), scale

    pairs = [prepared(gram) for gram in grams]
    start = [jnp.where(row == place, 1.0, 0.0)[8 * i : 8 * i + 8] for i in range(4)]
    rows = [list(start) for _ in grams]
    for k in range(SUB - 1, 0, -1):
        tile, at = k // 8, k % 8
        for n in range(len(grams)):
            pivot = jnp.broadcast_to(rows[n][tile][at : at + 1], (8, W))
            for i in range(tile + 1):
                if i * 8 < k:
                    factor = jnp.take_along_axis(
                        pairs[n][0][8 * i : 8 * i + 8], base[8 * i : 8 * i + 8] + k, axis=1, mode="promise_in_bounds"
                    )
                    rows[n][i] = rows[n][i] - factor * pivot
    row_scales = [jnp.take_along_axis(scale, base + row, axis=1, mode="promise_in_bounds") for _, scale in pairs]
    return [jnp.concatenate(r, axis=0) * s for r, s in zip(rows, row_scales)]


def dots3(lefts, rights):
    return [dot3(a, b) for a, b in zip(lefts, rights)]


def splits(values):
    return [split(v) for v in values]


def triangle_inverses(grams):
    small = diagonal_inverses(grams)
    lane = lax.broadcasted_iota(jnp.int32, (SUB, W), 1)
    group = lane // SUB
    half = 2 * SUB
    zero = jnp.zeros((SUB, W), F32)
    zeros = jnp.zeros((half, W), F32)
    parts = [[jnp.where(group == d, s, 0.0) for d in range(4)] for s in small]
    bases = splits([jnp.concatenate(p, axis=0) for p in parts])
    corners = splits(
        [
            jnp.concatenate(
                [jnp.where(group == 1, g[0:SUB], 0.0), jnp.where(group == 3, g[2 * SUB : 3 * SUB], 0.0)], axis=0
            )
            for g in grams
        ]
    )
    lane2 = lax.broadcasted_iota(jnp.int32, (half, W), 1)
    corners2 = splits([jnp.where(lane2 >= half, g[0:half], 0.0) for g in grams])
    products = dots3(corners, bases)
    fulls = splits([jnp.concatenate([p[0:SUB], zero, p[SUB:], zero], axis=0) for p in products])
    changes = dots3(splits([jnp.concatenate([p[0], p[2]], axis=0) for p in parts]), fulls)
    uppers = [jnp.concatenate([p[0] - c[0:SUB], p[1]], axis=0) for p, c in zip(parts, changes)]
    lowers = [jnp.concatenate([p[2] - c[SUB:], p[3]], axis=0) for p, c in zip(parts, changes)]
    products = dots3(corners2, splits([jnp.concatenate([zeros, low], axis=0) for low in lowers]))
    changes = dots3(splits(uppers), splits([jnp.concatenate([p, zeros], axis=0) for p in products]))
    return [jnp.concatenate([u - c, low], axis=0) for u, c, low in zip(uppers, changes, lowers)]


def factors(packed):
    reflectors = [unpacked(p) for p in packed]
    halves = splits(reflectors)
    nt = ((1,), (1,))
    grams = [mm(h, h, nt) + (mm(h, l, nt) + mm(l, h, nt)) for h, l in halves]
    inverses = splits(triangle_inverses(grams))
    products = splits(dots3(inverses, halves))
    return [(*a, *split(r.T)) for a, r in zip(products, reflectors)]


def whole(factor):
    ah, al, vh, vl = factor
    return jnp.concatenate(split(dot3((vh, vl), (ah, al))), axis=1)


def stored_wholes(packed, g_ref):
    for at, factor in enumerate(factors(packed)):
        g_ref[at] = whole(factor)


def slot_of(scalars, level, half):
    return scalars[4 + 2 * level + half]


def gathered(scalars, pieces, held, at):
    for k in range(4):
        held[(scalars[0] + 4 - k) % 4] = pieces[k][at]


def block_of(scalars, held, level, half):
    return held[2 * (level % 2) + slot_of(scalars, level, half)]


def twice(factor):
    ah, al, vh, vl = factor

    def update(x):
        return x - dot3((vh, vl), split(dot3((ah, al), split(x))))

    return update


def once(g_ref, at):
    g = g_ref[at]

    def update(x):
        xh, xl = split(x)
        wide = mm(g[:, : 2 * W], jnp.concatenate([xh, xl], axis=1))
        return x - (wide[:, :W] + (wide[:, W:] + mm(g[:, 2 * W :], xh)))

    return update


def across(top, low, update):
    middle = update(jnp.concatenate([top[W:], low[:W]], axis=0))
    return jnp.concatenate([top[:W], middle[:W]], axis=0), jnp.concatenate([middle[W:], low[W:]], axis=0)


def joined(g_ref, at):
    g = g_ref[at]
    return g[:W, :W].astype(F32) + g[:W, 2 * W : 3 * W].astype(F32)


def below_rows(message):
    return message[:W], message[W : 2 * W], message[2 * W :]


def across_below(last, low, near, update):
    middle = update(jnp.concatenate([low[W:], jnp.where(last, 0.0, near)], axis=0))
    return jnp.concatenate([low[:W], middle[:W]], axis=0), middle[W:]


def carried(settled, quarter, change):
    return settled + (change - dot3(split(quarter), split(change)))


def across_above(first, above, top, update):
    new_above, new_top = across(above, top, update)
    return new_above, jnp.where(first, top, new_top)


def keep_kernel(piece, kept):
    kept[...] = piece[...]


def order_kernel(plane, p0, p1, p2, p3, near, far, held):
    for k, piece in enumerate((p0, p1, p2, p3)):
        held[(plane[0] + 4 - k) % 4] = piece[...]
    near[...] = held[0:2]
    far[...] = held[2:4]


def first_kernel(scalars, x_ref, p0, p1, p2, p3, message, low_ref, rest, held):
    pieces = (p0, p1, p2, p3)
    gathered(scalars, pieces, held, 1)
    ahead = block_of(scalars, held, 2, 0)
    gathered(scalars, pieces, held, 0)
    found = factors([block_of(scalars, held, level, half) for level, half in ((0, 0), (0, 1), (1, 0))] + [ahead])
    ah, al, vh, vl = found[3]
    left = dot3((vh, vl), (ah[:, :W], al[:, :W]))
    top = twice(found[0])(x_ref[: 2 * W])
    low = twice(found[1])(x_ref[2 * W :])
    top, low = across(top, low, twice(found[2]))
    settled = twice(found[3])(top)
    message[:W] = top[:W]
    message[W : 2 * W] = settled[:W]
    message[2 * W :] = left[:W]
    rest[:W] = settled[W:]
    rest[W:] = left[W:]
    low_ref[...] = low


def factor1_kernel(scalars, after, p0, p1, p2, p3, g1, held):
    pieces = (p0, p1, p2, p3)
    gathered(scalars, pieces, held, 0)
    early = block_of(scalars, held, 1, 1)
    gathered(scalars, pieces, held, 1)
    late = [block_of(scalars, held, level, half) for level, half in ((2, 1), (3, 0), (3, 1))]
    stored_wholes([*late, early], g1)


def second_kernel(scalars, low_ref, message, g1, low_out, back):
    last = scalars[1] == 1
    near, settled, quarter = below_rows(message)
    low, moved = across_below(last, low_ref[...], near, once(g1, 3))
    change = moved - near
    low = once(g1, 0)(low)
    low, moved = across_below(last, low, carried(settled, quarter, change), once(g1, 2))
    low_out[...] = low
    back[:W] = moved
    back[W:] = change


def choose_kernel(scalars, after, p0, p1, p2, p3, down, held):
    pieces = (p0, p1, p2, p3)
    gathered(scalars, pieces, held, 1)
    down[1] = block_of(scalars, held, 6, 1)
    down[2] = block_of(scalars, held, 7, 1)
    gathered(scalars, pieces, held, 0)
    down[0] = block_of(scalars, held, 5, 1)


def factor2_kernel(scalars, after, p0, p1, p2, p3, g2, held):
    pieces = (p0, p1, p2, p3)
    gathered(scalars, pieces, held, 1)
    later = block_of(scalars, held, 6, 0)
    gathered(scalars, pieces, held, 0)
    stored_wholes([block_of(scalars, held, level, half) for level in (4, 5) for half in (0, 1)] + [later], g2)


def third_kernel(scalars, low_ref, own, rest, back, after, g1, g2, low_out, top_out, far_out, near_out):
    upper = jnp.where(scalars[2] == 1, own[W : 2 * W], back[:W])
    lower = rest[:W] - dot3(split(rest[W:]), split(back[W:]))
    top, low = across(jnp.concatenate([upper, lower], axis=0), low_ref[...], once(g1, 1))
    top = once(g2, 0)(top)
    low = once(g2, 1)(low)
    top, low = across(top, low, once(g2, 2))
    low_out[...] = low
    top_out[...] = top
    settled = once(g2, 4)(top)
    odd = scalars[3] == 1
    for at, (up, down) in enumerate(((top[:W], low[:W]), (settled[:W], low[W:]), (joined(g2, 4), top[W:]))):
        far_out[at * W : (at + 1) * W] = jnp.where(odd, down, up)
        near_out[at * W : (at + 1) * W] = jnp.where(odd, up, down)


def factor3_kernel(scalars, after, p0, p1, p2, p3, g3, held):
    gathered(scalars, (p0, p1, p2, p3), held, 1)
    stored_wholes([block_of(scalars, held, level, half) for level, half in ((6, 1), (7, 0), (7, 1))], g3)


def factor4_kernel(after, down, g4):
    stored_wholes([down[0], down[1], down[2]], g4)


def fourth_kernel(scalars, low_ref, top_ref, far, near, g2, g3, g4, out_ref):
    last = scalars[1] == 1
    first = scalars[2] == 1
    odd = scalars[3] == 1
    above = jnp.where(odd, near[: 2 * W], far[: 2 * W])
    near, settled, quarter = below_rows(jnp.where(odd, far[...], near[...]))
    low, moved = across_below(last, low_ref[...], near, once(g2, 3))
    above, top = across_above(first, above, top_ref[...], once(g4, 0))
    above = once(g4, 1)(above)
    top = once(g2, 4)(top)
    low = once(g3, 0)(low)
    _, top = across_above(first, above, top, once(g4, 2))
    low, _ = across_below(last, low, carried(settled, quarter, moved - near), once(g3, 2))
    top, low = across(top, low, once(g3, 1))
    out_ref[: 2 * W] = top
    out_ref[2 * W :] = low


def wholes(count):
    return jax.ShapeDtypeStruct((count, 2 * W, 4 * W), BF16)


def rows_shape(*shape):
    return jax.ShapeDtypeStruct(shape, F32)


HELD = [pltpu.VMEM((4, W, W), F32)]


def call(kernel, args, shapes, scratch=(), smem=1, flops=400_000_000):
    return pl.pallas_call(
        kernel,
        out_shape=tuple(shapes),
        in_specs=[pl.BlockSpec(memory_space=SMEM)] * smem + [pl.BlockSpec(memory_space=VMEM)] * (len(args) - smem),
        out_specs=(pl.BlockSpec(memory_space=VMEM),) * len(shapes),
        scratch_shapes=list(scratch),
        compiler_params=pltpu.CompilerParams(vmem_limit_bytes=24 * 1024 * 1024),
        cost_estimate=pl.CostEstimate(flops=flops, bytes_accessed=2_000_000, transcendentals=0),
        name=kernel.__name__,
    )(*args)


def shifted(value, axis, steps):
    count = lax.axis_size(axis)
    return lax.ppermute(value, axis, [(i, (i + steps) % count) for i in range(count)])


def to_neighbour(value, steps):
    count = lax.axis_size("rows")
    return lax.ppermute(value, "rows", [(i, i + steps) for i in range(count) if 0 <= i + steps < count])


def swapped(value, start):
    count = lax.axis_size("rows")
    pairs = [(i, i + 1) for i in range(start, count - 1, 2)]
    return lax.ppermute(value, "rows", pairs + [(j, i) for i, j in pairs])


def along_x(value):
    found = {k: lax.ppermute(value, "cols", [(i, (i // 4) * 4 + (i + k) % 4) for i in range(16)]) for k in (3, 2, 1)}
    return [value, found[1], found[2], found[3]]


def per_device(eigvecs, wy_packed, slot_block):
    column = lax.axis_index("cols")
    row = lax.axis_index("rows")
    plane, place = column // 4, column % 4
    edges = jnp.stack([place, row == lax.axis_size("rows") - 1, row == 0, row % 2]).astype(jnp.int32)
    scalars = jnp.concatenate([edges, slot_block.reshape(-1)])
    packed = wy_packed[0]
    half = rows_shape(2 * W, W)

    (held,) = call(keep_kernel, (packed,), [rows_shape(W, W)], smem=0)
    planes = [packed] + [shifted(packed, "cols", 4 * k) for k in (1, 2, 3)]
    pair = rows_shape(2, W, W)
    near, far = call(order_kernel, (plane.reshape(1), held, *planes[1:]), [pair, pair], HELD)
    near = along_x(near)
    far = along_x(far)
    three = rows_shape(3 * W, W)
    three = rows_shape(3 * W, W)
    own, low, rest = call(first_kernel, (scalars, eigvecs, *near), [three, half, half], HELD)
    message = to_neighbour(own, -1)
    (down,) = call(choose_kernel, (scalars, low, *far), [rows_shape(3, W, W)], HELD)
    (g1,) = call(factor1_kernel, (scalars, down, *near), [wholes(4)], HELD)
    low, back = call(second_kernel, (scalars, low, message, g1), [half, half])
    back = to_neighbour(back, 1)
    (g2,) = call(factor2_kernel, (scalars, low, *far), [wholes(5)], HELD)
    down = to_neighbour(down, 1)
    low, top, far_out, near_out = call(
        third_kernel, (scalars, low, own, rest, back, down, g1, g2), [half, half, three, three]
    )
    from_far = swapped(far_out, 1)
    from_near = swapped(near_out, 0)
    (g3,) = call(factor3_kernel, (scalars, low, *far), [wholes(3)], HELD)
    (g4,) = call(factor4_kernel, (low, down), [wholes(3)], smem=0)
    return call(
        fourth_kernel, (scalars, low, top, from_far, from_near, g2, g3, g4), [rows_shape(*eigvecs.shape)]
    )[0]


def solution(mesh):
    placed = (P("rows", "cols"), P(("rows", "cols"), None, None), P("rows", None, None))
    return jax.shard_map(
        per_device, mesh=mesh, in_specs=placed, out_specs=P("rows", "cols"), check_vma=False
    )
```

```python
import jax
import jax.numpy as jnp
from jax import lax
from jax.experimental import pallas as pl
from jax.experimental.pallas import tpu as pltpu
from jax.sharding import PartitionSpec as P

F32 = jnp.float32
BF16 = jnp.bfloat16
W = 128
SUB = 32
VMEM = pltpu.VMEM
SMEM = pltpu.SMEM


def split(x):
    high = x.astype(BF16)
    low = (x - high.astype(F32)).astype(BF16)
    return high, low


def mm(a, b, dims=((1,), (0,))):
    return lax.dot_general(a, b, (dims, ((), ())), preferred_element_type=F32)


def dot3(a, b):
    ah, al = a
    bh, bl = b
    return mm(ah, bh) + (mm(ah, bl) + mm(al, bh))


def unpacked(packed):
    wide = jnp.concatenate([packed.T, jnp.zeros((W, W), F32)], axis=1)
    return pltpu.roll(wide, 0, axis=1, stride=1, stride_axis=0)


def diagonal_inverses(grams):
    row = lax.broadcasted_iota(jnp.int32, (SUB, W), 0)
    lane = lax.broadcasted_iota(jnp.int32, (SUB, W), 1)
    group = lane // SUB
    place = lane % SUB
    base = group * SUB

    def prepared(gram):
        compact = gram[0:SUB]
        for d in range(1, 4):
            compact = jnp.where(group == d, gram[d * SUB : (d + 1) * SUB], compact)
        diagonal = jnp.sum(jnp.where(row == place, compact, 0.0), axis=0, keepdims=True)
        scale = jnp.broadcast_to(2.0 / diagonal, (SUB, W))
        return jnp.where(row < place, compact * scale, 0.0), scale

    pairs = [prepared(gram) for gram in grams]
    start = [jnp.where(row == place, 1.0, 0.0)[8 * i : 8 * i + 8] for i in range(4)]
    rows = [list(start) for _ in grams]
    for k in range(SUB - 1, 0, -1):
        tile, at = k // 8, k % 8
        for n in range(len(grams)):
            pivot = jnp.broadcast_to(rows[n][tile][at : at + 1], (8, W))
            for i in range(tile + 1):
                if i * 8 < k:
                    factor = jnp.take_along_axis(
                        pairs[n][0][8 * i : 8 * i + 8], base[8 * i : 8 * i + 8] + k, axis=1, mode="promise_in_bounds"
                    )
                    rows[n][i] = rows[n][i] - factor * pivot
    row_scales = [jnp.take_along_axis(scale, base + row, axis=1, mode="promise_in_bounds") for _, scale in pairs]
    return [jnp.concatenate(r, axis=0) * s for r, s in zip(rows, row_scales)]


def dots3(lefts, rights):
    return [dot3(a, b) for a, b in zip(lefts, rights)]


def splits(values):
    return [split(v) for v in values]


def triangle_inverses(grams):
    small = diagonal_inverses(grams)
    lane = lax.broadcasted_iota(jnp.int32, (SUB, W), 1)
    group = lane // SUB
    half = 2 * SUB
    zero = jnp.zeros((SUB, W), F32)
    zeros = jnp.zeros((half, W), F32)
    parts = [[jnp.where(group == d, s, 0.0) for d in range(4)] for s in small]
    bases = splits([jnp.concatenate(p, axis=0) for p in parts])
    corners = splits(
        [
            jnp.concatenate(
                [jnp.where(group == 1, g[0:SUB], 0.0), jnp.where(group == 3, g[2 * SUB : 3 * SUB], 0.0)], axis=0
            )
            for g in grams
        ]
    )
    lane2 = lax.broadcasted_iota(jnp.int32, (half, W), 1)
    corners2 = splits([jnp.where(lane2 >= half, g[0:half], 0.0) for g in grams])
    products = dots3(corners, bases)
    fulls = splits([jnp.concatenate([p[0:SUB], zero, p[SUB:], zero], axis=0) for p in products])
    changes = dots3(splits([jnp.concatenate([p[0], p[2]], axis=0) for p in parts]), fulls)
    uppers = [jnp.concatenate([p[0] - c[0:SUB], p[1]], axis=0) for p, c in zip(parts, changes)]
    lowers = [jnp.concatenate([p[2] - c[SUB:], p[3]], axis=0) for p, c in zip(parts, changes)]
    products = dots3(corners2, splits([jnp.concatenate([zeros, low], axis=0) for low in lowers]))
    changes = dots3(splits(uppers), splits([jnp.concatenate([p, zeros], axis=0) for p in products]))
    return [jnp.concatenate([u - c, low], axis=0) for u, c, low in zip(uppers, changes, lowers)]


def factors(packed):
    reflectors = [unpacked(p) for p in packed]
    halves = splits(reflectors)
    nt = ((1,), (1,))
    grams = [mm(h, h, nt) + (mm(h, l, nt) + mm(l, h, nt)) for h, l in halves]
    inverses = splits(triangle_inverses(grams))
    products = splits(dots3(inverses, halves))
    return [(*a, *split(r.T)) for a, r in zip(products, reflectors)]


def whole(factor):
    ah, al, vh, vl = factor
    return jnp.concatenate(split(dot3((vh, vl), (ah, al))), axis=1)


def stored_wholes(packed, g_ref):
    for at, factor in enumerate(factors(packed)):
        g_ref[at] = whole(factor)


def slot_of(scalars, level, half):
    return scalars[4 + 2 * level + half]


def gathered(scalars, pieces, held, at):
    for k in range(4):
        held[(scalars[0] + 4 - k) % 4] = pieces[k][at]


def block_of(scalars, held, level, half):
    return held[2 * (level % 2) + slot_of(scalars, level, half)]


def twice(factor):
    ah, al, vh, vl = factor

    def update(x):
        return x - dot3((vh, vl), split(dot3((ah, al), split(x))))

    return update


def once(g_ref, at):
    g = g_ref[at]

    def update(x):
        xh, xl = split(x)
        wide = mm(g[:, : 2 * W], jnp.concatenate([xh, xl], axis=1))
        return x - (wide[:, :W] + (wide[:, W:] + mm(g[:, 2 * W :], xh)))

    return update


def across(top, low, update):
    middle = update(jnp.concatenate([top[W:], low[:W]], axis=0))
    return jnp.concatenate([top[:W], middle[:W]], axis=0), jnp.concatenate([middle[W:], low[W:]], axis=0)


def joined(g_ref, at):
    g = g_ref[at]
    return g[:W, :W].astype(F32) + g[:W, 2 * W : 3 * W].astype(F32)


def below_rows(message):
    return message[:W], message[W : 2 * W], message[2 * W :]


def across_below(last, low, near, update):
    middle = update(jnp.concatenate([low[W:], jnp.where(last, 0.0, near)], axis=0))
    return jnp.concatenate([low[:W], middle[:W]], axis=0), middle[W:]


def carried(settled, quarter, change):
    return settled + (change - dot3(split(quarter), split(change)))


def across_above(first, above, top, update):
    new_above, new_top = across(above, top, update)
    return new_above, jnp.where(first, top, new_top)


def keep_kernel(piece, kept):
    kept[...] = piece[...]


def order_kernel(plane, p0, p1, p2, p3, near, far, held):
    for k, piece in enumerate((p0, p1, p2, p3)):
        held[(plane[0] + 4 - k) % 4] = piece[...]
    near[...] = held[0:2]
    far[...] = held[2:4]


def first_kernel(scalars, x_ref, p0, p1, p2, p3, message, low_ref, rest, held):
    pieces = (p0, p1, p2, p3)
    gathered(scalars, pieces, held, 1)
    ahead = block_of(scalars, held, 2, 0)
    gathered(scalars, pieces, held, 0)
    found = factors([block_of(scalars, held, level, half) for level, half in ((0, 0), (0, 1), (1, 0))] + [ahead])
    ah, al, vh, vl = found[3]
    left = dot3((vh, vl), (ah[:, :W], al[:, :W]))
    top = twice(found[0])(x_ref[: 2 * W])
    low = twice(found[1])(x_ref[2 * W :])
    top, low = across(top, low, twice(found[2]))
    settled = twice(found[3])(top)
    message[:W] = top[:W]
    message[W : 2 * W] = settled[:W]
    message[2 * W :] = left[:W]
    rest[:W] = settled[W:]
    rest[W:] = left[W:]
    low_ref[...] = low


def factor1_kernel(scalars, after, p0, p1, p2, p3, g1, held):
    pieces = (p0, p1, p2, p3)
    gathered(scalars, pieces, held, 0)
    early = block_of(scalars, held, 1, 1)
    gathered(scalars, pieces, held, 1)
    late = [block_of(scalars, held, level, half) for level, half in ((2, 1), (3, 0), (3, 1))]
    stored_wholes([*late, early], g1)


def second_kernel(scalars, low_ref, message, g1, low_out, back):
    last = scalars[1] == 1
    near, settled, quarter = below_rows(message)
    low, moved = across_below(last, low_ref[...], near, once(g1, 3))
    change = moved - near
    low = once(g1, 0)(low)
    low, moved = across_below(last, low, carried(settled, quarter, change), once(g1, 2))
    low_out[...] = low
    back[:W] = moved
    back[W:] = change


def choose_kernel(scalars, after, p0, p1, p2, p3, down, held):
    pieces = (p0, p1, p2, p3)
    gathered(scalars, pieces, held, 1)
    down[1] = block_of(scalars, held, 6, 1)
    down[2] = block_of(scalars, held, 7, 1)
    gathered(scalars, pieces, held, 0)
    down[0] = block_of(scalars, held, 5, 1)


def choose2_kernel(scalars, after, p0, p1, p2, p3, up, held):
    gathered(scalars, (p0, p1, p2, p3), held, 1)
    up[...] = block_of(scalars, held, 6, 0)


def factor2_kernel(scalars, after, p0, p1, p2, p3, g2, held):
    pieces = (p0, p1, p2, p3)
    gathered(scalars, pieces, held, 1)
    later = block_of(scalars, held, 6, 0)
    gathered(scalars, pieces, held, 0)
    stored_wholes([block_of(scalars, held, level, half) for level in (4, 5) for half in (0, 1)] + [later], g2)


def third_kernel(scalars, low_ref, own, rest, back, after, after2, g1, g2, low_out, top_out, far_out, near_out):
    upper = jnp.where(scalars[2] == 1, own[W : 2 * W], back[:W])
    lower = rest[:W] - dot3(split(rest[W:]), split(back[W:]))
    top, low = across(jnp.concatenate([upper, lower], axis=0), low_ref[...], once(g1, 1))
    top = once(g2, 0)(top)
    low = once(g2, 1)(low)
    top, low = across(top, low, once(g2, 2))
    low_out[...] = low
    top_out[...] = top
    settled = once(g2, 4)(top)
    odd = scalars[3] == 1
    for at, (up, down) in enumerate(((top[:W], low[:W]), (settled[:W], low[W:]))):
        far_out[at * W : (at + 1) * W] = jnp.where(odd, down, up)
        near_out[at * W : (at + 1) * W] = jnp.where(odd, up, down)


def factor3_kernel(scalars, after, p0, p1, p2, p3, g3, held):
    gathered(scalars, (p0, p1, p2, p3), held, 1)
    stored_wholes([block_of(scalars, held, level, half) for level, half in ((6, 1), (7, 0), (7, 1))], g3)


def factor4_kernel(after, down, up, g4):
    stored_wholes([down[0], down[1], down[2], up[...]], g4)


def fourth_kernel(scalars, low_ref, top_ref, far, near, g2, g3, g4, out_ref):
    last = scalars[1] == 1
    first = scalars[2] == 1
    odd = scalars[3] == 1
    above = jnp.where(odd, near[...], far[...])
    below = jnp.where(odd, far[...], near[...])
    near, settled, quarter = below[:W], below[W:], joined(g4, 3)
    low, moved = across_below(last, low_ref[...], near, once(g2, 3))
    above, top = across_above(first, above, top_ref[...], once(g4, 0))
    above = once(g4, 1)(above)
    top = once(g2, 4)(top)
    low = once(g3, 0)(low)
    _, top = across_above(first, above, top, once(g4, 2))
    low, _ = across_below(last, low, carried(settled, quarter, moved - near), once(g3, 2))
    top, low = across(top, low, once(g3, 1))
    out_ref[: 2 * W] = top
    out_ref[2 * W :] = low


def wholes(count):
    return jax.ShapeDtypeStruct((count, 2 * W, 4 * W), BF16)


def rows_shape(*shape):
    return jax.ShapeDtypeStruct(shape, F32)


HELD = [pltpu.VMEM((4, W, W), F32)]


def call(kernel, args, shapes, scratch=(), smem=1, flops=400_000_000):
    return pl.pallas_call(
        kernel,
        out_shape=tuple(shapes),
        in_specs=[pl.BlockSpec(memory_space=SMEM)] * smem + [pl.BlockSpec(memory_space=VMEM)] * (len(args) - smem),
        out_specs=(pl.BlockSpec(memory_space=VMEM),) * len(shapes),
        scratch_shapes=list(scratch),
        compiler_params=pltpu.CompilerParams(vmem_limit_bytes=24 * 1024 * 1024),
        cost_estimate=pl.CostEstimate(flops=flops, bytes_accessed=2_000_000, transcendentals=0),
        name=kernel.__name__,
    )(*args)


def shifted(value, axis, steps):
    count = lax.axis_size(axis)
    return lax.ppermute(value, axis, [(i, (i + steps) % count) for i in range(count)])


def to_neighbour(value, steps):
    count = lax.axis_size("rows")
    return lax.ppermute(value, "rows", [(i, i + steps) for i in range(count) if 0 <= i + steps < count])


def swapped(value, start):
    count = lax.axis_size("rows")
    pairs = [(i, i + 1) for i in range(start, count - 1, 2)]
    return lax.ppermute(value, "rows", pairs + [(j, i) for i, j in pairs])


def along_x(value):
    found = {k: lax.ppermute(value, "cols", [(i, (i // 4) * 4 + (i + k) % 4) for i in range(16)]) for k in (3, 2, 1)}
    return [value, found[1], found[2], found[3]]


def per_device(eigvecs, wy_packed, slot_block):
    column = lax.axis_index("cols")
    row = lax.axis_index("rows")
    plane, place = column // 4, column % 4
    edges = jnp.stack([place, row == lax.axis_size("rows") - 1, row == 0, row % 2]).astype(jnp.int32)
    scalars = jnp.concatenate([edges, slot_block.reshape(-1)])
    packed = wy_packed[0]
    half = rows_shape(2 * W, W)

    (held,) = call(keep_kernel, (packed,), [rows_shape(W, W)], smem=0)
    planes = [packed] + [shifted(packed, "cols", 4 * k) for k in (1, 2, 3)]
    pair = rows_shape(2, W, W)
    near, far = call(order_kernel, (plane.reshape(1), held, *planes[1:]), [pair, pair], HELD)
    near = along_x(near)
    far = along_x(far)
    three = rows_shape(3 * W, W)
    three = rows_shape(3 * W, W)
    own, low, rest = call(first_kernel, (scalars, eigvecs, *near), [three, half, half], HELD)
    message = to_neighbour(own, -1)
    (down,) = call(choose_kernel, (scalars, low, *far), [rows_shape(3, W, W)], HELD)
    (g1,) = call(factor1_kernel, (scalars, down, *near), [wholes(4)], HELD)
    low, back = call(second_kernel, (scalars, low, message, g1), [half, half])
    back = to_neighbour(back, 1)
    (up,) = call(choose2_kernel, (scalars, low, *far), [rows_shape(W, W)], HELD)
    (g2,) = call(factor2_kernel, (scalars, up, *far), [wholes(5)], HELD)
    up = to_neighbour(up, -1)
    down = to_neighbour(down, 1)
    low, top, far_out, near_out = call(
        third_kernel, (scalars, low, own, rest, back, down, up, g1, g2), [half, half, half, half]
    )
    from_far = swapped(far_out, 1)
    from_near = swapped(near_out, 0)
    (g3,) = call(factor3_kernel, (scalars, low, *far), [wholes(3)], HELD)
    (g4,) = call(factor4_kernel, (low, down, up), [wholes(4)], smem=0)
    return call(
        fourth_kernel, (scalars, low, top, from_far, from_near, g2, g3, g4), [rows_shape(*eigvecs.shape)]
    )[0]


def solution(mesh):
    placed = (P("rows", "cols"), P(("rows", "cols"), None, None), P("rows", None, None))
    return jax.shard_map(
        per_device, mesh=mesh, in_specs=placed, out_specs=P("rows", "cols"), check_vma=False
    )
```

```python
import jax
import jax.numpy as jnp
from jax import lax
from jax.experimental import pallas as pl
from jax.experimental.pallas import tpu as pltpu
from jax.sharding import PartitionSpec as P

F32 = jnp.float32
BF16 = jnp.bfloat16
W = 128
SUB = 32
VMEM = pltpu.VMEM
SMEM = pltpu.SMEM


def split(x):
    high = x.astype(BF16)
    low = (x - high.astype(F32)).astype(BF16)
    return high, low


def mm(a, b, dims=((1,), (0,))):
    return lax.dot_general(a, b, (dims, ((), ())), preferred_element_type=F32)


def dot3(a, b):
    ah, al = a
    bh, bl = b
    return mm(ah, bh) + (mm(ah, bl) + mm(al, bh))


def unpacked(packed):
    wide = jnp.concatenate([packed.T, jnp.zeros((W, W), F32)], axis=1)
    return pltpu.roll(wide, 0, axis=1, stride=1, stride_axis=0)


def diagonal_inverses(grams):
    row = lax.broadcasted_iota(jnp.int32, (SUB, W), 0)
    lane = lax.broadcasted_iota(jnp.int32, (SUB, W), 1)
    group = lane // SUB
    place = lane % SUB
    base = group * SUB

    def prepared(gram):
        compact = gram[0:SUB]
        for d in range(1, 4):
            compact = jnp.where(group == d, gram[d * SUB : (d + 1) * SUB], compact)
        diagonal = jnp.sum(jnp.where(row == place, compact, 0.0), axis=0, keepdims=True)
        scale = jnp.broadcast_to(2.0 / diagonal, (SUB, W))
        return jnp.where(row < place, compact * scale, 0.0), scale

    pairs = [prepared(gram) for gram in grams]
    start = [jnp.where(row == place, 1.0, 0.0)[8 * i : 8 * i + 8] for i in range(4)]
    rows = [list(start) for _ in grams]
    for k in range(SUB - 1, 0, -1):
        tile, at = k // 8, k % 8
        for n in range(len(grams)):
            pivot = jnp.broadcast_to(rows[n][tile][at : at + 1], (8, W))
            for i in range(tile + 1):
                if i * 8 < k:
                    factor = jnp.take_along_axis(
                        pairs[n][0][8 * i : 8 * i + 8], base[8 * i : 8 * i + 8] + k, axis=1, mode="promise_in_bounds"
                    )
                    rows[n][i] = rows[n][i] - factor * pivot
    row_scales = [jnp.take_along_axis(scale, base + row, axis=1, mode="promise_in_bounds") for _, scale in pairs]
    return [jnp.concatenate(r, axis=0) * s for r, s in zip(rows, row_scales)]


def dots3(lefts, rights):
    return [dot3(a, b) for a, b in zip(lefts, rights)]


def splits(values):
    return [split(v) for v in values]


def triangle_inverses(grams):
    small = diagonal_inverses(grams)
    lane = lax.broadcasted_iota(jnp.int32, (SUB, W), 1)
    group = lane // SUB
    half = 2 * SUB
    zero = jnp.zeros((SUB, W), F32)
    zeros = jnp.zeros((half, W), F32)
    parts = [[jnp.where(group == d, s, 0.0) for d in range(4)] for s in small]
    bases = splits([jnp.concatenate(p, axis=0) for p in parts])
    corners = splits(
        [
            jnp.concatenate(
                [jnp.where(group == 1, g[0:SUB], 0.0), jnp.where(group == 3, g[2 * SUB : 3 * SUB], 0.0)], axis=0
            )
            for g in grams
        ]
    )
    lane2 = lax.broadcasted_iota(jnp.int32, (half, W), 1)
    corners2 = splits([jnp.where(lane2 >= half, g[0:half], 0.0) for g in grams])
    products = dots3(corners, bases)
    fulls = splits([jnp.concatenate([p[0:SUB], zero, p[SUB:], zero], axis=0) for p in products])
    changes = dots3(splits([jnp.concatenate([p[0], p[2]], axis=0) for p in parts]), fulls)
    uppers = [jnp.concatenate([p[0] - c[0:SUB], p[1]], axis=0) for p, c in zip(parts, changes)]
    lowers = [jnp.concatenate([p[2] - c[SUB:], p[3]], axis=0) for p, c in zip(parts, changes)]
    products = dots3(corners2, splits([jnp.concatenate([zeros, low], axis=0) for low in lowers]))
    changes = dots3(splits(uppers), splits([jnp.concatenate([p, zeros], axis=0) for p in products]))
    return [jnp.concatenate([u - c, low], axis=0) for u, c, low in zip(uppers, changes, lowers)]


def factors(packed):
    reflectors = [unpacked(p) for p in packed]
    halves = splits(reflectors)
    nt = ((1,), (1,))
    grams = [mm(h, h, nt) + (mm(h, l, nt) + mm(l, h, nt)) for h, l in halves]
    inverses = splits(triangle_inverses(grams))
    products = splits(dots3(inverses, halves))
    return [(*a, *split(r.T)) for a, r in zip(products, reflectors)]


def whole(factor):
    ah, al, vh, vl = factor
    return jnp.concatenate(split(dot3((vh, vl), (ah, al))), axis=1)


def stored_wholes(packed, g_ref):
    for at, factor in enumerate(factors(packed)):
        g_ref[at] = whole(factor)


def slot_of(scalars, level, half):
    return scalars[4 + 2 * level + half]


def gathered(scalars, pieces, held, at):
    for k in range(4):
        held[(scalars[0] + 4 - k) % 4] = pieces[k][at]


def block_of(scalars, held, level, half):
    return held[2 * (level % 2) + slot_of(scalars, level, half)]


def twice(factor):
    ah, al, vh, vl = factor

    def update(x):
        return x - dot3((vh, vl), split(dot3((ah, al), split(x))))

    return update


def once(g_ref, at):
    g = g_ref[at]

    def update(x):
        xh, xl = split(x)
        wide = mm(g[:, : 2 * W], jnp.concatenate([xh, xl], axis=1))
        return x - (wide[:, :W] + (wide[:, W:] + mm(g[:, 2 * W :], xh)))

    return update


def across(top, low, update):
    middle = update(jnp.concatenate([top[W:], low[:W]], axis=0))
    return jnp.concatenate([top[:W], middle[:W]], axis=0), jnp.concatenate([middle[W:], low[W:]], axis=0)


def joined(g_ref, at):
    g = g_ref[at]
    return g[:W, :W].astype(F32) + g[:W, 2 * W : 3 * W].astype(F32)


def below_rows(message):
    return message[:W], message[W : 2 * W], message[2 * W :]


def across_below(last, low, near, update):
    middle = update(jnp.concatenate([low[W:], jnp.where(last, 0.0, near)], axis=0))
    return jnp.concatenate([low[:W], middle[:W]], axis=0), middle[W:]


def carried(settled, quarter, change):
    return settled + (change - dot3(split(quarter), split(change)))


def across_above(first, above, top, update):
    new_above, new_top = across(above, top, update)
    return new_above, jnp.where(first, top, new_top)


def keep_kernel(piece, kept):
    kept[...] = piece[...]


def order_kernel(plane, p0, p1, p2, p3, near, far, held):
    for k, piece in enumerate((p0, p1, p2, p3)):
        held[(plane[0] + 4 - k) % 4] = piece[...]
    near[...] = held[0:2]
    far[...] = held[2:4]


def first_kernel(scalars, x_ref, p0, p1, p2, p3, message, low_ref, rest, held):
    pieces = (p0, p1, p2, p3)
    gathered(scalars, pieces, held, 1)
    ahead = block_of(scalars, held, 2, 0)
    gathered(scalars, pieces, held, 0)
    found = factors([block_of(scalars, held, level, half) for level, half in ((0, 0), (0, 1), (1, 0))] + [ahead])
    ah, al, vh, vl = found[3]
    left = dot3((vh, vl), (ah[:, :W], al[:, :W]))
    top = twice(found[0])(x_ref[: 2 * W])
    low = twice(found[1])(x_ref[2 * W :])
    top, low = across(top, low, twice(found[2]))
    settled = twice(found[3])(top)
    message[:W] = top[:W]
    message[W : 2 * W] = settled[:W]
    message[2 * W :] = left[:W]
    rest[:W] = settled[W:]
    rest[W:] = left[W:]
    low_ref[...] = low


def factor1_kernel(scalars, after, p0, p1, p2, p3, g1, held):
    pieces = (p0, p1, p2, p3)
    gathered(scalars, pieces, held, 0)
    early = block_of(scalars, held, 1, 1)
    gathered(scalars, pieces, held, 1)
    late = [block_of(scalars, held, level, half) for level, half in ((2, 1), (3, 0), (3, 1))]
    stored_wholes([*late, early], g1)


def second_kernel(scalars, low_ref, message, g1, low_out, back):
    last = scalars[1] == 1
    near, settled, quarter = below_rows(message)
    low, moved = across_below(last, low_ref[...], near, once(g1, 3))
    change = moved - near
    low = once(g1, 0)(low)
    low, moved = across_below(last, low, carried(settled, quarter, change), once(g1, 2))
    low_out[...] = low
    back[:W] = moved
    back[W:] = change


def choose_kernel(scalars, after, p0, p1, p2, p3, down, held):
    pieces = (p0, p1, p2, p3)
    gathered(scalars, pieces, held, 1)
    down[1] = block_of(scalars, held, 6, 1)
    down[2] = block_of(scalars, held, 7, 1)
    gathered(scalars, pieces, held, 0)
    down[0] = block_of(scalars, held, 5, 1)


def factor2_kernel(scalars, after, p0, p1, p2, p3, g2, held):
    pieces = (p0, p1, p2, p3)
    gathered(scalars, pieces, held, 1)
    later = block_of(scalars, held, 6, 0)
    gathered(scalars, pieces, held, 0)
    stored_wholes([block_of(scalars, held, level, half) for level in (4, 5) for half in (0, 1)] + [later], g2)


def third_kernel(scalars, low_ref, own, rest, back, after, g1, g2, low_out, top_out, far_out, near_out):
    upper = jnp.where(scalars[2] == 1, own[W : 2 * W], back[:W])
    lower = rest[:W] - dot3(split(rest[W:]), split(back[W:]))
    top, low = across(jnp.concatenate([upper, lower], axis=0), low_ref[...], once(g1, 1))
    top = once(g2, 0)(top)
    low = once(g2, 1)(low)
    top, low = across(top, low, once(g2, 2))
    low_out[...] = low
    top_out[...] = top
    settled = once(g2, 4)(top)
    odd = scalars[3] == 1
    for at, (up, down) in enumerate(((top[:W], low[:W]), (settled[:W], low[W:]), (joined(g2, 4), top[W:]))):
        far_out[at * W : (at + 1) * W] = jnp.where(odd, down, up)
        near_out[at * W : (at + 1) * W] = jnp.where(odd, up, down)


def factor3_kernel(scalars, after, p0, p1, p2, p3, g3, held):
    gathered(scalars, (p0, p1, p2, p3), held, 1)
    stored_wholes([block_of(scalars, held, level, half) for level, half in ((6, 1), (7, 0), (7, 1))], g3)


def factor4_kernel(after, down, g4):
    stored_wholes([down[0], down[1], down[2]], g4)


def fourth_kernel(scalars, low_ref, top_ref, far, near, g2, g3, g4, out_ref):
    last = scalars[1] == 1
    first = scalars[2] == 1
    odd = scalars[3] == 1
    above = jnp.where(odd, near[: 2 * W], far[: 2 * W])
    near, settled, quarter = below_rows(jnp.where(odd, far[...], near[...]))
    low, moved = across_below(last, low_ref[...], near, once(g2, 3))
    above, top = across_above(first, above, top_ref[...], once(g4, 0))
    above = once(g4, 1)(above)
    top = once(g2, 4)(top)
    low = once(g3, 0)(low)
    _, top = across_above(first, above, top, once(g4, 2))
    low, _ = across_below(last, low, carried(settled, quarter, moved - near), once(g3, 2))
    top, low = across(top, low, once(g3, 1))
    out_ref[: 2 * W] = top
    out_ref[2 * W :] = low


def wholes(count):
    return jax.ShapeDtypeStruct((count, 2 * W, 4 * W), BF16)


def rows_shape(*shape):
    return jax.ShapeDtypeStruct(shape, F32)


HELD = [pltpu.VMEM((4, W, W), F32)]


def call(kernel, args, shapes, scratch=(), smem=1, flops=400_000_000):
    return pl.pallas_call(
        kernel,
        out_shape=tuple(shapes),
        in_specs=[pl.BlockSpec(memory_space=SMEM)] * smem + [pl.BlockSpec(memory_space=VMEM)] * (len(args) - smem),
        out_specs=(pl.BlockSpec(memory_space=VMEM),) * len(shapes),
        scratch_shapes=list(scratch),
        compiler_params=pltpu.CompilerParams(vmem_limit_bytes=24 * 1024 * 1024),
        cost_estimate=pl.CostEstimate(flops=flops, bytes_accessed=2_000_000, transcendentals=0),
        name=kernel.__name__,
    )(*args)


def shifted(value, axis, steps):
    count = lax.axis_size(axis)
    return lax.ppermute(value, axis, [(i, (i + steps) % count) for i in range(count)])


def to_neighbour(value, steps):
    count = lax.axis_size("rows")
    return lax.ppermute(value, "rows", [(i, i + steps) for i in range(count) if 0 <= i + steps < count])


def swapped(value, start):
    count = lax.axis_size("rows")
    pairs = [(i, i + 1) for i in range(start, count - 1, 2)]
    return lax.ppermute(value, "rows", pairs + [(j, i) for i, j in pairs])


def along_x(value):
    found = {k: lax.ppermute(value, "cols", [(i, (i // 4) * 4 + (i + k) % 4) for i in range(16)]) for k in (3, 2, 1)}
    return [value, found[1], found[2], found[3]]


def per_device(eigvecs, wy_packed, slot_block):
    column = lax.axis_index("cols")
    row = lax.axis_index("rows")
    plane, place = column // 4, column % 4
    edges = jnp.stack([place, row == lax.axis_size("rows") - 1, row == 0, row % 2]).astype(jnp.int32)
    scalars = jnp.concatenate([edges, slot_block.reshape(-1)])
    packed = wy_packed[0]
    half = rows_shape(2 * W, W)

    (held,) = call(keep_kernel, (packed,), [rows_shape(W, W)], smem=0)
    planes = [packed] + [shifted(packed, "cols", 4 * k) for k in (1, 2, 3)]
    pair = rows_shape(2, W, W)
    near, far = call(order_kernel, (plane.reshape(1), held, *planes[1:]), [pair, pair], HELD)
    near = along_x(near)
    far = along_x(far)
    three = rows_shape(3 * W, W)
    three = rows_shape(3 * W, W)
    own, low, rest = call(first_kernel, (scalars, eigvecs, *near), [three, half, half], HELD)
    message = to_neighbour(own, -1)
    (g1,) = call(factor1_kernel, (scalars, low, *near), [wholes(4)], HELD)
    (down,) = call(choose_kernel, (scalars, g1, *far), [rows_shape(3, W, W)], HELD)
    low, back = call(second_kernel, (scalars, low, message, g1), [half, half])
    back = to_neighbour(back, 1)
    (g2,) = call(factor2_kernel, (scalars, low, *far), [wholes(5)], HELD)
    down = to_neighbour(down, 1)
    low, top, far_out, near_out = call(
        third_kernel, (scalars, low, own, rest, back, down, g1, g2), [half, half, three, three]
    )
    from_far = swapped(far_out, 1)
    from_near = swapped(near_out, 0)
    (g3,) = call(factor3_kernel, (scalars, low, *far), [wholes(3)], HELD)
    (g4,) = call(factor4_kernel, (low, down), [wholes(3)], smem=0)
    return call(
        fourth_kernel, (scalars, low, top, from_far, from_near, g2, g3, g4), [rows_shape(*eigvecs.shape)]
    )[0]


def solution(mesh):
    placed = (P("rows", "cols"), P(("rows", "cols"), None, None), P("rows", None, None))
    return jax.shard_map(
        per_device, mesh=mesh, in_specs=placed, out_specs=P("rows", "cols"), check_vma=False
    )
```

```python
import jax
import jax.numpy as jnp
from jax import lax
from jax.experimental import pallas as pl
from jax.experimental.pallas import tpu as pltpu
from jax.sharding import PartitionSpec as P

F32 = jnp.float32
BF16 = jnp.bfloat16
W = 128
SUB = 32
VMEM = pltpu.VMEM
SMEM = pltpu.SMEM


def split(x):
    high = x.astype(BF16)
    low = (x - high.astype(F32)).astype(BF16)
    return high, low


def mm(a, b, dims=((1,), (0,))):
    return lax.dot_general(a, b, (dims, ((), ())), preferred_element_type=F32)


def dot3(a, b):
    ah, al = a
    bh, bl = b
    return mm(ah, bh) + (mm(ah, bl) + mm(al, bh))


def unpacked(packed):
    wide = jnp.concatenate([packed.T, jnp.zeros((W, W), F32)], axis=1)
    return pltpu.roll(wide, 0, axis=1, stride=1, stride_axis=0)


def diagonal_inverses(grams):
    row = lax.broadcasted_iota(jnp.int32, (SUB, W), 0)
    lane = lax.broadcasted_iota(jnp.int32, (SUB, W), 1)
    group = lane // SUB
    place = lane % SUB
    base = group * SUB

    def prepared(gram):
        compact = gram[0:SUB]
        for d in range(1, 4):
            compact = jnp.where(group == d, gram[d * SUB : (d + 1) * SUB], compact)
        diagonal = jnp.sum(jnp.where(row == place, compact, 0.0), axis=0, keepdims=True)
        scale = jnp.broadcast_to(2.0 / diagonal, (SUB, W))
        return jnp.where(row < place, compact * scale, 0.0), scale

    pairs = [prepared(gram) for gram in grams]
    start = [jnp.where(row == place, 1.0, 0.0)[8 * i : 8 * i + 8] for i in range(4)]
    rows = [list(start) for _ in grams]
    for k in range(SUB - 1, 0, -1):
        tile, at = k // 8, k % 8
        for n in range(len(grams)):
            pivot = jnp.broadcast_to(rows[n][tile][at : at + 1], (8, W))
            for i in range(tile + 1):
                if i * 8 < k:
                    factor = jnp.take_along_axis(
                        pairs[n][0][8 * i : 8 * i + 8], base[8 * i : 8 * i + 8] + k, axis=1, mode="promise_in_bounds"
                    )
                    rows[n][i] = rows[n][i] - factor * pivot
    row_scales = [jnp.take_along_axis(scale, base + row, axis=1, mode="promise_in_bounds") for _, scale in pairs]
    return [jnp.concatenate(r, axis=0) * s for r, s in zip(rows, row_scales)]


def dots3(lefts, rights):
    return [dot3(a, b) for a, b in zip(lefts, rights)]


def splits(values):
    return [split(v) for v in values]


def triangle_inverses(grams):
    small = diagonal_inverses(grams)
    lane = lax.broadcasted_iota(jnp.int32, (SUB, W), 1)
    group = lane // SUB
    half = 2 * SUB
    zero = jnp.zeros((SUB, W), F32)
    zeros = jnp.zeros((half, W), F32)
    parts = [[jnp.where(group == d, s, 0.0) for d in range(4)] for s in small]
    bases = splits([jnp.concatenate(p, axis=0) for p in parts])
    corners = splits(
        [
            jnp.concatenate(
                [jnp.where(group == 1, g[0:SUB], 0.0), jnp.where(group == 3, g[2 * SUB : 3 * SUB], 0.0)], axis=0
            )
            for g in grams
        ]
    )
    lane2 = lax.broadcasted_iota(jnp.int32, (half, W), 1)
    corners2 = splits([jnp.where(lane2 >= half, g[0:half], 0.0) for g in grams])
    products = dots3(corners, bases)
    fulls = splits([jnp.concatenate([p[0:SUB], zero, p[SUB:], zero], axis=0) for p in products])
    changes = dots3(splits([jnp.concatenate([p[0], p[2]], axis=0) for p in parts]), fulls)
    uppers = [jnp.concatenate([p[0] - c[0:SUB], p[1]], axis=0) for p, c in zip(parts, changes)]
    lowers = [jnp.concatenate([p[2] - c[SUB:], p[3]], axis=0) for p, c in zip(parts, changes)]
    products = dots3(corners2, splits([jnp.concatenate([zeros, low], axis=0) for low in lowers]))
    changes = dots3(splits(uppers), splits([jnp.concatenate([p, zeros], axis=0) for p in products]))
    return [jnp.concatenate([u - c, low], axis=0) for u, c, low in zip(uppers, changes, lowers)]


def factors(packed):
    reflectors = [unpacked(p) for p in packed]
    halves = splits(reflectors)
    nt = ((1,), (1,))
    grams = [mm(h, h, nt) + (mm(h, l, nt) + mm(l, h, nt)) for h, l in halves]
    inverses = splits(triangle_inverses(grams))
    products = splits(dots3(inverses, halves))
    return [(*a, *split(r.T)) for a, r in zip(products, reflectors)]


def whole(factor):
    ah, al, vh, vl = factor
    return jnp.concatenate(split(dot3((vh, vl), (ah, al))), axis=1)


def stored_wholes(packed, g_ref):
    for at, factor in enumerate(factors(packed)):
        g_ref[at] = whole(factor)


def slot_of(scalars, level, half):
    return scalars[4 + 2 * level + half]


def gathered(scalars, pieces, held, at):
    for k in range(4):
        held[(scalars[0] + 4 - k) % 4] = pieces[k][at]


def block_of(scalars, held, level, half):
    return held[2 * (level % 2) + slot_of(scalars, level, half)]


def twice(factor):
    ah, al, vh, vl = factor

    def update(x):
        return x - dot3((vh, vl), split(dot3((ah, al), split(x))))

    return update


def once(g_ref, at):
    g = g_ref[at]

    def update(x):
        xh, xl = split(x)
        wide = mm(g[:, : 2 * W], jnp.concatenate([xh, xl], axis=1))
        return x - (wide[:, :W] + (wide[:, W:] + mm(g[:, 2 * W :], xh)))

    return update


def across(top, low, update):
    middle = update(jnp.concatenate([top[W:], low[:W]], axis=0))
    return jnp.concatenate([top[:W], middle[:W]], axis=0), jnp.concatenate([middle[W:], low[W:]], axis=0)


def joined(g_ref, at):
    g = g_ref[at]
    return g[:W, :W].astype(F32) + g[:W, 2 * W : 3 * W].astype(F32)


def below_rows(message):
    return message[:W], message[W : 2 * W], message[2 * W :]


def across_below(last, low, near, update):
    middle = update(jnp.concatenate([low[W:], jnp.where(last, 0.0, near)], axis=0))
    return jnp.concatenate([low[:W], middle[:W]], axis=0), middle[W:]


def carried(settled, quarter, change):
    return settled + (change - dot3(split(quarter), split(change)))


def across_above(first, above, top, update):
    new_above, new_top = across(above, top, update)
    return new_above, jnp.where(first, top, new_top)


def keep_kernel(piece, kept):
    kept[...] = piece[...]


def pass_kernel(after, value, passed):
    passed[...] = value[...]


def order_kernel(plane, p0, p1, p2, p3, near, far, held):
    for k, piece in enumerate((p0, p1, p2, p3)):
        held[(plane[0] + 4 - k) % 4] = piece[...]
    near[...] = held[0:2]
    far[...] = held[2:4]


def first_kernel(scalars, x_ref, p0, p1, p2, p3, message, low_ref, rest, held):
    pieces = (p0, p1, p2, p3)
    gathered(scalars, pieces, held, 1)
    ahead = block_of(scalars, held, 2, 0)
    gathered(scalars, pieces, held, 0)
    found = factors([block_of(scalars, held, level, half) for level, half in ((0, 0), (0, 1), (1, 0))] + [ahead])
    ah, al, vh, vl = found[3]
    left = dot3((vh, vl), (ah[:, :W], al[:, :W]))
    top = twice(found[0])(x_ref[: 2 * W])
    low = twice(found[1])(x_ref[2 * W :])
    top, low = across(top, low, twice(found[2]))
    settled = twice(found[3])(top)
    message[:W] = top[:W]
    message[W : 2 * W] = settled[:W]
    message[2 * W :] = left[:W]
    rest[:W] = settled[W:]
    rest[W:] = left[W:]
    low_ref[...] = low


def factor1_kernel(scalars, after, p0, p1, p2, p3, g1, held):
    pieces = (p0, p1, p2, p3)
    gathered(scalars, pieces, held, 0)
    early = block_of(scalars, held, 1, 1)
    gathered(scalars, pieces, held, 1)
    late = [block_of(scalars, held, level, half) for level, half in ((2, 1), (3, 0), (3, 1))]
    stored_wholes([*late, early], g1)


def second_kernel(scalars, low_ref, message, g1, low_out, back):
    last = scalars[1] == 1
    near, settled, quarter = below_rows(message)
    low, moved = across_below(last, low_ref[...], near, once(g1, 3))
    change = moved - near
    low = once(g1, 0)(low)
    low, moved = across_below(last, low, carried(settled, quarter, change), once(g1, 2))
    low_out[...] = low
    back[:W] = moved
    back[W:] = change


def choose_kernel(scalars, after, p0, p1, p2, p3, down, held):
    pieces = (p0, p1, p2, p3)
    gathered(scalars, pieces, held, 1)
    down[1] = block_of(scalars, held, 6, 1)
    down[2] = block_of(scalars, held, 7, 1)
    gathered(scalars, pieces, held, 0)
    down[0] = block_of(scalars, held, 5, 1)


def factor2_kernel(scalars, after, p0, p1, p2, p3, g2, held):
    pieces = (p0, p1, p2, p3)
    gathered(scalars, pieces, held, 1)
    later = block_of(scalars, held, 6, 0)
    gathered(scalars, pieces, held, 0)
    stored_wholes([block_of(scalars, held, level, half) for level in (4, 5) for half in (0, 1)] + [later], g2)


def third_kernel(scalars, low_ref, own, rest, back, after, g1, g2, low_out, top_out, far_out, near_out):
    upper = jnp.where(scalars[2] == 1, own[W : 2 * W], back[:W])
    lower = rest[:W] - dot3(split(rest[W:]), split(back[W:]))
    top, low = across(jnp.concatenate([upper, lower], axis=0), low_ref[...], once(g1, 1))
    top = once(g2, 0)(top)
    low = once(g2, 1)(low)
    top, low = across(top, low, once(g2, 2))
    low_out[...] = low
    top_out[...] = top
    settled = once(g2, 4)(top)
    odd = scalars[3] == 1
    for at, (up, down) in enumerate(((top[:W], low[:W]), (settled[:W], low[W:]), (joined(g2, 4), top[W:]))):
        far_out[at * W : (at + 1) * W] = jnp.where(odd, down, up)
        near_out[at * W : (at + 1) * W] = jnp.where(odd, up, down)


def factor3_kernel(scalars, after, p0, p1, p2, p3, g3, held):
    gathered(scalars, (p0, p1, p2, p3), held, 1)
    stored_wholes([block_of(scalars, held, level, half) for level, half in ((6, 1), (7, 0), (7, 1))], g3)


def factor4_kernel(after, down, g4):
    stored_wholes([down[0], down[1], down[2]], g4)


def fourth_kernel(scalars, low_ref, top_ref, far, near, g2, g3, g4, out_ref):
    last = scalars[1] == 1
    first = scalars[2] == 1
    odd = scalars[3] == 1
    above = jnp.where(odd, near[: 2 * W], far[: 2 * W])
    near, settled, quarter = below_rows(jnp.where(odd, far[...], near[...]))
    low, moved = across_below(last, low_ref[...], near, once(g2, 3))
    above, top = across_above(first, above, top_ref[...], once(g4, 0))
    above = once(g4, 1)(above)
    top = once(g2, 4)(top)
    low = once(g3, 0)(low)
    _, top = across_above(first, above, top, once(g4, 2))
    low, _ = across_below(last, low, carried(settled, quarter, moved - near), once(g3, 2))
    top, low = across(top, low, once(g3, 1))
    out_ref[: 2 * W] = top
    out_ref[2 * W :] = low


def wholes(count):
    return jax.ShapeDtypeStruct((count, 2 * W, 4 * W), BF16)


def rows_shape(*shape):
    return jax.ShapeDtypeStruct(shape, F32)


HELD = [pltpu.VMEM((4, W, W), F32)]


def call(kernel, args, shapes, scratch=(), smem=1, flops=400_000_000):
    return pl.pallas_call(
        kernel,
        out_shape=tuple(shapes),
        in_specs=[pl.BlockSpec(memory_space=SMEM)] * smem + [pl.BlockSpec(memory_space=VMEM)] * (len(args) - smem),
        out_specs=(pl.BlockSpec(memory_space=VMEM),) * len(shapes),
        scratch_shapes=list(scratch),
        compiler_params=pltpu.CompilerParams(vmem_limit_bytes=24 * 1024 * 1024),
        cost_estimate=pl.CostEstimate(flops=flops, bytes_accessed=2_000_000, transcendentals=0),
        name=kernel.__name__,
    )(*args)


def shifted(value, axis, steps):
    count = lax.axis_size(axis)
    return lax.ppermute(value, axis, [(i, (i + steps) % count) for i in range(count)])


def to_neighbour(value, steps):
    count = lax.axis_size("rows")
    return lax.ppermute(value, "rows", [(i, i + steps) for i in range(count) if 0 <= i + steps < count])


def swapped(value, start):
    count = lax.axis_size("rows")
    pairs = [(i, i + 1) for i in range(start, count - 1, 2)]
    return lax.ppermute(value, "rows", pairs + [(j, i) for i, j in pairs])


def along_x(value):
    found = {k: lax.ppermute(value, "cols", [(i, (i // 4) * 4 + (i + k) % 4) for i in range(16)]) for k in (3, 2, 1)}
    return [value, found[1], found[2], found[3]]


def per_device(eigvecs, wy_packed, slot_block):
    column = lax.axis_index("cols")
    row = lax.axis_index("rows")
    plane, place = column // 4, column % 4
    edges = jnp.stack([place, row == lax.axis_size("rows") - 1, row == 0, row % 2]).astype(jnp.int32)
    scalars = jnp.concatenate([edges, slot_block.reshape(-1)])
    packed = wy_packed[0]
    half = rows_shape(2 * W, W)

    (held,) = call(keep_kernel, (packed,), [rows_shape(W, W)], smem=0)
    planes = [packed] + [shifted(packed, "cols", 4 * k) for k in (1, 2, 3)]
    pair = rows_shape(2, W, W)
    near, far = call(order_kernel, (plane.reshape(1), held, *planes[1:]), [pair, pair], HELD)
    near = along_x(near)
    (far,) = call(pass_kernel, (near[3], far), [pair], smem=0)
    far = along_x(far)
    three = rows_shape(3 * W, W)
    three = rows_shape(3 * W, W)
    own, low, rest = call(first_kernel, (scalars, eigvecs, *near), [three, half, half], HELD)
    message = to_neighbour(own, -1)
    (down,) = call(choose_kernel, (scalars, low, *far), [rows_shape(3, W, W)], HELD)
    (g1,) = call(factor1_kernel, (scalars, down, *near), [wholes(4)], HELD)
    low, back = call(second_kernel, (scalars, low, message, g1), [half, half])
    back = to_neighbour(back, 1)
    (g2,) = call(factor2_kernel, (scalars, low, *far), [wholes(5)], HELD)
    down = to_neighbour(down, 1)
    low, top, far_out, near_out = call(
        third_kernel, (scalars, low, own, rest, back, down, g1, g2), [half, half, three, three]
    )
    from_far = swapped(far_out, 1)
    from_near = swapped(near_out, 0)
    (g3,) = call(factor3_kernel, (scalars, low, *far), [wholes(3)], HELD)
    (g4,) = call(factor4_kernel, (low, down), [wholes(3)], smem=0)
    return call(
        fourth_kernel, (scalars, low, top, from_far, from_near, g2, g3, g4), [rows_shape(*eigvecs.shape)]
    )[0]


def solution(mesh):
    placed = (P("rows", "cols"), P(("rows", "cols"), None, None), P("rows", None, None))
    return jax.shard_map(
        per_device, mesh=mesh, in_specs=placed, out_specs=P("rows", "cols"), check_vma=False
    )
```
